32 devices in a mesh: dp: 8 (over y, x, core), fsdp: 4 (over z).
Axes of the slice: x: 2, y: 2, z: 4, core: 2. Of those that a mesh axis runs over, the one named last changes fastest.
Arguments:
- document_tokens: bfloat16 [32, 512, 768], P(('dp', 'fsdp')), may hold values from -6 to 6
- document_lengths: int32 [32, 4], P(('dp', 'fsdp')), may hold values from 1 to 256, 488 in all within a row
- query_tokens: bfloat16 [256, 32, 768], P(('dp', 'fsdp')), may hold values from -6 to 6
- query_lengths: int32 [256], P(('dp', 'fsdp')), may hold values from 16 to 32
- weight_query: bfloat16 [589824], P(('dp', 'fsdp')), may hold values from -0.0546875 to 0.0546875
- weight_key: bfloat16 [589824], P(('dp', 'fsdp')), may hold values from -0.21875 to 0.21875
- weight_value: bfloat16 [589824], P(('dp', 'fsdp')), may hold values from -0.21875 to 0.21875
- weight_out: bfloat16 [589824], P(('dp', 'fsdp')), may hold values from -0.625 to 0.625
- weight_gate: bfloat16 [2359296], P(('dp', 'fsdp')), may hold values from -0.21875 to 0.21875
- weight_up: bfloat16 [2359296], P(('dp', 'fsdp')), may hold values from -0.21875 to 0.21875
- weight_down: bfloat16 [2359296], P(('dp', 'fsdp')), may hold values from -0.15625 to 0.15625
- weight_proj: bfloat16 [98304], P(('dp', 'fsdp')), may hold values from -0.21875 to 0.21875
- norm_gains: bfloat16 [2304], P('fsdp'), may hold values from 0.099609375 to 1.8984375
- rel_table: bfloat16 [384], P('fsdp'), may hold values from -4 to 4
- document_cotangent: bfloat16 [32, 512, 128], P(('dp', 'fsdp')), may hold values from -6 to 6
- query_cotangent: bfloat16 [256, 32, 128], P(('dp', 'fsdp')), may hold values from -6 to 6
Outputs:
- document_output: bfloat16 [32, 512, 128], P(('dp', 'fsdp'))
- query_output: bfloat16 [256, 32, 128], P(('dp', 'fsdp'))
- document_grad: bfloat16 [32, 512, 768], P(('dp', 'fsdp'))
- query_grad: bfloat16 [256, 32, 768], P(('dp', 'fsdp'))
- grad_query: float32 [589824], P(('dp', 'fsdp'))
- grad_key: float32 [589824], P(('dp', 'fsdp'))
- grad_value: float32 [589824], P(('dp', 'fsdp'))
- grad_out: float32 [589824], P(('dp', 'fsdp'))
- grad_gate: float32 [2359296], P(('dp', 'fsdp'))
- grad_up: float32 [2359296], P(('dp', 'fsdp'))
- grad_down: float32 [2359296], P(('dp', 'fsdp'))
- grad_proj: float32 [98304], P(('dp', 'fsdp'))
- grad_gains: float32 [2304], P('fsdp')
- grad_table: float32 [384], P('fsdp')
The draws below stay inside these ranges and needn't reach their ends.
Inputs may be any that keep to these rules, and one draw needn't show every extreme that they name: `document_lengths`: in every row the 4 lengths sum to 488, and the longest is 256; positions from 488 on are padding. `query_lengths`: positions from a query's length on are padding.
All inputs are finite; a program needn't handle non-finite values.
Results may differ from the reference program's by a relative error of at most 0.014.
The reference program's roundings to bfloat16 on the way count: a program that leaves them out, or rounds other values in their place, can miss the bound.
Values may be sent and summed in bfloat16 or wider, within the bound.
A program may use at most 256 MiB of HBM per device.

```python
import math
import jax
import jax.numpy as jnp
import numpy as np
from jax import lax

D = 768
HEADS = 12
HEAD_DIM = 64
FF = 3072
BUCKETS = 32
PROJ = 128
DOC_LEN = 512
DOC_FILL = 488
DOC_SEGS = 4
DOC_MOST = 256
QRY_LEN = 32
DOCS = 32
QUERIES = 256


def set_ends(drawn, stream_key, least, top_value):
    dims = drawn.shape
    index_at = [jax.random.randint(jax.random.fold_in(stream_key, axis), (), 0, dims[axis]) for axis in range(len(dims))]
    drawn = drawn.at[tuple(index_at)].set(least)
    longest = dims.index(max(dims))
    index_at[longest] = (index_at[longest] + 1) % dims[longest]
    return drawn.at[tuple(index_at)].set(top_value)


def strengthened(result, rng, source, target, shards_of, factor):
    owner, partner = [(jnp.arange(result.shape[axis_at]) // (result.shape[axis_at] // shards_of)).reshape([-1 if axis == axis_at else 1 for axis in range(result.ndim)]) for axis_at in (source, target)]
    chosen = jax.random.permutation(rng, shards_of)[partner]
    strong = (owner == chosen) | (owner == (partner + shards_of // 2) % shards_of)
    return jnp.where(strong, factor * result, result)


def steps_of(rng, extent, split, least, top_value):
    def one(dim, parts):
        steps = jax.random.uniform(jax.random.fold_in(jax.random.fold_in(rng, 6), dim), (parts,), jnp.float32, least / len(split), top_value / len(split))
        return jnp.repeat(jnp.exp(steps), extent[dim] // parts).reshape((-1,) + (1,) * (len(extent) - dim - 1))

    level = one(*split[0])
    for cut in split[1:]:
        level = level * one(*cut)
    return level


def split_up(number_of, total, limit, slope):
    loads = [(1 << 20) // math.isqrt(grade ** slope) + 1 for grade in range(2, number_of + 1)]
    rest, counts = total - limit - (number_of - 1), [1] * (number_of - 1)
    while rest > 0:
        movable = [i for i in range(number_of - 1) if counts[i] < limit]
        whole, remaining = sum([loads[i] for i in movable]), rest
        for i in movable:
            addition = min(limit - counts[i], max(1, remaining * loads[i] // whole), rest)
            counts[i] = counts[i] + addition
            rest = rest - addition
    return np.array([limit] + counts)


def uneven_parts(rng, amount, total, limit, slope):
    if amount == 2:
        one = jax.random.randint(rng, (), max(1, total - limit), min(limit, total - 1) + 1)
        return jnp.stack([one, total - one])
    sizes = jnp.asarray(split_up(amount, total, limit, slope), jnp.int32)
    twos = (amount - 1) // 2
    giver, sink = sizes[1:1 + 2 * twos:2], sizes[2:2 + 2 * twos:2]
    room = jnp.minimum(giver - 1, limit - sink)
    moved = jax.random.randint(jax.random.fold_in(rng, 1), (twos,), 0, 1 << 20) % (room + 1)
    sizes = sizes.at[1:1 + 2 * twos:2].set(giver - moved).at[2:2 + 2 * twos:2].set(sink + moved)
    return sizes[jax.random.permutation(jax.random.fold_in(rng, 2), amount)]


def centred(key, extent, deviation, limit, split=(), kind=jnp.bfloat16):
    drawn = jax.random.normal(key, extent, jnp.float32) * deviation
    if len(split) > 0:
        drawn = steps_of(key, extent, split, -0.22, 0.18) * drawn
    return jnp.clip(drawn, min=-limit, max=limit).astype(kind)


def bell_draw_with(stream_key, dims, width, limit, pieces, heavy, kind=jnp.bfloat16):
    entries = width * jax.random.normal(stream_key, dims, jnp.float32)
    if pieces:
        entries = entries * steps_of(stream_key, dims, pieces, -0.22, 0.18)
    return jnp.clip(strengthened(entries, jax.random.fold_in(stream_key, 3), *heavy), -limit, limit).astype(kind)


def setup_inputs(seed: int = 0) -> dict:
    seeds = jax.random.split(jax.random.key(seed), 17)
    return {
        "document_tokens": bell_draw_with(seeds[0], (DOCS, DOC_LEN, D), 1.0, 6.0, ((0, 32),), (0, 2, 32, 2.75)),
        "document_lengths": jax.vmap(lambda own: uneven_parts(own, DOC_SEGS, DOC_FILL, DOC_MOST, 2))(jax.random.split(seeds[1], DOCS)).reshape((DOCS, DOC_SEGS)).astype(jnp.int32),
        "query_tokens": centred(seeds[2], (QUERIES, QRY_LEN, D), 1.0, 6.0, ((0, 32),)),
        "query_lengths": set_ends(jax.random.randint(seeds[3], (QUERIES,), QRY_LEN // 2, QRY_LEN + 1), jax.random.fold_in(seeds[3], 1), QRY_LEN // 2, QRY_LEN).astype(jnp.int32),
        "weight_query": centred(seeds[4], (D * D,), (16 * D) ** -0.5, 0.0546875, ((0, 32),)),
        "weight_key": centred(seeds[5], (D * D,), D ** -0.5, 0.21875, ((0, 32),)),
        "weight_value": centred(seeds[6], (D * D,), D ** -0.5, 0.21875, ((0, 32),)),
        "weight_out": centred(seeds[7], (D * D,), (D // 8) ** -0.5, 0.625, ((0, 32),)),
        "weight_gate": centred(seeds[8], (D * FF,), D ** -0.5, 0.21875, ((0, 32),)),
        "weight_up": centred(seeds[9], (D * FF,), D ** -0.5, 0.21875, ((0, 32),)),
        "weight_down": centred(seeds[10], (FF * D,), (FF // 2) ** -0.5, 0.15625, ((0, 32),)),
        "weight_proj": centred(seeds[11], (D * PROJ,), D ** -0.5, 0.21875, ((0, 32),)),
        "norm_gains": jnp.clip(1.0 + 0.18 * jax.random.normal(seeds[12], (3 * D,), jnp.float32), 0.099609375, 1.8984375).astype(jnp.bfloat16),
        "rel_table": centred(seeds[13], (BUCKETS * HEADS,), 1.0, 4.0, ((0, 4),)),
        "document_cotangent": centred(seeds[14], (DOCS, DOC_LEN, PROJ), 1.0, 6.0, ((0, 32),)),
        "query_cotangent": centred(seeds[15], (QUERIES, QRY_LEN, PROJ), 1.0, 6.0, ((0, 32),)),
    }


@jax.custom_vjp
def low(v):
    return lax.optimization_barrier(v.astype(jnp.bfloat16)).astype(jnp.float32)

@jax.custom_vjp
def low_back(v):
    return v

def low_keep(v):
    return (low(v), None)

def low_pass(kept, grad):
    return (grad,)

def back_keep(v):
    return (v, None)

def back_low(kept, grad):
    return (low(grad),)
low.defvjp(low_keep, low_pass)
low_back.defvjp(back_keep, back_low)
EPSILON = 1e-06
NEGATIVE = -1e+30
HIGHEST = lax.Precision.HIGHEST

def rms_norm(values, gain_row):
    inverse = lax.rsqrt(lax.optimization_barrier(jnp.mean(values * values, axis=-1, keepdims=True)) + EPSILON)
    return values * inverse * gain_row

def bucket_ids(length):
    positions = jnp.arange(length, dtype=jnp.int32)
    relative = positions[None, :] - positions[:, None]
    distance = jnp.abs(relative)
    distant = 8 + sum(((distance * distance >= 64 * 2 ** power).astype(jnp.int32) for power in range(1, 8)))
    nearby = jnp.where(distance < 8, distance, distant)
    return nearby + 16 * (relative > 0).astype(jnp.int32)

def segment_ids(lengths, length):
    boundary = jnp.cumsum(lengths, axis=-1)
    positions = jnp.arange(length, dtype=jnp.int32)
    return lax.optimization_barrier(jnp.sum((positions[None, :, None] >= boundary[:, None, :]).astype(jnp.int32), axis=-1))

def project(source, matrix):
    return jnp.einsum('bld,de->ble', source, matrix, precision=HIGHEST)

def encoder_layer(inputs, segments, matrices, gain_rows, bias_table):
    query_mat, key_mat, value_mat, out_mat, gate_mat, up_mat, down_mat, proj_mat = matrices
    members = inputs.shape[0]
    length = inputs.shape[1]
    normed_one = low(rms_norm(inputs, gain_rows[0]))
    queries = low_back(low(project(normed_one, query_mat))).reshape(members, length, HEADS, HEAD_DIM)
    key_rows = low_back(low(project(normed_one, key_mat))).reshape(members, length, HEADS, HEAD_DIM)
    values = low_back(low(project(normed_one, value_mat))).reshape(members, length, HEADS, HEAD_DIM)
    rel_bias = jnp.transpose(bias_table[bucket_ids(length)], (2, 0, 1))
    scores = jnp.einsum('bqhd,bkhd->bhqk', queries, key_rows, precision=HIGHEST) + rel_bias[None]
    scores = low_back(scores)
    allowed = segments[:, None, :, None] == segments[:, None, None, :]
    scores = jnp.where(allowed, scores, NEGATIVE)
    attention = low(jax.nn.softmax(scores, axis=-1))
    context = jnp.einsum('bhqk,bkhd->bqhd', attention, values, precision=HIGHEST).reshape(members, length, D)
    context = low_back(low(context))
    hidden = inputs + low_back(project(context, out_mat))
    normed_two = low(rms_norm(hidden, gain_rows[1]))
    gate = low_back(project(normed_two, gate_mat))
    upper = low_back(project(normed_two, up_mat))
    inner = low(jax.nn.gelu(gate, approximate=True) * upper)
    final = hidden + low_back(project(inner, down_mat))
    normed_three = low(rms_norm(final, gain_rows[2]))
    return project(normed_three, proj_mat)

def run_groups(tokens, segments, matrices, gain_rows, bias_table, group_size):
    total_rows = tokens.shape[0]
    length = tokens.shape[1]
    grouped = tokens.reshape(total_rows // group_size, group_size, length, D)
    grouped_ids = segments.reshape(total_rows // group_size, group_size, length)
    checked = jax.checkpoint(encoder_layer)

    def one_group(members):
        return checked(members[0], members[1], matrices, gain_rows, bias_table)
    results = lax.map(one_group, (grouped, grouped_ids))
    return results.reshape(total_rows, length, PROJ)

def reference(document_tokens, document_lengths, query_tokens, query_lengths, weight_query, weight_key, weight_value, weight_out, weight_gate, weight_up, weight_down, weight_proj, norm_gains, rel_table, document_cotangent, query_cotangent):
    doc_segments = segment_ids(document_lengths, DOC_LEN)
    query_segments = segment_ids(query_lengths.reshape(QUERIES, 1), QRY_LEN)
    doc_group = math.gcd(DOCS, max(1, 4096 // DOC_LEN))
    query_group = math.gcd(QUERIES, max(1, 4096 // QRY_LEN))

    def forward(doc_inputs, query_inputs, query_weights, key_weights, value_weights, out_weights, gate_weights, up_weights, down_weights, proj_weights, gains_flat, table_flat):
        matrices = (query_weights.reshape(D, D), key_weights.reshape(D, D), value_weights.reshape(D, D), out_weights.reshape(D, D), gate_weights.reshape(D, FF), up_weights.reshape(D, FF), down_weights.reshape(FF, D), proj_weights.reshape(D, PROJ))
        gain_rows = gains_flat.reshape(3, D)
        bias_table = table_flat.reshape(BUCKETS, HEADS)
        doc_out = run_groups(doc_inputs, doc_segments, matrices, gain_rows, bias_table, doc_group)
        query_out = run_groups(query_inputs, query_segments, matrices, gain_rows, bias_table, query_group)
        return (doc_out, query_out)
    primals = [item.astype(jnp.float32) for item in (document_tokens, query_tokens, weight_query, weight_key, weight_value, weight_out, weight_gate, weight_up, weight_down, weight_proj, norm_gains, rel_table)]
    outputs, pullback = jax.vjp(forward, primals[0], primals[1], primals[2], primals[3], primals[4], primals[5], primals[6], primals[7], primals[8], primals[9], primals[10], primals[11])
    grads = pullback((document_cotangent.astype(jnp.float32), query_cotangent.astype(jnp.float32)))
    return (outputs[0].astype(jnp.bfloat16), outputs[1].astype(jnp.bfloat16), grads[0].astype(jnp.bfloat16), grads[1].astype(jnp.bfloat16), grads[2], grads[3], grads[4], grads[5], grads[6], grads[7], grads[8], grads[9], grads[10], grads[11])
```

```python
import functools

import jax
import jax.numpy as jnp
from jax import lax
from jax.experimental import pallas as pl
from jax.experimental.pallas import tpu as pltpu
from jax.sharding import PartitionSpec as P

D = 768
HEADS = 12
HEAD_DIM = 64
FF = 3072
BUCKETS = 32
PROJ = 128
DOC_LEN = 512
QRY_LEN = 32


EPSILON = 1e-06
NEGATIVE = -1e30


def rms_norm(values, gain_row):
    inverse = lax.rsqrt(jnp.mean(values * values, axis=-1, keepdims=True) + EPSILON)
    return values * inverse * gain_row


def gated_unit(gate_in, upper_in):
    return jax.nn.gelu(gate_in, approximate=True) * upper_in


def bucket_ids(length):
    positions = jnp.arange(length, dtype=jnp.int32)
    relative = positions[None, :] - positions[:, None]
    distance = jnp.abs(relative)
    distant = 8 + sum(
        ((distance * distance >= 64 * 2**power).astype(jnp.int32) for power in range(1, 8))
    )
    nearby = jnp.where(distance < 8, distance, distant)
    return nearby + 16 * (relative > 0).astype(jnp.int32)


def bucket_onehot(length):
    flat_ids = bucket_ids(length).reshape(1, length * length)
    labels = jnp.arange(BUCKETS, dtype=jnp.int32).reshape(BUCKETS, 1)
    return (flat_ids == labels).astype(jnp.bfloat16)


def segment_ids(lengths, length):
    boundary = jnp.cumsum(lengths, axis=-1)
    positions = jnp.arange(length, dtype=jnp.int32)
    return jnp.sum((positions[None, :, None] >= boundary[:, None, :]).astype(jnp.int32), axis=-1)


def outer_sum(left_rows, right_rows):
    return lax.dot_general(
        left_rows, right_rows, (((0,), (0,)), ((), ())), preferred_element_type=jnp.float32
    )


def times_transposed(left_rows, matrix):
    return lax.dot_general(
        left_rows, matrix, (((1,), (1,)), ((), ())), preferred_element_type=jnp.float32
    )


def flat_piece(left_rows, right_rows, start, count):
    width = right_rows.shape[1]
    needed = count // width + 2
    padded = jnp.pad(left_rows, ((0, 0), (0, needed)))
    first_row = start // width
    columns = lax.dynamic_slice_in_dim(padded, first_row, needed, 1)
    block = outer_sum(columns, right_rows).reshape(-1)
    return lax.dynamic_slice_in_dim(block, start, count)


def grad_terms(pairs, devices):
    shares = [pair[0].shape[1] * pair[1].shape[1] // devices for pair in pairs]
    total_share = sum(shares)

    def term(start, count):
        blocks = count // total_share
        first_block = start // total_share
        pieces = [
            flat_piece(pair[0], pair[1], first_block * share, blocks * share).reshape(blocks, share)
            for pair, share in zip(pairs, shares)
        ]
        return jnp.concatenate(pieces, axis=1).reshape(-1)

    return (term, total_share, shares)


def split_shares(mine, shares):
    results = []
    offset = 0
    for share in shares:
        results.append(mine[offset : offset + share])
        offset = offset + share
    return results


def bias_rows(table_mat, onehot, length):
    rel_bias = lax.dot_general(
        table_mat, onehot, (((0,), (0,)), ((), ())), preferred_element_type=jnp.float32
    )
    return rel_bias.reshape(1, HEADS, length, length)


def masked_scores(queries, key_rows, rel_bias, allowed):
    scores = (
        jnp.einsum("bqhd,bkhd->bhqk", queries, key_rows, preferred_element_type=jnp.float32)
        + rel_bias
    )
    return jnp.where(allowed, scores, NEGATIVE)


def attend(queries, key_rows, values, rel_bias, allowed):
    scores = masked_scores(queries, key_rows, rel_bias, allowed)
    largest = jnp.max(scores, axis=-1, keepdims=True)
    summed = jnp.sum(jnp.exp(scores - largest), axis=-1, keepdims=True)
    log_total = largest + jnp.log(summed)
    attention = jnp.exp(scores - log_total).astype(jnp.bfloat16)
    context = jnp.einsum("bhqk,bkhd->bqhd", attention, values, preferred_element_type=jnp.float32)
    return (context.astype(jnp.bfloat16), log_total)


def attend_back(queries, key_rows, values, rel_bias, allowed, log_total, grad_context):
    scores = masked_scores(queries, key_rows, rel_bias, allowed)
    attention = jnp.exp(scores - log_total)
    grad_attention = jnp.einsum(
        "bqhd,bkhd->bhqk", grad_context, values, preferred_element_type=jnp.float32
    )
    grad_values = jnp.einsum(
        "bhqk,bqhd->bkhd",
        attention.astype(jnp.bfloat16),
        grad_context,
        preferred_element_type=jnp.float32,
    )
    weighted = jnp.sum(attention * grad_attention, axis=-1, keepdims=True)
    grad_scores = (attention * (grad_attention - weighted)).astype(jnp.bfloat16)
    grad_queries = jnp.einsum(
        "bhqk,bkhd->bqhd", grad_scores, key_rows, preferred_element_type=jnp.float32
    )
    grad_keys = jnp.einsum(
        "bhqk,bqhd->bkhd", grad_scores, queries, preferred_element_type=jnp.float32
    )
    return (
        grad_queries.astype(jnp.bfloat16),
        grad_keys.astype(jnp.bfloat16),
        grad_values.astype(jnp.bfloat16),
        grad_scores,
    )


def bias_grads(grad_scores, onehot):
    members = grad_scores.shape[0]
    flattened = grad_scores.reshape(members * HEADS, -1)
    summed = lax.dot_general(
        flattened, onehot, (((1,), (1,)), ((), ())), preferred_element_type=jnp.float32
    )
    return jnp.sum(summed.reshape(members, HEADS, BUCKETS), axis=0)


def local(
    document_tokens,
    document_lengths,
    query_tokens,
    query_lengths,
    weight_query,
    weight_key,
    weight_value,
    weight_out,
    weight_gate,
    weight_up,
    weight_down,
    weight_proj,
    norm_gains,
    rel_table,
    document_cotangent,
    query_cotangent,
):
    layouts = ((D, D), (D, D), (D, D), (D, D), (D, FF), (D, FF), (FF, D), (D, PROJ))
    devices = lax.axis_size("dp") * lax.axis_size("fsdp")
    gathered = (
        lax.all_gather(weight_query, ("dp", "fsdp"), axis=0, tiled=True),
        lax.all_gather(weight_key, ("dp", "fsdp"), axis=0, tiled=True),
        lax.all_gather(weight_value, ("dp", "fsdp"), axis=0, tiled=True),
        lax.all_gather(weight_out, ("dp", "fsdp"), axis=0, tiled=True),
        lax.all_gather(weight_gate, ("dp", "fsdp"), axis=0, tiled=True),
        lax.all_gather(weight_up, ("dp", "fsdp"), axis=0, tiled=True),
        lax.all_gather(weight_down, ("dp", "fsdp"), axis=0, tiled=True),
        lax.all_gather(weight_proj, ("dp", "fsdp"), axis=0, tiled=True),
    )
    matrices = [flat_rows.reshape(layout) for flat_rows, layout in zip(gathered, layouts)]
    gains_all, table_all = (
        lax.all_gather(norm_gains, "fsdp", axis=0, tiled=True),
        lax.all_gather(rel_table, "fsdp", axis=0, tiled=True),
    )
    gain_rows = gains_all.astype(jnp.float32).reshape(3, D)
    table_mat = table_all.reshape(BUCKETS, HEADS)
    documents = document_tokens.shape[0]
    queries_here = query_tokens.shape[0]
    doc_rows = documents * DOC_LEN
    doc_segments = segment_ids(document_lengths, DOC_LEN)
    query_segments = segment_ids(query_lengths.reshape(queries_here, 1), QRY_LEN)
    doc_allowed = doc_segments[:, None, :, None] == doc_segments[:, None, None, :]
    query_allowed = query_segments[:, None, :, None] == query_segments[:, None, None, :]
    doc_onehot = bucket_onehot(DOC_LEN)
    query_onehot = bucket_onehot(QRY_LEN)
    doc_bias = bias_rows(table_mat, doc_onehot, DOC_LEN)
    query_bias = bias_rows(table_mat, query_onehot, QRY_LEN)
    settings = [(doc_bias, doc_allowed, doc_onehot)]
    settings.append((query_bias, query_allowed, query_onehot))

    def split_blocks(matrix):
        blocks_out = [matrix[0:DOC_LEN].reshape(1, DOC_LEN, HEADS, HEAD_DIM)]
        blocks_out.append(matrix[doc_rows:].reshape(queries_here, QRY_LEN, HEADS, HEAD_DIM))
        return blocks_out

    query_mat, key_mat, value_mat, out_mat, gate_mat, up_mat, down_mat, proj_mat = matrices
    inputs = jnp.concatenate(
        [document_tokens.reshape(doc_rows, D), query_tokens.reshape(-1, D)], axis=0
    )
    residual_in = inputs.astype(jnp.float32)
    normed_one, norm_one_back = jax.vjp(rms_norm, residual_in, gain_rows[0])
    normed_one = normed_one.astype(jnp.bfloat16)
    queries = jnp.dot(normed_one, query_mat, preferred_element_type=jnp.float32).astype(
        jnp.bfloat16
    )
    key_rows = jnp.dot(normed_one, key_mat, preferred_element_type=jnp.float32).astype(jnp.bfloat16)
    values = jnp.dot(normed_one, value_mat, preferred_element_type=jnp.float32).astype(jnp.bfloat16)
    query_blocks = split_blocks(queries)
    key_blocks = split_blocks(key_rows)
    value_blocks = split_blocks(values)
    contexts = []
    log_totals = []
    for query_block, key_block, value_block, setting in zip(
        query_blocks, key_blocks, value_blocks, settings
    ):
        context_block, log_total = attend(
            query_block, key_block, value_block, setting[0], setting[1]
        )
        contexts.append(context_block.reshape(-1, D))
        log_totals.append(log_total)
    context = jnp.concatenate(contexts, axis=0)
    hidden = residual_in + jnp.dot(context, out_mat, preferred_element_type=jnp.float32)
    normed_two, norm_two_back = jax.vjp(rms_norm, hidden, gain_rows[1])
    normed_two = normed_two.astype(jnp.bfloat16)
    gate = jnp.dot(normed_two, gate_mat, preferred_element_type=jnp.float32)
    upper = jnp.dot(normed_two, up_mat, preferred_element_type=jnp.float32)
    inner, gated_back = jax.vjp(gated_unit, gate, upper)
    inner = inner.astype(jnp.bfloat16)
    final = hidden + jnp.dot(inner, down_mat, preferred_element_type=jnp.float32)
    normed_three, norm_three_back = jax.vjp(rms_norm, final, gain_rows[2])
    normed_three = normed_three.astype(jnp.bfloat16)
    output = jnp.dot(normed_three, proj_mat, preferred_element_type=jnp.float32).astype(
        jnp.bfloat16
    )
    again = (
        lax.all_gather(weight_query, ("dp", "fsdp"), axis=0, tiled=True),
        lax.all_gather(weight_key, ("dp", "fsdp"), axis=0, tiled=True),
        lax.all_gather(weight_value, ("dp", "fsdp"), axis=0, tiled=True),
        lax.all_gather(weight_out, ("dp", "fsdp"), axis=0, tiled=True),
        lax.all_gather(weight_gate, ("dp", "fsdp"), axis=0, tiled=True),
        lax.all_gather(weight_up, ("dp", "fsdp"), axis=0, tiled=True),
        lax.all_gather(weight_down, ("dp", "fsdp"), axis=0, tiled=True),
        lax.all_gather(weight_proj, ("dp", "fsdp"), axis=0, tiled=True),
    )
    back_mats = [flat_rows.reshape(layout) for flat_rows, layout in zip(again, layouts)]
    back_query, back_key, back_value, back_out, back_gate, back_up, back_down, back_proj = back_mats
    cotangent = jnp.concatenate(
        [document_cotangent.reshape(doc_rows, PROJ), query_cotangent.reshape(-1, PROJ)], axis=0
    )
    grad_final, grad_gain_three = norm_three_back(times_transposed(cotangent, back_proj))
    grad_ffn = grad_final.astype(jnp.bfloat16)
    grad_gate_f, grad_upper_f = gated_back(times_transposed(grad_ffn, back_down))
    grad_gate_b = grad_gate_f.astype(jnp.bfloat16)
    grad_upper_b = grad_upper_f.astype(jnp.bfloat16)
    grad_normed_two = times_transposed(grad_gate_b, back_gate) + times_transposed(
        grad_upper_b, back_up
    )
    grad_hidden_part, grad_gain_two = norm_two_back(grad_normed_two)
    grad_hidden = grad_final + grad_hidden_part
    ffn_pairs = [
        (normed_two, grad_gate_b),
        (normed_two, grad_upper_b),
        (inner, grad_ffn),
        (normed_three, cotangent),
    ]
    grad_branch = grad_hidden.astype(jnp.bfloat16)
    grad_context = times_transposed(grad_branch, back_out).astype(jnp.bfloat16)
    table_grad = jnp.zeros((HEADS, BUCKETS), jnp.float32)
    grad_query_parts = []
    grad_key_parts = []
    grad_value_parts = []
    for query_block, key_block, value_block, setting, log_total, grad_block in zip(
        query_blocks, key_blocks, value_blocks, settings, log_totals, split_blocks(grad_context)
    ):
        grad_q_block, grad_k_block, grad_v_block, grad_scores = attend_back(
            query_block, key_block, value_block, setting[0], setting[1], log_total, grad_block
        )
        table_grad = table_grad + bias_grads(grad_scores, setting[2])
        grad_query_parts.append(grad_q_block.reshape(-1, D))
        grad_key_parts.append(grad_k_block.reshape(-1, D))
        grad_value_parts.append(grad_v_block.reshape(-1, D))
    grad_queries = jnp.concatenate(grad_query_parts, axis=0)
    grad_keys = jnp.concatenate(grad_key_parts, axis=0)
    grad_values = jnp.concatenate(grad_value_parts, axis=0)
    grad_normed_one = (
        times_transposed(grad_queries, back_query)
        + times_transposed(grad_keys, back_key)
        + times_transposed(grad_values, back_value)
    )
    grad_input_part, grad_gain_one = norm_one_back(grad_normed_one)
    grad_inputs = (grad_hidden + grad_input_part).astype(jnp.bfloat16)
    attn_pairs = [
        (normed_one, grad_queries),
        (normed_one, grad_keys),
        (normed_one, grad_values),
        (context, grad_branch),
    ]
    all_term, all_total, all_shares = grad_terms(attn_pairs + ffn_pairs, devices)
    shares = tuple(
        split_shares(
            lax.psum_scatter(
                all_term(jnp.int32(0), lax.axis_size(("dp", "fsdp")) * all_total),
                ("dp", "fsdp"),
                scatter_dimension=0,
                tiled=True,
            ),
            all_shares,
        )
    )
    gain_grads = jnp.concatenate([grad_gain_one, grad_gain_two, grad_gain_three], axis=0)
    table_flat = jnp.transpose(table_grad).reshape(-1)
    gain_whole, table_whole = lax.psum((gain_grads, table_flat), ("dp", "fsdp"))
    fsdp_index = lax.axis_index("fsdp")
    fsdp_count = lax.axis_size("fsdp")
    gain_share = 3 * D // fsdp_count
    table_share = BUCKETS * HEADS // fsdp_count
    own_gains = lax.dynamic_slice_in_dim(gain_whole, fsdp_index * gain_share, gain_share)
    own_table = lax.dynamic_slice_in_dim(table_whole, fsdp_index * table_share, table_share)
    return (
        output[:doc_rows].reshape(documents, DOC_LEN, PROJ),
        output[doc_rows:].reshape(queries_here, QRY_LEN, PROJ),
        grad_inputs[:doc_rows].reshape(documents, DOC_LEN, D),
        grad_inputs[doc_rows:].reshape(queries_here, QRY_LEN, D),
        shares[0],
        shares[1],
        shares[2],
        shares[3],
        shares[4],
        shares[5],
        shares[6],
        shares[7],
        own_gains,
        own_table,
    )


WIDTHS = (3 * D, D + PROJ, 2 * FF, D)
SHARE_ROWS = (24, 24, 24, 96)
GATHER_STAGES = (
    (0, 0, 768),
    (0, 768, 768),
    (0, 1536, 768),
    (1, 0, 896),
    (2, 0, 1536),
    (2, 1536, 1536),
    (2, 3072, 1536),
    (2, 4608, 1536),
    (3, 0, 384),
    (3, 384, 384),
)
SCATTER_STAGES = (
    (3, 0, 384),
    (3, 384, 384),
    (2, 0, 1536),
    (2, 1536, 1536),
    (2, 3072, 1536),
    (2, 4608, 1536),
    (1, 0, 896),
    (0, 0, 768),
    (0, 768, 768),
    (0, 1536, 768),
)
MESH_ID = pl.DeviceIdType.MESH


def remote(source, target, send_sem, recv_sem, device):
    return pltpu.make_async_remote_copy(
        src_ref=source,
        dst_ref=target,
        send_sem=send_sem,
        recv_sem=recv_sem,
        device_id=device,
        device_id_type=MESH_ID,
    )


class Place:
    def __init__(self):
        self.dp = lax.axis_index("dp")
        self.z = lax.axis_index("fsdp")
        self.core = lax.rem(self.dp, 2)
        self.xy = self.dp // 2
        self.xy_x = self.xy + 1 - 2 * lax.rem(self.xy, 2)
        self.xy_y = lax.rem(self.xy + 2, 4)
        self.xy_d = 3 - self.xy
        self.sib = self.dp + 1 - 2 * self.core
        self.dp_x = 2 * self.xy_x + self.core
        self.dp_y = 2 * self.xy_y + self.core
        self.dp_d = 2 * self.xy_d + self.core
        self.zs = [lax.rem(self.z + step, 4) for step in (1, 2, 3)]
        self.to_sib = {"dp": self.sib}
        self.to_x = {"dp": self.dp_x}
        self.to_y = {"dp": self.dp_y}
        self.to_z = [{"fsdp": other} for other in self.zs]

    def barrier(self):
        semaphore = pltpu.get_barrier_semaphore()
        for device in [self.to_sib, self.to_x, self.to_y] + self.to_z:
            pl.semaphore_signal(semaphore, inc=1, device_id=device, device_id_type=MESH_ID)
        pl.semaphore_wait(semaphore, 6)


class Gather:
    def __init__(self, place, shards, whole, parts, sems):
        self.place, self.shards, self.whole, self.parts = place, shards, whole, parts
        (self.z_send, self.z_recv, self.send, self.recv) = sems
        self.stages = GATHER_STAGES

    @staticmethod
    def scratch():
        count = len(GATHER_STAGES)
        dma = pltpu.SemaphoreType.DMA
        return [dma((count, 3)), dma((count, 3)), dma((count, 9)), dma((count, 9))]

    def z_copy(self, s, k):
        array, first, width = self.stages[s]
        place = self.place
        columns = pl.ds(first, width)
        if array == 3:
            rows = pl.ds(pl.multiple_of(384 * place.dp + 96 * place.z, 96), 96)
            target = self.whole[3].at[rows, columns]
        else:
            target = self.parts[array].at[k, :, columns]
        return remote(
            self.shards[array].at[:, columns],
            target,
            self.z_send.at[s, k],
            self.z_recv.at[s, k],
            place.to_z[k],
        )

    def block(self, s, dp, half=None):
        array, first, width = self.stages[s]
        count = 4 * SHARE_ROWS[array]
        start = count * dp
        if half is not None:
            count = count // 2
            start = start + half * count
        return self.whole[array].at[
            pl.ds(pl.multiple_of(start, 48), count), pl.ds(first, width)
        ]

    def hop(self, s, index):
        place = self.place
        dp, half, device = (
            (place.dp, None, place.to_x),
            (place.dp, None, place.to_y),
            (place.dp_x, 0, place.to_y),
            (place.dp_y, 1, place.to_x),
            (place.dp, None, place.to_sib),
            (place.dp_x, None, place.to_sib),
            (place.dp_y, None, place.to_sib),
            (place.dp_d, 0, place.to_sib),
            (place.dp_d, 1, place.to_sib),
        )[index]
        block = self.block(s, dp, half)
        return remote(block, block, self.send.at[s, index], self.recv.at[s, index], device)

    def begin(self):
        for s in range(len(self.stages)):
            for k in range(3):
                self.z_copy(s, k).start()

    def spread(self, s):
        array, first, width = self.stages[s]
        place = self.place
        columns = pl.ds(first, width)
        for k in range(3):
            self.z_copy(s, k).wait_recv()
        if array == 3:
            rows = pl.ds(pl.multiple_of(384 * place.dp + 96 * place.z, 96), 96)
            self.whole[3][rows, columns] = self.shards[3][:, columns]
        else:
            pieces = []
            for other in range(4):
                piece = self.shards[array][:, columns]
                for k in range(3):
                    here = lax.rem(place.z + 3 - k, 4) == other
                    piece = jnp.where(here, self.parts[array][k, :, columns], piece)
                pieces.append(piece)
            rows = pl.ds(pl.multiple_of(96 * place.dp, 96), 96)
            self.whole[array][rows, columns] = jnp.concatenate(pieces, axis=0)
        for index in (0, 1, 4):
            self.hop(s, index).start()

    def relay(self, s):
        self.hop(s, 0).wait_recv()
        self.hop(s, 2).start()
        self.hop(s, 5).start()
        self.hop(s, 1).wait_recv()
        self.hop(s, 3).start()
        self.hop(s, 6).start()

    def hand_over(self, s):
        self.hop(s, 2).wait_recv()
        self.hop(s, 7).start()
        self.hop(s, 3).wait_recv()
        self.hop(s, 8).start()

    def arrive(self, s):
        for index in range(4, 9):
            self.hop(s, index).wait_recv()

    def step(self, t):
        count = len(self.stages)
        for lag, work in enumerate((self.spread, self.relay, self.hand_over, self.arrive)):
            if 0 <= t - lag < count:
                work(t - lag)

    def finish(self):
        for s in range(len(self.stages)):
            for k in range(3):
                self.z_copy(s, k).wait_send()
            for index in range(9):
                self.hop(s, index).wait_send()


class Scatter:
    def __init__(self, place, local, buffers, outputs, sems):
        self.place, self.local, self.outputs = place, local, outputs
        self.from_sib, self.from_x, self.from_y, self.z_out, self.z_in = (
            buffers[0:4],
            buffers[4:8],
            buffers[8:12],
            buffers[12:16],
            buffers[16:20],
        )
        self.diag_x, self.diag_y = buffers[20:24], buffers[24:28]
        self.send, self.recv = sems
        self.stages = SCATTER_STAGES

    @staticmethod
    def scratch():
        rows = [4 * count for count in SHARE_ROWS]
        kind = jnp.bfloat16
        shapes = [pltpu.VMEM((4, r, w), kind) for r, w in zip(rows, WIDTHS)]
        shapes += [pltpu.VMEM((r, w), kind) for r, w in zip(rows, WIDTHS)] * 2
        shapes += [pltpu.VMEM((4, r // 4, w), kind) for r, w in zip(rows, WIDTHS)]
        shapes += [pltpu.VMEM((3, r // 4, w), kind) for r, w in zip(rows, WIDTHS)]
        shapes += [pltpu.VMEM((r // 2, w), kind) for r, w in zip(rows, WIDTHS)] * 2
        return shapes

    @staticmethod
    def semaphores():
        count = len(SCATTER_STAGES)
        dma = pltpu.SemaphoreType.DMA
        return [dma((count, 8)), dma((count, 8))]

    def copy(self, s, index):
        array, first, width = self.stages[s]
        place = self.place
        columns = pl.ds(first, width)
        half = 2 * SHARE_ROWS[array]
        local = self.local(s)
        if index == 0:
            source = local.at[:, 1 - place.core]
            target = self.from_sib[array].at[:, :, columns]
            device = place.to_sib
        elif index == 1:
            source = local.at[place.xy_d, place.core, pl.ds(0, half)]
            target = self.diag_x[array].at[:, columns]
            device = place.to_x
        elif index == 2:
            source = local.at[place.xy_d, place.core, pl.ds(half, half)]
            target = self.diag_y[array].at[:, columns]
            device = place.to_y
        elif index == 3:
            source = local.at[place.xy_x, place.core]
            target = self.from_x[array].at[:, columns]
            device = place.to_x
        elif index == 4:
            source = local.at[place.xy_y, place.core]
            target = self.from_y[array].at[:, columns]
            device = place.to_y
        else:
            k = index - 5
            source = self.z_out[array].at[place.zs[k], :, columns]
            target = self.z_in[array].at[k, :, columns]
            device = place.to_z[k]
        return remote(source, target, self.send.at[s, index], self.recv.at[s, index], device)

    def add(self, s, block, other, rows=None):
        local = self.local(s)
        here = (block, self.place.core) if rows is None else (block, self.place.core, rows)
        total = local[here].astype(jnp.float32) + other.astype(jnp.float32)
        local[here] = total.astype(jnp.bfloat16)

    def begin(self, s):
        self.copy(s, 0).start()

    def pair(self, s):
        array, first, width = self.stages[s]
        place = self.place
        columns = pl.ds(first, width)
        self.copy(s, 0).wait_recv()
        self.add(s, place.xy_d, self.from_sib[array][place.xy_d, :, columns])
        self.copy(s, 1).start()
        self.copy(s, 2).start()
        for block in (place.xy_x, place.xy_y, place.xy):
            self.add(s, block, self.from_sib[array][block, :, columns])

    def cross(self, s):
        array, first, width = self.stages[s]
        place = self.place
        columns = pl.ds(first, width)
        half = 2 * SHARE_ROWS[array]
        self.copy(s, 1).wait_recv()
        self.add(s, place.xy_y, self.diag_x[array][:, columns], pl.ds(0, half))
        self.copy(s, 4).start()
        self.copy(s, 2).wait_recv()
        self.add(s, place.xy_x, self.diag_y[array][:, columns], pl.ds(half, half))
        self.copy(s, 3).start()

    def square(self, s):
        array, first, width = self.stages[s]
        place = self.place
        columns = pl.ds(first, width)
        rows = SHARE_ROWS[array]
        self.copy(s, 3).wait_recv()
        self.copy(s, 4).wait_recv()
        local = self.local(s)
        for other in range(4):
            piece = pl.ds(rows * other, rows)
            total = (
                local[place.xy, place.core, piece].astype(jnp.float32)
                + self.from_x[array][piece, columns].astype(jnp.float32)
                + self.from_y[array][piece, columns].astype(jnp.float32)
            )
            self.z_out[array][other, :, columns] = total.astype(jnp.bfloat16)
        for k in range(3):
            self.copy(s, 5 + k).start()

    def settle(self, s):
        array, first, width = self.stages[s]
        columns = pl.ds(first, width)
        total = self.z_out[array][self.place.z, :, columns].astype(jnp.float32)
        for k in range(3):
            self.copy(s, 5 + k).wait_recv()
            total = total + self.z_in[array][k, :, columns].astype(jnp.float32)
        self.outputs(s, total)

    def step(self, t):
        count = len(self.stages)
        for lag, work in enumerate((self.begin, self.pair, self.cross, self.square, self.settle)):
            if 0 <= t - lag < count:
                work(t - lag)

    def finish(self):
        for s in range(len(self.stages)):
            for index in range(8):
                self.copy(s, index).wait_send()


def gather_kernel(*refs):
    shards, outs, whole, parts = refs[0:4], refs[4:8], refs[8:12], refs[12:15]
    gather_sems, out_sem = refs[15:19], refs[19]
    place = Place()
    place.barrier()
    gather = Gather(place, shards, whole, parts, gather_sems)
    gather.begin()
    count = len(GATHER_STAGES)
    copies = []
    for t in range(count + 3):
        gather.step(t)
        if t >= 3:
            array, first, width = GATHER_STAGES[t - 3]
            columns = pl.ds(first, width)
            copies.append(
                pltpu.make_async_copy(
                    whole[array].at[:, columns], outs[array].at[:, columns], out_sem.at[t - 3]
                )
            )
            copies[-1].start()
    gather.finish()
    for copy in copies:
        copy.wait()


def gather_all(shards):
    rows = [32 * count for count in SHARE_ROWS]
    kind = jnp.bfloat16
    return pl.pallas_call(
        gather_kernel,
        out_shape=tuple(jax.ShapeDtypeStruct((r, w), kind) for r, w in zip(rows, WIDTHS)),
        in_specs=[pl.BlockSpec(memory_space=pltpu.VMEM)] * 4,
        out_specs=tuple(pl.BlockSpec(memory_space=pl.ANY) for _ in range(4)),
        scratch_shapes=[pltpu.VMEM((r, w), kind) for r, w in zip(rows, WIDTHS)]
        + [pltpu.VMEM((3, r, w), kind) for r, w in zip(SHARE_ROWS[:3], WIDTHS[:3])]
        + Gather.scratch()
        + [pltpu.SemaphoreType.DMA((len(GATHER_STAGES),))],
        compiler_params=pltpu.CompilerParams(
            collective_id=0, has_side_effects=True, vmem_limit_bytes=60 * 2**20
        ),
    )(*shards)


def scatter_kernel(*refs):
    grads, outs, local, buffers = refs[0:4], refs[4:8], refs[8:12], refs[12:40]
    sems, in_sem = refs[40:42], refs[42]
    place = Place()
    copies = []
    for s, (array, first, width) in enumerate(SCATTER_STAGES):
        columns = pl.ds(first, width)
        copies.append(
            pltpu.make_async_copy(
                grads[array].at[:, :, :, columns], local[array].at[:, :, :, columns], in_sem.at[s]
            )
        )
        copies[-1].start()
    place.barrier()

    def part(s):
        array, first, width = SCATTER_STAGES[s]
        return local[array].at[:, :, :, pl.ds(first, width)]

    def outputs(s, total):
        array, first, width = SCATTER_STAGES[s]
        outs[array][:, pl.ds(first, width)] = total

    scatter = Scatter(place, part, buffers, outputs, sems)
    for t in range(len(SCATTER_STAGES) + 4):
        if t < len(SCATTER_STAGES):
            copies[t].wait()
        scatter.step(t)
    scatter.finish()


def scatter_all(grads):
    kind = jnp.bfloat16
    return pl.pallas_call(
        scatter_kernel,
        out_shape=tuple(
            jax.ShapeDtypeStruct((r, w), jnp.float32) for r, w in zip(SHARE_ROWS, WIDTHS)
        ),
        in_specs=[pl.BlockSpec(memory_space=pl.ANY)] * 4,
        out_specs=tuple(pl.BlockSpec(memory_space=pltpu.VMEM) for _ in range(4)),
        scratch_shapes=[
            pltpu.VMEM((4, 2, 4 * r, w), kind) for r, w in zip(SHARE_ROWS, WIDTHS)
        ]
        + Scatter.scratch()
        + Scatter.semaphores()
        + [pltpu.SemaphoreType.DMA((len(SCATTER_STAGES),))],
        compiler_params=pltpu.CompilerParams(
            collective_id=1, has_side_effects=True, vmem_limit_bytes=60 * 2**20
        ),
    )(*[grad.reshape(4, 2, 4 * r, w) for grad, r, w in zip(grads, SHARE_ROWS, WIDTHS)])


def local_fast(
    document_tokens,
    document_lengths,
    query_tokens,
    query_lengths,
    weight_query,
    weight_key,
    weight_value,
    weight_out,
    weight_gate,
    weight_up,
    weight_down,
    weight_proj,
    norm_gains,
    rel_table,
    document_cotangent,
    query_cotangent,
):
    shards = (
        jnp.concatenate(
            [w.reshape(-1, D) for w in (weight_query, weight_key, weight_value)], axis=1
        ),
        jnp.concatenate([weight_out.reshape(-1, D), weight_proj.reshape(-1, PROJ)], axis=1),
        jnp.stack(
            [weight_gate.reshape(-1, 4, D), weight_up.reshape(-1, 4, D)], axis=2
        ).reshape(-1, 2 * FF),
        weight_down.reshape(-1, D),
    )
    qkv_mat, out_proj_mat, gate_up_mat, down_mat = gather_all(shards)
    gains_all, table_all = (
        lax.all_gather(norm_gains, "fsdp", axis=0, tiled=True),
        lax.all_gather(rel_table, "fsdp", axis=0, tiled=True),
    )
    gain_rows = gains_all.astype(jnp.float32).reshape(3, D)
    table_mat = table_all.reshape(BUCKETS, HEADS)
    documents = document_tokens.shape[0]
    queries_here = query_tokens.shape[0]
    doc_rows = documents * DOC_LEN
    doc_segments = segment_ids(document_lengths, DOC_LEN)
    query_segments = segment_ids(query_lengths.reshape(queries_here, 1), QRY_LEN)
    doc_allowed = doc_segments[:, None, :, None] == doc_segments[:, None, None, :]
    query_allowed = query_segments[:, None, :, None] == query_segments[:, None, None, :]
    doc_onehot = bucket_onehot(DOC_LEN)
    query_onehot = bucket_onehot(QRY_LEN)
    doc_bias = bias_rows(table_mat, doc_onehot, DOC_LEN)
    query_bias = bias_rows(table_mat, query_onehot, QRY_LEN)
    settings = [(doc_bias, doc_allowed, doc_onehot)]
    settings.append((query_bias, query_allowed, query_onehot))

    def split_blocks(matrix):
        blocks_out = [matrix[0:DOC_LEN].reshape(1, DOC_LEN, HEADS, HEAD_DIM)]
        blocks_out.append(matrix[doc_rows:].reshape(queries_here, QRY_LEN, HEADS, HEAD_DIM))
        return blocks_out

    query_mat, key_mat, value_mat = (qkv_mat[:, i * D : (i + 1) * D] for i in range(3))
    out_mat, proj_mat = out_proj_mat[:, :D], out_proj_mat[:, D:]
    inputs = jnp.concatenate(
        [document_tokens.reshape(doc_rows, D), query_tokens.reshape(-1, D)], axis=0
    )
    residual_in = inputs.astype(jnp.float32)
    normed_one, norm_one_back = jax.vjp(rms_norm, residual_in, gain_rows[0])
    normed_one = normed_one.astype(jnp.bfloat16)
    queries = jnp.dot(normed_one, query_mat, preferred_element_type=jnp.float32).astype(
        jnp.bfloat16
    )
    key_rows = jnp.dot(normed_one, key_mat, preferred_element_type=jnp.float32).astype(jnp.bfloat16)
    values = jnp.dot(normed_one, value_mat, preferred_element_type=jnp.float32).astype(jnp.bfloat16)
    query_blocks = split_blocks(queries)
    key_blocks = split_blocks(key_rows)
    value_blocks = split_blocks(values)
    contexts = []
    log_totals = []
    for query_block, key_block, value_block, setting in zip(
        query_blocks, key_blocks, value_blocks, settings
    ):
        context_block, log_total = attend(
            query_block, key_block, value_block, setting[0], setting[1]
        )
        contexts.append(context_block.reshape(-1, D))
        log_totals.append(log_total)
    context = jnp.concatenate(contexts, axis=0)
    hidden = residual_in + jnp.dot(context, out_mat, preferred_element_type=jnp.float32)
    normed_two, norm_two_back = jax.vjp(rms_norm, hidden, gain_rows[1])
    normed_two = normed_two.astype(jnp.bfloat16)
    def gated(mixed):
        parts = [mixed[:, i * D : (i + 1) * D] for i in range(8)]
        return jnp.concatenate([gated_unit(parts[2 * i], parts[2 * i + 1]) for i in range(4)], axis=1)

    gate_up = jnp.dot(normed_two, gate_up_mat, preferred_element_type=jnp.float32)
    inner, gated_back = jax.vjp(gated, gate_up)
    inner = inner.astype(jnp.bfloat16)
    final = hidden + jnp.dot(inner, down_mat, preferred_element_type=jnp.float32)
    normed_three, norm_three_back = jax.vjp(rms_norm, final, gain_rows[2])
    normed_three = normed_three.astype(jnp.bfloat16)
    output = jnp.dot(normed_three, proj_mat, preferred_element_type=jnp.float32).astype(
        jnp.bfloat16
    )
    cotangent = jnp.concatenate(
        [document_cotangent.reshape(doc_rows, PROJ), query_cotangent.reshape(-1, PROJ)], axis=0
    )
    grad_final, grad_gain_three = norm_three_back(times_transposed(cotangent, proj_mat))
    grad_ffn = grad_final.astype(jnp.bfloat16)
    (grad_gate_up_f,) = gated_back(times_transposed(grad_ffn, down_mat))
    grad_gate_up = grad_gate_up_f.astype(jnp.bfloat16)
    grad_normed_two = times_transposed(grad_gate_up, gate_up_mat)
    grad_hidden_part, grad_gain_two = norm_two_back(grad_normed_two)
    grad_hidden = grad_final + grad_hidden_part
    grad_branch = grad_hidden.astype(jnp.bfloat16)
    grad_context = times_transposed(grad_branch, out_mat).astype(jnp.bfloat16)
    table_grad = jnp.zeros((HEADS, BUCKETS), jnp.float32)
    grad_query_parts = []
    grad_key_parts = []
    grad_value_parts = []
    for query_block, key_block, value_block, setting, log_total, grad_block in zip(
        query_blocks, key_blocks, value_blocks, settings, log_totals, split_blocks(grad_context)
    ):
        grad_q_block, grad_k_block, grad_v_block, grad_scores = attend_back(
            query_block, key_block, value_block, setting[0], setting[1], log_total, grad_block
        )
        table_grad = table_grad + bias_grads(grad_scores, setting[2])
        grad_query_parts.append(grad_q_block.reshape(-1, D))
        grad_key_parts.append(grad_k_block.reshape(-1, D))
        grad_value_parts.append(grad_v_block.reshape(-1, D))
    grad_qkv = jnp.concatenate(
        [jnp.concatenate(p, axis=0) for p in (grad_query_parts, grad_key_parts, grad_value_parts)],
        axis=1,
    )
    grad_normed_one = times_transposed(grad_qkv, qkv_mat)
    grad_input_part, grad_gain_one = norm_one_back(grad_normed_one)
    grad_inputs = (grad_hidden + grad_input_part).astype(jnp.bfloat16)
    summed = scatter_all(
        (
            outer_sum(normed_one, grad_qkv).astype(jnp.bfloat16),
            jnp.concatenate(
                [outer_sum(context, grad_branch), outer_sum(normed_three, cotangent)], axis=1
            ).astype(jnp.bfloat16),
            outer_sum(normed_two, grad_gate_up).astype(jnp.bfloat16),
            outer_sum(inner, grad_ffn).astype(jnp.bfloat16),
        )
    )
    mixed = summed[2].reshape(24, 4, 2, D)
    shares = (
        summed[0][:, :D].reshape(-1),
        summed[0][:, D : 2 * D].reshape(-1),
        summed[0][:, 2 * D :].reshape(-1),
        summed[1][:, :D].reshape(-1),
        mixed[:, :, 0].reshape(-1),
        mixed[:, :, 1].reshape(-1),
        summed[3].reshape(-1),
        summed[1][:, D:].reshape(-1),
    )
    gain_grads = jnp.concatenate([grad_gain_one, grad_gain_two, grad_gain_three], axis=0)
    table_flat = jnp.transpose(table_grad).reshape(-1)
    gain_whole, table_whole = lax.psum((gain_grads, table_flat), ("dp", "fsdp"))
    fsdp_index = lax.axis_index("fsdp")
    fsdp_count = lax.axis_size("fsdp")
    gain_share = 3 * D // fsdp_count
    table_share = BUCKETS * HEADS // fsdp_count
    own_gains = lax.dynamic_slice_in_dim(gain_whole, fsdp_index * gain_share, gain_share)
    own_table = lax.dynamic_slice_in_dim(table_whole, fsdp_index * table_share, table_share)
    return (
        output[:doc_rows].reshape(documents, DOC_LEN, PROJ),
        output[doc_rows:].reshape(queries_here, QRY_LEN, PROJ),
        grad_inputs[:doc_rows].reshape(documents, DOC_LEN, D),
        grad_inputs[doc_rows:].reshape(queries_here, QRY_LEN, D),
        shares[0],
        shares[1],
        shares[2],
        shares[3],
        shares[4],
        shares[5],
        shares[6],
        shares[7],
        own_gains,
        own_table,
    )


def solution(mesh):
    placed = (
        P(("dp", "fsdp"), None, None),
        P(("dp", "fsdp"), None),
        P(("dp", "fsdp"), None, None),
        P(("dp", "fsdp")),
        P(("dp", "fsdp")),
        P(("dp", "fsdp")),
        P(("dp", "fsdp")),
        P(("dp", "fsdp")),
        P(("dp", "fsdp")),
        P(("dp", "fsdp")),
        P(("dp", "fsdp")),
        P(("dp", "fsdp")),
        P("fsdp"),
        P("fsdp"),
        P(("dp", "fsdp"), None, None),
        P(("dp", "fsdp"), None, None),
    )
    return jax.shard_map(
        local_fast if (mesh.shape["dp"], mesh.shape["fsdp"]) == (8, 4) else local,
        mesh=mesh,
        in_specs=placed,
        out_specs=(
            P(("dp", "fsdp"), None, None),
            P(("dp", "fsdp"), None, None),
            P(("dp", "fsdp"), None, None),
            P(("dp", "fsdp"), None, None),
            P(("dp", "fsdp")),
            P(("dp", "fsdp")),
            P(("dp", "fsdp")),
            P(("dp", "fsdp")),
            P(("dp", "fsdp")),
            P(("dp", "fsdp")),
            P(("dp", "fsdp")),
            P(("dp", "fsdp")),
            P("fsdp"),
            P("fsdp"),
        ),
        check_vma=False,
    )
```

```python
import jax
import jax.numpy as jnp
from jax import lax
from jax.experimental import pallas as pl
from jax.experimental.pallas import tpu as pltpu
from jax.sharding import PartitionSpec as P

D = 768
HEADS = 12
HEAD_DIM = 64
FF = 3072
BUCKETS = 32
PROJ = 128
DOC_LEN = 512
QRY_LEN = 32


EPSILON = 1e-06
NEGATIVE = -1e30


def rms_norm(values, gain_row):
    inverse = lax.rsqrt(jnp.mean(values * values, axis=-1, keepdims=True) + EPSILON)
    return values * inverse * gain_row


def gated_unit(gate_in, upper_in):
    return jax.nn.gelu(gate_in, approximate=True) * upper_in


def bucket_ids(length):
    positions = jnp.arange(length, dtype=jnp.int32)
    relative = positions[None, :] - positions[:, None]
    distance = jnp.abs(relative)
    distant = 8 + sum(
        ((distance * distance >= 64 * 2**power).astype(jnp.int32) for power in range(1, 8))
    )
    nearby = jnp.where(distance < 8, distance, distant)
    return nearby + 16 * (relative > 0).astype(jnp.int32)


def bucket_onehot(length):
    flat_ids = bucket_ids(length).reshape(1, length * length)
    labels = jnp.arange(BUCKETS, dtype=jnp.int32).reshape(BUCKETS, 1)
    return (flat_ids == labels).astype(jnp.bfloat16)


def segment_ids(lengths, length):
    boundary = jnp.cumsum(lengths, axis=-1)
    positions = jnp.arange(length, dtype=jnp.int32)
    return jnp.sum((positions[None, :, None] >= boundary[:, None, :]).astype(jnp.int32), axis=-1)


def outer_sum(left_rows, right_rows):
    return lax.dot_general(
        left_rows, right_rows, (((0,), (0,)), ((), ())), preferred_element_type=jnp.float32
    )


def times_transposed(left_rows, matrix):
    return lax.dot_general(
        left_rows, matrix, (((1,), (1,)), ((), ())), preferred_element_type=jnp.float32
    )


def flat_piece(left_rows, right_rows, start, count):
    width = right_rows.shape[1]
    needed = count // width + 2
    padded = jnp.pad(left_rows, ((0, 0), (0, needed)))
    first_row = start // width
    columns = lax.dynamic_slice_in_dim(padded, first_row, needed, 1)
    block = outer_sum(columns, right_rows).reshape(-1)
    return lax.dynamic_slice_in_dim(block, start, count)


def grad_terms(pairs, devices):
    shares = [pair[0].shape[1] * pair[1].shape[1] // devices for pair in pairs]
    total_share = sum(shares)

    def term(start, count):
        blocks = count // total_share
        first_block = start // total_share
        pieces = [
            flat_piece(pair[0], pair[1], first_block * share, blocks * share).reshape(blocks, share)
            for pair, share in zip(pairs, shares)
        ]
        return jnp.concatenate(pieces, axis=1).reshape(-1)

    return (term, total_share, shares)


def split_shares(mine, shares):
    results = []
    offset = 0
    for share in shares:
        results.append(mine[offset : offset + share])
        offset = offset + share
    return results


def bias_rows(table_mat, onehot, length):
    rel_bias = lax.dot_general(
        table_mat, onehot, (((0,), (0,)), ((), ())), preferred_element_type=jnp.float32
    )
    return rel_bias.reshape(1, HEADS, length, length)


def masked_scores(queries, key_rows, rel_bias, allowed):
    scores = (
        jnp.einsum("bqhd,bkhd->bhqk", queries, key_rows, preferred_element_type=jnp.float32)
        + rel_bias
    )
    return jnp.where(allowed, scores, NEGATIVE)


def attend(queries, key_rows, values, rel_bias, allowed):
    scores = masked_scores(queries, key_rows, rel_bias, allowed)
    largest = jnp.max(scores, axis=-1, keepdims=True)
    summed = jnp.sum(jnp.exp(scores - largest), axis=-1, keepdims=True)
    log_total = largest + jnp.log(summed)
    attention = jnp.exp(scores - log_total).astype(jnp.bfloat16)
    context = jnp.einsum("bhqk,bkhd->bqhd", attention, values, preferred_element_type=jnp.float32)
    return (context.astype(jnp.bfloat16), log_total)


def attend_back(queries, key_rows, values, rel_bias, allowed, log_total, grad_context):
    scores = masked_scores(queries, key_rows, rel_bias, allowed)
    attention = jnp.exp(scores - log_total)
    grad_attention = jnp.einsum(
        "bqhd,bkhd->bhqk", grad_context, values, preferred_element_type=jnp.float32
    )
    grad_values = jnp.einsum(
        "bhqk,bqhd->bkhd",
        attention.astype(jnp.bfloat16),
        grad_context,
        preferred_element_type=jnp.float32,
    )
    weighted = jnp.sum(attention * grad_attention, axis=-1, keepdims=True)
    grad_scores = (attention * (grad_attention - weighted)).astype(jnp.bfloat16)
    grad_queries = jnp.einsum(
        "bhqk,bkhd->bqhd", grad_scores, key_rows, preferred_element_type=jnp.float32
    )
    grad_keys = jnp.einsum(
        "bhqk,bqhd->bkhd", grad_scores, queries, preferred_element_type=jnp.float32
    )
    return (
        grad_queries.astype(jnp.bfloat16),
        grad_keys.astype(jnp.bfloat16),
        grad_values.astype(jnp.bfloat16),
        grad_scores,
    )


def bias_grads(grad_scores, onehot):
    members = grad_scores.shape[0]
    flattened = grad_scores.reshape(members * HEADS, -1)
    summed = lax.dot_general(
        flattened, onehot, (((1,), (1,)), ((), ())), preferred_element_type=jnp.float32
    )
    return jnp.sum(summed.reshape(members, HEADS, BUCKETS), axis=0)


def local(
    document_tokens,
    document_lengths,
    query_tokens,
    query_lengths,
    weight_query,
    weight_key,
    weight_value,
    weight_out,
    weight_gate,
    weight_up,
    weight_down,
    weight_proj,
    norm_gains,
    rel_table,
    document_cotangent,
    query_cotangent,
):
    layouts = ((D, D), (D, D), (D, D), (D, D), (D, FF), (D, FF), (FF, D), (D, PROJ))
    devices = lax.axis_size("dp") * lax.axis_size("fsdp")
    gathered = (
        lax.all_gather(weight_query, ("dp", "fsdp"), axis=0, tiled=True),
        lax.all_gather(weight_key, ("dp", "fsdp"), axis=0, tiled=True),
        lax.all_gather(weight_value, ("dp", "fsdp"), axis=0, tiled=True),
        lax.all_gather(weight_out, ("dp", "fsdp"), axis=0, tiled=True),
        lax.all_gather(weight_gate, ("dp", "fsdp"), axis=0, tiled=True),
        lax.all_gather(weight_up, ("dp", "fsdp"), axis=0, tiled=True),
        lax.all_gather(weight_down, ("dp", "fsdp"), axis=0, tiled=True),
        lax.all_gather(weight_proj, ("dp", "fsdp"), axis=0, tiled=True),
    )
    matrices = [flat_rows.reshape(layout) for flat_rows, layout in zip(gathered, layouts)]
    gains_all, table_all = (
        lax.all_gather(norm_gains, "fsdp", axis=0, tiled=True),
        lax.all_gather(rel_table, "fsdp", axis=0, tiled=True),
    )
    gain_rows = gains_all.astype(jnp.float32).reshape(3, D)
    table_mat = table_all.reshape(BUCKETS, HEADS)
    documents = document_tokens.shape[0]
    queries_here = query_tokens.shape[0]
    doc_rows = documents * DOC_LEN
    doc_segments = segment_ids(document_lengths, DOC_LEN)
    query_segments = segment_ids(query_lengths.reshape(queries_here, 1), QRY_LEN)
    doc_allowed = doc_segments[:, None, :, None] == doc_segments[:, None, None, :]
    query_allowed = query_segments[:, None, :, None] == query_segments[:, None, None, :]
    doc_onehot = bucket_onehot(DOC_LEN)
    query_onehot = bucket_onehot(QRY_LEN)
    doc_bias = bias_rows(table_mat, doc_onehot, DOC_LEN)
    query_bias = bias_rows(table_mat, query_onehot, QRY_LEN)
    settings = [(doc_bias, doc_allowed, doc_onehot)]
    settings.append((query_bias, query_allowed, query_onehot))

    def split_blocks(matrix):
        blocks_out = [matrix[0:DOC_LEN].reshape(1, DOC_LEN, HEADS, HEAD_DIM)]
        blocks_out.append(matrix[doc_rows:].reshape(queries_here, QRY_LEN, HEADS, HEAD_DIM))
        return blocks_out

    query_mat, key_mat, value_mat, out_mat, gate_mat, up_mat, down_mat, proj_mat = matrices
    inputs = jnp.concatenate(
        [document_tokens.reshape(doc_rows, D), query_tokens.reshape(-1, D)], axis=0
    )
    residual_in = inputs.astype(jnp.float32)
    normed_one, norm_one_back = jax.vjp(rms_norm, residual_in, gain_rows[0])
    normed_one = normed_one.astype(jnp.bfloat16)
    queries = jnp.dot(normed_one, query_mat, preferred_element_type=jnp.float32).astype(
        jnp.bfloat16
    )
    key_rows = jnp.dot(normed_one, key_mat, preferred_element_type=jnp.float32).astype(jnp.bfloat16)
    values = jnp.dot(normed_one, value_mat, preferred_element_type=jnp.float32).astype(jnp.bfloat16)
    query_blocks = split_blocks(queries)
    key_blocks = split_blocks(key_rows)
    value_blocks = split_blocks(values)
    contexts = []
    log_totals = []
    for query_block, key_block, value_block, setting in zip(
        query_blocks, key_blocks, value_blocks, settings
    ):
        context_block, log_total = attend(
            query_block, key_block, value_block, setting[0], setting[1]
        )
        contexts.append(context_block.reshape(-1, D))
        log_totals.append(log_total)
    context = jnp.concatenate(contexts, axis=0)
    hidden = residual_in + jnp.dot(context, out_mat, preferred_element_type=jnp.float32)
    normed_two, norm_two_back = jax.vjp(rms_norm, hidden, gain_rows[1])
    normed_two = normed_two.astype(jnp.bfloat16)
    gate = jnp.dot(normed_two, gate_mat, preferred_element_type=jnp.float32)
    upper = jnp.dot(normed_two, up_mat, preferred_element_type=jnp.float32)
    inner, gated_back = jax.vjp(gated_unit, gate, upper)
    inner = inner.astype(jnp.bfloat16)
    final = hidden + jnp.dot(inner, down_mat, preferred_element_type=jnp.float32)
    normed_three, norm_three_back = jax.vjp(rms_norm, final, gain_rows[2])
    normed_three = normed_three.astype(jnp.bfloat16)
    output = jnp.dot(normed_three, proj_mat, preferred_element_type=jnp.float32).astype(
        jnp.bfloat16
    )
    again = (
        lax.all_gather(weight_query, ("dp", "fsdp"), axis=0, tiled=True),
        lax.all_gather(weight_key, ("dp", "fsdp"), axis=0, tiled=True),
        lax.all_gather(weight_value, ("dp", "fsdp"), axis=0, tiled=True),
        lax.all_gather(weight_out, ("dp", "fsdp"), axis=0, tiled=True),
        lax.all_gather(weight_gate, ("dp", "fsdp"), axis=0, tiled=True),
        lax.all_gather(weight_up, ("dp", "fsdp"), axis=0, tiled=True),
        lax.all_gather(weight_down, ("dp", "fsdp"), axis=0, tiled=True),
        lax.all_gather(weight_proj, ("dp", "fsdp"), axis=0, tiled=True),
    )
    back_mats = [flat_rows.reshape(layout) for flat_rows, layout in zip(again, layouts)]
    back_query, back_key, back_value, back_out, back_gate, back_up, back_down, back_proj = back_mats
    cotangent = jnp.concatenate(
        [document_cotangent.reshape(doc_rows, PROJ), query_cotangent.reshape(-1, PROJ)], axis=0
    )
    grad_final, grad_gain_three = norm_three_back(times_transposed(cotangent, back_proj))
    grad_ffn = grad_final.astype(jnp.bfloat16)
    grad_gate_f, grad_upper_f = gated_back(times_transposed(grad_ffn, back_down))
    grad_gate_b = grad_gate_f.astype(jnp.bfloat16)
    grad_upper_b = grad_upper_f.astype(jnp.bfloat16)
    grad_normed_two = times_transposed(grad_gate_b, back_gate) + times_transposed(
        grad_upper_b, back_up
    )
    grad_hidden_part, grad_gain_two = norm_two_back(grad_normed_two)
    grad_hidden = grad_final + grad_hidden_part
    ffn_pairs = [
        (normed_two, grad_gate_b),
        (normed_two, grad_upper_b),
        (inner, grad_ffn),
        (normed_three, cotangent),
    ]
    grad_branch = grad_hidden.astype(jnp.bfloat16)
    grad_context = times_transposed(grad_branch, back_out).astype(jnp.bfloat16)
    table_grad = jnp.zeros((HEADS, BUCKETS), jnp.float32)
    grad_query_parts = []
    grad_key_parts = []
    grad_value_parts = []
    for query_block, key_block, value_block, setting, log_total, grad_block in zip(
        query_blocks, key_blocks, value_blocks, settings, log_totals, split_blocks(grad_context)
    ):
        grad_q_block, grad_k_block, grad_v_block, grad_scores = attend_back(
            query_block, key_block, value_block, setting[0], setting[1], log_total, grad_block
        )
        table_grad = table_grad + bias_grads(grad_scores, setting[2])
        grad_query_parts.append(grad_q_block.reshape(-1, D))
        grad_key_parts.append(grad_k_block.reshape(-1, D))
        grad_value_parts.append(grad_v_block.reshape(-1, D))
    grad_queries = jnp.concatenate(grad_query_parts, axis=0)
    grad_keys = jnp.concatenate(grad_key_parts, axis=0)
    grad_values = jnp.concatenate(grad_value_parts, axis=0)
    grad_normed_one = (
        times_transposed(grad_queries, back_query)
        + times_transposed(grad_keys, back_key)
        + times_transposed(grad_values, back_value)
    )
    grad_input_part, grad_gain_one = norm_one_back(grad_normed_one)
    grad_inputs = (grad_hidden + grad_input_part).astype(jnp.bfloat16)
    attn_pairs = [
        (normed_one, grad_queries),
        (normed_one, grad_keys),
        (normed_one, grad_values),
        (context, grad_branch),
    ]
    all_term, all_total, all_shares = grad_terms(attn_pairs + ffn_pairs, devices)
    shares = tuple(
        split_shares(
            lax.psum_scatter(
                all_term(jnp.int32(0), lax.axis_size(("dp", "fsdp")) * all_total),
                ("dp", "fsdp"),
                scatter_dimension=0,
                tiled=True,
            ),
            all_shares,
        )
    )
    gain_grads = jnp.concatenate([grad_gain_one, grad_gain_two, grad_gain_three], axis=0)
    table_flat = jnp.transpose(table_grad).reshape(-1)
    gain_whole, table_whole = lax.psum((gain_grads, table_flat), ("dp", "fsdp"))
    fsdp_index = lax.axis_index("fsdp")
    fsdp_count = lax.axis_size("fsdp")
    gain_share = 3 * D // fsdp_count
    table_share = BUCKETS * HEADS // fsdp_count
    own_gains = lax.dynamic_slice_in_dim(gain_whole, fsdp_index * gain_share, gain_share)
    own_table = lax.dynamic_slice_in_dim(table_whole, fsdp_index * table_share, table_share)
    return (
        output[:doc_rows].reshape(documents, DOC_LEN, PROJ),
        output[doc_rows:].reshape(queries_here, QRY_LEN, PROJ),
        grad_inputs[:doc_rows].reshape(documents, DOC_LEN, D),
        grad_inputs[doc_rows:].reshape(queries_here, QRY_LEN, D),
        shares[0],
        shares[1],
        shares[2],
        shares[3],
        shares[4],
        shares[5],
        shares[6],
        shares[7],
        own_gains,
        own_table,
    )


WIDTHS = (3 * D, D + PROJ, 2 * FF, D)
SHARE_ROWS = (24, 24, 24, 96)
GATHER_STAGES = (
    (0, 0, 768),
    (0, 768, 768),
    (0, 1536, 768),
    (1, 0, 896),
    (2, 0, 1536),
    (2, 1536, 1536),
    (2, 3072, 1536),
    (2, 4608, 1536),
    (3, 0, 384),
    (3, 384, 384),
)
MESH_ID = pl.DeviceIdType.MESH


def remote(source, target, send_sem, recv_sem, device):
    return pltpu.make_async_remote_copy(
        src_ref=source,
        dst_ref=target,
        send_sem=send_sem,
        recv_sem=recv_sem,
        device_id=device,
        device_id_type=MESH_ID,
    )


class Place:
    def __init__(self):
        self.dp = lax.axis_index("dp")
        self.z = lax.axis_index("fsdp")
        self.core = lax.rem(self.dp, 2)
        self.xy = self.dp // 2
        self.xy_x = self.xy + 1 - 2 * lax.rem(self.xy, 2)
        self.xy_y = lax.rem(self.xy + 2, 4)
        self.xy_d = 3 - self.xy
        self.sib = self.dp + 1 - 2 * self.core
        self.dp_x = 2 * self.xy_x + self.core
        self.dp_y = 2 * self.xy_y + self.core
        self.dp_d = 2 * self.xy_d + self.core
        self.zs = [lax.rem(self.z + step, 4) for step in (1, 2, 3)]
        self.to_sib = {"dp": self.sib}
        self.to_x = {"dp": self.dp_x}
        self.to_y = {"dp": self.dp_y}
        self.to_z = [{"fsdp": other} for other in self.zs]

    def barrier(self):
        semaphore = pltpu.get_barrier_semaphore()
        for device in [self.to_sib, self.to_x, self.to_y] + self.to_z:
            pl.semaphore_signal(semaphore, inc=1, device_id=device, device_id_type=MESH_ID)
        pl.semaphore_wait(semaphore, 6)


class Gather:
    def __init__(self, place, shards, whole, parts, sems):
        self.place, self.shards, self.whole, self.parts = place, shards, whole, parts
        (self.z_send, self.z_recv, self.send, self.recv) = sems
        self.stages = GATHER_STAGES

    @staticmethod
    def scratch():
        count = len(GATHER_STAGES)
        dma = pltpu.SemaphoreType.DMA
        return [dma((count, 3)), dma((count, 3)), dma((count, 9)), dma((count, 9))]

    def z_copy(self, s, k):
        array, first, width = self.stages[s]
        place = self.place
        columns = pl.ds(first, width)
        if array == 3:
            rows = pl.ds(pl.multiple_of(384 * place.dp + 96 * place.z, 96), 96)
            target = self.whole[3].at[rows, columns]
        else:
            target = self.parts[array].at[k, :, columns]
        return remote(
            self.shards[array].at[:, columns],
            target,
            self.z_send.at[s, k],
            self.z_recv.at[s, k],
            place.to_z[k],
        )

    def block(self, s, dp, half=None):
        array, first, width = self.stages[s]
        count = 4 * SHARE_ROWS[array]
        start = count * dp
        if half is not None:
            count = count // 2
            start = start + half * count
        return self.whole[array].at[
            pl.ds(pl.multiple_of(start, 48), count), pl.ds(first, width)
        ]

    def hop(self, s, index):
        place = self.place
        dp, half, device = (
            (place.dp, None, place.to_x),
            (place.dp, None, place.to_y),
            (place.dp_x, 0, place.to_y),
            (place.dp_y, 1, place.to_x),
            (place.dp, None, place.to_sib),
            (place.dp_x, None, place.to_sib),
            (place.dp_y, None, place.to_sib),
            (place.dp_d, 0, place.to_sib),
            (place.dp_d, 1, place.to_sib),
        )[index]
        block = self.block(s, dp, half)
        return remote(block, block, self.send.at[s, index], self.recv.at[s, index], device)

    def begin(self, s):
        for k in range(3):
            self.z_copy(s, k).start()

    def spread(self, s):
        array, first, width = self.stages[s]
        place = self.place
        columns = pl.ds(first, width)
        for k in range(3):
            self.z_copy(s, k).wait_recv()
        if array == 3:
            rows = pl.ds(pl.multiple_of(384 * place.dp + 96 * place.z, 96), 96)
            self.whole[3][rows, columns] = self.shards[3][:, columns]
        else:
            pieces = []
            for other in range(4):
                piece = self.shards[array][:, columns]
                for k in range(3):
                    here = lax.rem(place.z + 3 - k, 4) == other
                    piece = jnp.where(here, self.parts[array][k, :, columns], piece)
                pieces.append(piece)
            rows = pl.ds(pl.multiple_of(96 * place.dp, 96), 96)
            self.whole[array][rows, columns] = jnp.concatenate(pieces, axis=0)
        for index in (0, 1, 4):
            self.hop(s, index).start()

    def relay(self, s):
        self.hop(s, 0).wait_recv()
        self.hop(s, 2).start()
        self.hop(s, 5).start()
        self.hop(s, 1).wait_recv()
        self.hop(s, 3).start()
        self.hop(s, 6).start()

    def hand_over(self, s):
        self.hop(s, 2).wait_recv()
        self.hop(s, 7).start()
        self.hop(s, 3).wait_recv()
        self.hop(s, 8).start()

    def arrive(self, s):
        for index in range(4, 9):
            self.hop(s, index).wait_recv()

    def step(self, t):
        count = len(self.stages)
        for lag, work in enumerate((self.spread, self.relay, self.hand_over, self.arrive)):
            if 0 <= t - lag < count:
                work(t - lag)

    def finish(self):
        for s in range(len(self.stages)):
            for k in range(3):
                self.z_copy(s, k).wait_send()
            for index in range(9):
                self.hop(s, index).wait_send()


SCATTER_WIDTHS = (3 * D, D + PROJ, 2 * FF, 4 * D)
SCATTER_STAGES = (
    (3, 0, 1536),
    (3, 1536, 1536),
    (2, 0, 1536),
    (2, 1536, 1536),
    (2, 3072, 1536),
    (2, 4608, 1536),
    (1, 0, 896),
    (0, 0, 768),
    (0, 768, 768),
    (0, 1536, 768),
)
SCATTER_SLOTS = (
    (0, 0, None),
    (1, 0, None),
    (2, 0, None),
    (3, 0, None),
    (0, 0, 0),
    (1, 0, 1),
    (2, 0, 2),
    (3, 0, 3),
    (3, 768, 3),
    (0, 0, 4),
)


class Scatter:
    def __init__(self, place, buffers, settled, sems):
        self.place, self.settled = place, settled
        self.local_all, self.sib_all = buffers[0:2]
        self.from_x, self.from_y = buffers[2:6], buffers[6:10]
        self.diag_x, self.diag_y = buffers[10:14], buffers[14:18]
        self.z_out, self.z_in = buffers[18:22], buffers[22:26]
        self.send, self.recv, self.credit = sems
        self.begun = {}
        self.sent = set()

    @staticmethod
    def scratch():
        kind = jnp.bfloat16
        shapes = [pltpu.VMEM((4, 4, 2, 96, 1536), kind), pltpu.VMEM((4, 4, 96, 1536), kind)]
        shapes += [pltpu.VMEM((96, w), kind) for w in SCATTER_WIDTHS] * 2
        shapes += [pltpu.VMEM((48, w), kind) for w in SCATTER_WIDTHS] * 2
        pieces = [(24, w) for w in SCATTER_WIDTHS[:3]] + [(96, D)]
        shapes += [pltpu.VMEM((4, r, w), kind) for r, w in pieces]
        shapes += [pltpu.VMEM((3, r, w), kind) for r, w in pieces]
        return shapes

    @staticmethod
    def semaphores():
        count = len(SCATTER_STAGES)
        dma = pltpu.SemaphoreType.DMA
        return [dma((count, 8)), dma((count, 8)), pltpu.SemaphoreType.REGULAR((count,))]

    def local(self, s):
        slot, offset, _ = SCATTER_SLOTS[s]
        width = SCATTER_STAGES[s][2]
        return self.local_all.at[slot, :, :, :, pl.ds(offset, width)]

    def columns(self, s):
        return pl.ds(SCATTER_STAGES[s][1], SCATTER_STAGES[s][2])

    def z_columns(self, s):
        array, first, width = SCATTER_STAGES[s]
        return pl.ds(first // 4, width // 4) if array == 3 else pl.ds(first, width)

    def copy(self, s, index):
        array, first, width = SCATTER_STAGES[s]
        place = self.place
        columns = self.columns(s)
        local = self.local(s)
        if index == 0:
            source = local.at[:, 1 - place.core]
            target = self.sib_all.at[s % 4, :, :, pl.ds(0, width)]
            device = place.to_sib
        elif index == 1:
            source = local.at[place.xy_d, place.core, pl.ds(0, 48)]
            target = self.diag_x[array].at[:, columns]
            device = place.to_x
        elif index == 2:
            source = local.at[place.xy_d, place.core, pl.ds(48, 48)]
            target = self.diag_y[array].at[:, columns]
            device = place.to_y
        elif index == 3:
            source = local.at[place.xy_x, place.core]
            target = self.from_x[array].at[:, columns]
            device = place.to_x
        elif index == 4:
            source = local.at[place.xy_y, place.core]
            target = self.from_y[array].at[:, columns]
            device = place.to_y
        else:
            k = index - 5
            source = self.z_out[array].at[place.zs[k], :, self.z_columns(s)]
            target = self.z_in[array].at[k, :, self.z_columns(s)]
            device = place.to_z[k]
        return remote(source, target, self.send.at[s, index], self.recv.at[s, index], device)

    def add(self, s, block, other, rows=slice(None)):
        local = self.local(s)
        here = (block, self.place.core, rows)
        total = local[here].astype(jnp.float32) + other.astype(jnp.float32)
        local[here] = total.astype(jnp.bfloat16)

    def free(self, s):
        before = SCATTER_SLOTS[s][2]
        if before is not None and before not in self.sent:
            self.sent.add(before)
            for index in range(5):
                self.copy(before, index).wait_send()

    def begin(self, s):
        if s >= 4:
            pl.semaphore_wait(self.credit.at[s], 1)
        self.copy(s, 0).start()

    def pair(self, s):
        place = self.place
        columns = pl.ds(0, SCATTER_STAGES[s][2])
        self.copy(s, 0).wait_recv()
        self.add(s, place.xy_d, self.sib_all[s % 4, place.xy_d, :, columns])
        self.copy(s, 1).start()
        self.copy(s, 2).start()
        for block in (place.xy_x, place.xy_y, place.xy):
            self.add(s, block, self.sib_all[s % 4, block, :, columns])
        if s + 4 < len(SCATTER_STAGES):
            pl.semaphore_signal(
                self.credit.at[s + 4], inc=1, device_id=place.to_sib, device_id_type=MESH_ID
            )

    def cross(self, s):
        array = SCATTER_STAGES[s][0]
        place = self.place
        columns = self.columns(s)
        self.copy(s, 1).wait_recv()
        self.add(s, place.xy_y, self.diag_x[array][:, columns], slice(0, 48))
        self.copy(s, 4).start()
        self.copy(s, 2).wait_recv()
        self.add(s, place.xy_x, self.diag_y[array][:, columns], slice(48, 96))
        self.copy(s, 3).start()

    def square(self, s):
        array, first, width = SCATTER_STAGES[s]
        place = self.place
        self.copy(s, 3).wait_recv()
        self.copy(s, 4).wait_recv()
        local = self.local(s)
        for other in range(4):
            if array == 3:
                rows, inside = slice(0, 96), pl.ds(384 * other, 384)
                outside = pl.ds(first + 384 * other, 384)
            else:
                rows, inside = slice(24 * other, 24 * other + 24), pl.ds(0, width)
                outside = pl.ds(first, width)
            total = (
                local[place.xy, place.core, rows, inside].astype(jnp.float32)
                + self.from_x[array][rows, outside].astype(jnp.float32)
                + self.from_y[array][rows, outside].astype(jnp.float32)
            )
            self.z_out[array][other, :, self.z_columns(s)] = total.astype(jnp.bfloat16)
        for k in range(3):
            self.copy(s, 5 + k).start()

    def settle(self, s):
        array = SCATTER_STAGES[s][0]
        columns = self.z_columns(s)
        total = self.z_out[array][self.place.z, :, columns].astype(jnp.float32)
        for k in range(3):
            self.copy(s, 5 + k).wait_recv()
            total = total + self.z_in[array][k, :, columns].astype(jnp.float32)
        self.settled(s, total)

    def step(self, turn, s=None):
        if s is not None:
            self.begun[s] = turn
        for other in sorted(self.begun, reverse=True):
            lag = turn - self.begun[other]
            if lag < 5:
                (self.begin, self.pair, self.cross, self.square, self.settle)[lag](other)

    def finish(self):
        for s in range(len(SCATTER_STAGES)):
            for index in range(8):
                if index >= 5 or s not in self.sent:
                    self.copy(s, index).wait_send()


ROW_BLOCK = 128
SCALE = 0.7978845608028654
BF = jnp.bfloat16
F32 = jnp.float32
ROWS_ALL = 768
NEAR = 3 * ROW_BLOCK


def dot(left, right, left_dim=1, right_dim=0):
    return lax.dot_general(
        left, right, (((left_dim,), (right_dim,)), ((), ())), preferred_element_type=F32
    )


def loop(count, body):
    def step(index, carry):
        body(index)
        return carry

    lax.fori_loop(0, count, step, 0)


def aligned(start, multiple, size):
    return pl.ds(pl.multiple_of(start, multiple), size)


def unflatten(flat, wide, target, start_of):
    lines = flat.shape[0]
    rows = target.shape[0]
    blocks = lines // rows
    wide[0:lines] = flat[...].astype(F32)
    for block in range(blocks):
        first = start_of(block)
        target[:, first : first + 128] = wide[pl.ds(block, rows, blocks), :].astype(BF)


def marks_of(relative):
    distance = jnp.abs(relative)
    distant = jnp.full_like(distance, 8)
    for power in range(1, 8):
        distant = distant + (distance * distance >= 64 * 2**power).astype(jnp.int32)
    bucket = jnp.where(distance < 8, distance, distant)
    bucket = bucket + 16 * (relative > 0).astype(jnp.int32)
    labels = lax.broadcasted_iota(jnp.int32, relative.shape, 0)
    return bucket == labels


def normed(values, gain_row):
    inverse = lax.rsqrt(jnp.mean(values * values, axis=-1, keepdims=True) + EPSILON)
    return values * inverse * gain_row


def window(block):
    return max(0, block - 2), min(3, block + 2)


def head_lanes(rows, which):
    lane = lax.broadcasted_iota(jnp.int32, (rows, 128), 1)
    return lane < HEAD_DIM if which == 0 else lane >= HEAD_DIM


def keep(values, which):
    return jnp.where(head_lanes(values.shape[0], which), values, jnp.zeros_like(values))


def softmax_rows(scores):
    largest = jnp.max(scores, axis=-1, keepdims=True)
    powers = jnp.exp(scores - largest)
    return (powers * (1.0 / jnp.sum(powers, axis=-1, keepdims=True))).astype(BF)


FORWARD_SAVED = (
    ((768, 3 * D), BF),
    ((768, D + PROJ), BF),
    ((768, 2 * FF), BF),
    ((FF, D), BF),
    ((768, D), BF),
    ((768, 3 * D), BF),
    ((768, D), BF),
    ((768, D), F32),
    ((768, D), BF),
    ((768, 2 * FF), BF),
    ((768, FF), BF),
    ((768, D), F32),
    ((768, D), BF),
    ((6, 512, 1024), BF),
    ((256, 1536), BF),
)


def forward_kernel(*refs):
    (doc, qry, doc_lengths, qry_lengths, small) = refs[0:5]
    flats = refs[5:13]
    doc_out, qry_out, gains_out = refs[13:16]
    saved = refs[16:31]
    rest = refs[31:]
    whole, parts, shards = rest[0:4], rest[4:7], rest[7:11]
    (wide, small_in, gains, diagonals, bias, id_column, id_row) = rest[11:18]
    (norm_one, qkv, context, hidden, norm_two, factors, inner, norm_three) = rest[18:26]
    (prob_doc, prob_qry, scores) = rest[26:29]
    gather_sems = rest[29:33]
    small_send, small_recv, save_sem, whole_sem = rest[33:37]

    place = Place()
    place.barrier()
    gains[...] = jnp.zeros_like(gains)
    gather = Gather(place, shards, whole, parts, gather_sems)

    def small_copy(k):
        return remote(
            small, small_in.at[k], small_send.at[k], small_recv.at[k], place.to_z[k]
        )

    for k in range(3):
        small_copy(k).start()
    for index in range(3):
        unflatten(flats[index], wide, shards[0].at[:, D * index : D * index + D], lambda j: 128 * j)
        gather.begin(index)
    unflatten(flats[3], wide, shards[1].at[:, 0:D], lambda j: 128 * j)
    shards[1][:, D:] = flats[7][...]
    gather.begin(3)
    unflatten(flats[4], wide, shards[2], lambda j: 1536 * (j // 6) + 128 * (j % 6))
    unflatten(flats[5], wide, shards[2], lambda j: 1536 * (j // 6) + 128 * (j % 6) + D)
    for index in range(4, 8):
        gather.begin(index)
    unflatten(flats[6], wide, shards[3], lambda j: 128 * j)
    for index in range(8, 10):
        gather.begin(index)

    saves = []

    def save(index, source, target=None):
        copy = pltpu.make_async_copy(
            source, saved[index] if target is None else target, save_sem.at[index]
        )
        copy.start()
        saves.append((index, copy))
        return copy

    def save_whole(s):
        array, first, width = GATHER_STAGES[s]
        columns = pl.ds(first, width)
        copy = pltpu.make_async_copy(
            whole[array].at[:, columns], saved[array].at[:, columns], whole_sem.at[s]
        )
        copy.start()
        saves.append((-1, copy))

    def small_arrive():
        for k in range(3):
            small_copy(k).wait_recv()
        pieces = []
        for other in range(4):
            piece = small[...]
            for k in range(3):
                here = lax.rem(place.z + 3 - k, 4) == other
                piece = jnp.where(here, small_in[k], piece)
            pieces.append(piece)
        low = lax.broadcasted_iota(jnp.int32, (1, 128), 1) < 64
        for row in range(3):
            for tile in range(6):
                unit = 12 * row + 2 * tile
                left = pieces[unit // 9][unit % 9 : unit % 9 + 1, :]
                unit = unit + 1
                right = pieces[unit // 9][unit % 9 : unit % 9 + 1, :]
                gains[row : row + 1, 128 * tile : 128 * tile + 128] = jnp.where(low, left, right)
        gains_out[...] = gains[...]
        table = jnp.concatenate([piece[16:24, :] for piece in pieces], axis=0).astype(BF)
        relative = lax.broadcasted_iota(jnp.int32, (BUCKETS, 512), 1) - 256
        diagonals[...] = dot(table, marks_of(relative).astype(BF), 0, 0)[0:16]

    def make_bias(head):
        rows = jnp.broadcast_to(diagonals[pl.ds(head, 1), :], (8, 512))
        lines = lax.broadcasted_iota(jnp.int32, (8, 512), 0)
        for bit in range(3):
            moved = pltpu.roll(rows, 2**bit, 1)
            rows = jnp.where(lax.rem(lines // 2**bit, 2) == 1, moved, rows)
        for group in range(ROW_BLOCK // 8):
            moved = pltpu.roll(rows, 8 * group, 1) if group else rows
            bias[head, 8 * group : 8 * group + 8, :] = moved[:, 128:512]

    def make_ids():
        position = lax.broadcasted_iota(jnp.int32, (512, 128), 0)
        across = lax.broadcasted_iota(jnp.int32, (8, 512), 1)
        down_id, across_id = jnp.zeros_like(position), jnp.zeros_like(across)
        edge = 0
        for index in range(4):
            edge = edge + doc_lengths[0, index]
            down_id = down_id + (position >= edge).astype(jnp.int32)
            across_id = across_id + (across >= edge).astype(jnp.int32)
        id_column[0:512] = down_id
        id_row[:, 0:512] = across_id
        position = lax.broadcasted_iota(jnp.int32, (32, 128), 0)
        across = lax.broadcasted_iota(jnp.int32, (8, 256), 1)
        across_id = jnp.zeros_like(across)
        for index in range(8):
            length = qry_lengths[0, index]
            id_column[512 + 32 * index : 544 + 32 * index] = 2 * index + (
                position >= length
            ).astype(jnp.int32)
            mine = (across >= 32 * index) & (across < 32 * index + 32)
            value = 2 * index + (across >= length + 32 * index).astype(jnp.int32)
            across_id = jnp.where(mine, value, across_id)
        id_row[:, 512:768] = across_id

    def first_norm():
        gain = gains[0:1, :]

        def documents(index):
            rows = aligned(128 * index, 128, 128)
            norm_one[rows] = normed(doc[rows].astype(F32), gain).astype(BF)

        def queries(index):
            rows = aligned(128 * index, 128, 128)
            norm_one[aligned(512 + 128 * index, 128, 128)] = normed(
                qry[rows].astype(F32), gain
            ).astype(BF)

        loop(4, documents)
        loop(2, queries)
        save(4, norm_one)

    def project(index):
        columns = pl.ds(D * index, D)
        qkv[:, columns] = dot(norm_one[...], whole[0][:, columns]).astype(BF)

    def attend_pair(pair):
        query = qkv[0:512, aligned(128 * pair, 128, 128)]
        key = qkv[0:512, aligned(D + 128 * pair, 128, 128)]
        value = qkv[0:512, aligned(2 * D + 128 * pair, 128, 128)]
        for which in range(2):
            head = 2 * pair + which
            scores[...] = dot(keep(query, which), key, 1, 1)
            far_left = jnp.broadcast_to(bias[head, 127:128, 0:1], (128, 128))
            far_right = jnp.broadcast_to(bias[head, 0:1, NEAR - 1 : NEAR], (128, 128))
            for block in range(4):
                low, high = window(block)
                near_low, near_high = max(low, block - 1), min(high, block + 1)
                pieces = [far_left] * (near_low - low)
                pieces.append(
                    bias[
                        head,
                        :,
                        128 * (near_low - block + 1) : 128 * (near_high - block + 2),
                    ]
                )
                pieces += [far_right] * (high - near_high)
                rows = slice(128 * block, 128 * block + 128)
                columns = slice(128 * low, 128 * high + 128)
                allowed = id_column[rows, 0:1] == id_row[0:1, columns]
                values = scores[rows, columns] + jnp.concatenate(pieces, axis=1)
                share = softmax_rows(jnp.where(allowed, values, NEGATIVE))
                prob_doc[
                    pair, rows, 512 * which + 128 * low : 512 * which + 128 * high + 128
                ] = share
        both = jnp.concatenate([keep(value, 0), keep(value, 1)], axis=0)
        context[0:512, aligned(128 * pair, 128, 128)] = dot(prob_doc[pair], both).astype(BF)
        for block in range(2):
            rows = slice(512 + 128 * block, 640 + 128 * block)
            query = qkv[rows, aligned(128 * pair, 128, 128)]
            key = qkv[rows, aligned(D + 128 * pair, 128, 128)]
            value = qkv[rows, aligned(2 * D + 128 * pair, 128, 128)]
            allowed = id_column[rows, 0:1] == id_row[0:1, rows]
            shares = []
            for which in range(2):
                values = dot(keep(query, which), key, 1, 1)
                values = values + bias[2 * pair + which, :, 128:256]
                shares.append(softmax_rows(jnp.where(allowed, values, NEGATIVE)))
            shares = jnp.concatenate(shares, axis=1)
            prob_qry[128 * block : 128 * block + 128, aligned(256 * pair, 128, 256)] = shares
            both = jnp.concatenate([keep(value, 0), keep(value, 1)], axis=0)
            context[rows, aligned(128 * pair, 128, 128)] = dot(shares, both).astype(BF)

    def attend(first, last):
        lax.fori_loop(first, last, lambda pair, carry: (attend_pair(pair), carry)[1], 0)

    def after_attention():
        save(5, qkv)
        save(6, context)
        save(13, prob_doc)
        save(14, prob_qry)

        def one(tokens, offset):
            def block(index):
                source = aligned(128 * index, 128, 128)
                rows = aligned(offset + 128 * index, 128, 128)
                total = tokens[source].astype(F32) + dot(context[rows], whole[1][:, 0:D])
                hidden[rows] = total
                norm_two[rows] = normed(total, gains[1:2, :]).astype(BF)

            return block

        loop(4, one(doc, 0))
        loop(2, one(qry, 512))
        copy = save(7, hidden)
        save(8, norm_two)
        return copy

    def gated(chunk):
        def block(index):
            rows = aligned(256 * index, 256, 256)
            left = norm_two[rows]
            gate = dot(left, whole[2][:, 1536 * chunk : 1536 * chunk + D])
            upper = dot(left, whole[2][:, 1536 * chunk + D : 1536 * chunk + 2 * D])
            square = gate * gate
            bend = jnp.tanh(SCALE * gate * (1.0 + 0.044715 * square))
            half = 0.5 * (1.0 + bend)
            active = gate * half
            slope = half + 0.5 * gate * (1.0 - bend * bend) * (
                SCALE + (3.0 * 0.044715 * SCALE) * square
            )
            inner[rows, D * chunk : D * chunk + D] = (active * upper).astype(BF)
            factors[rows, 1536 * chunk : 1536 * chunk + D] = (upper * slope).astype(BF)
            factors[rows, 1536 * chunk + D : 1536 * chunk + 2 * D] = active.astype(BF)

        loop(3, block)

    def descend(half):
        columns = slice(384 * half, 384 * half + 384)

        def block(index):
            rows = aligned(256 * index, 256, 256)
            hidden[rows, columns] = hidden[rows, columns] + dot(inner[rows], whole[3][:, columns])

        loop(3, block)

    def last():
        def block(index):
            rows = aligned(128 * index, 128, 128)
            norm_three[rows] = normed(hidden[rows], gains[2:3, :]).astype(BF)

        loop(6, block)
        result = dot(norm_three[...], whole[1][:, D:]).astype(BF)
        doc_out[...] = result[0:512]
        qry_out[...] = result[512:768]
        save(11, hidden)
        save(12, norm_three)

    def clear(pair):
        nothing = jnp.zeros((128, 128), BF)
        for which in range(2):
            prob_doc[pair, 0:128, 512 * which + 384 : 512 * which + 512] = nothing
            prob_doc[pair, 384:512, 512 * which : 512 * which + 128] = nothing

    count = len(GATHER_STAGES)
    hidden_copy = None
    for t in range(count + 3):
        gather.step(t)
        if t >= 3:
            save_whole(t - 3)
        if t == 0:
            small_arrive()
            loop(12, make_bias)
            make_ids()
            loop(6, clear)
        if t == 1:
            first_norm()
        if 3 <= t < 6:
            project(t - 3)
        if t == 5:
            attend(0, 1)
        if t == 6:
            attend(1, 4)
        if t == 7:
            attend(4, 6)
            hidden_copy = after_attention()
        if 8 <= t < 12:
            gated(t - 8)
        if t == 11:
            save(9, factors)
            save(10, inner)
            hidden_copy.wait()
            descend(0)
        if t == 12:
            descend(1)
    last()
    gather.finish()
    for k in range(3):
        small_copy(k).wait_send()
    for index, copy in saves:
        if index != 7:
            copy.wait()


def forward(doc, qry, doc_lengths, qry_lengths, small, flats):
    vmem = pl.BlockSpec(memory_space=pltpu.VMEM)
    smem = pl.BlockSpec(memory_space=pltpu.SMEM)
    hbm = pl.BlockSpec(memory_space=pl.ANY)
    dma = pltpu.SemaphoreType.DMA
    whole_rows = [32 * count for count in SHARE_ROWS]
    scratch = [pltpu.VMEM((r, w), BF) for r, w in zip(whole_rows, WIDTHS)]
    scratch += [pltpu.VMEM((3, r, w), BF) for r, w in zip(SHARE_ROWS[:3], WIDTHS[:3])]
    scratch += [pltpu.VMEM((r, w), BF) for r, w in zip(SHARE_ROWS, WIDTHS)]
    scratch += [
        pltpu.VMEM((576, 128), F32),
        pltpu.VMEM((3, 24, 128), F32),
        pltpu.VMEM((8, D), F32),
        pltpu.VMEM((16, 512), F32),
        pltpu.VMEM((HEADS, 128, NEAR), F32),
        pltpu.VMEM((768, 128), jnp.int32),
        pltpu.VMEM((8, 768), jnp.int32),
        pltpu.VMEM((768, D), BF),
        pltpu.VMEM((768, 3 * D), BF),
        pltpu.VMEM((768, D), BF),
        pltpu.VMEM((768, D), F32),
        pltpu.VMEM((768, D), BF),
        pltpu.VMEM((768, 2 * FF), BF),
        pltpu.VMEM((768, FF), BF),
        pltpu.VMEM((768, D), BF),
        pltpu.VMEM((6, 512, 1024), BF),
        pltpu.VMEM((256, 1536), BF),
        pltpu.VMEM((512, 512), F32),
    ]
    scratch += Gather.scratch()
    scratch += [dma((3,)), dma((3,)), dma((15,)), dma((len(GATHER_STAGES),))]
    return pl.pallas_call(
        forward_kernel,
        out_shape=(
            jax.ShapeDtypeStruct((512, PROJ), BF),
            jax.ShapeDtypeStruct((256, PROJ), BF),
            jax.ShapeDtypeStruct((8, D), F32),
        )
        + tuple(jax.ShapeDtypeStruct(shape, kind) for shape, kind in FORWARD_SAVED),
        in_specs=[vmem, vmem, smem, smem, vmem] + [vmem] * 8,
        out_specs=(vmem, vmem, vmem) + (hbm,) * len(FORWARD_SAVED),
        scratch_shapes=scratch,
        compiler_params=pltpu.CompilerParams(
            collective_id=0, has_side_effects=True, vmem_limit_bytes=VMEM_LIMIT
        ),
        name="forward",
    )(doc, qry, doc_lengths, qry_lengths, small, *flats)


VMEM_LIMIT = 63 * 2**20


def norm_back(values, gain_row, incoming):
    inverse = lax.rsqrt(jnp.mean(values * values, axis=-1, keepdims=True) + EPSILON)
    scaled = gain_row * incoming
    inner = jnp.mean(scaled * values, axis=-1, keepdims=True)
    result = inverse * scaled - values * (inverse * inverse * inverse * inner)
    terms = incoming * values * inverse
    return result, jnp.sum(terms.reshape(-1, 8, D), axis=0)


def diagonal_sums(near):
    wide = jnp.concatenate([near, jnp.zeros((128, 128), F32)], axis=1)
    rows = wide[0:8]
    for group in range(1, 16):
        rows = rows + pltpu.roll(wide[8 * group : 8 * group + 8], 512 - 8 * group, 1)
    lines = lax.broadcasted_iota(jnp.int32, (8, 512), 0)
    for bit in range(3):
        moved = pltpu.roll(rows, 512 - 2**bit, 1)
        rows = jnp.where(lax.rem(lines // 2**bit, 2) == 1, moved, rows)
    return jnp.sum(rows, axis=0, keepdims=True)


def backward_kernel(*refs):
    doc, qry, doc_cotangent, qry_cotangent, gains = refs[0:5]
    saved = refs[5:20]
    doc_grad, qry_grad = refs[20:22]
    flats = refs[22:30]
    small_out = refs[30]
    rest = refs[31:]
    (out_mat, down, gate_up, factors, mixed, residual, hidden, incoming) = rest[0:8]
    (norm_two, norm_three, narrow, context, cotangent) = rest[8:13]
    (gain_terms, diagonal_rows, scores, small, small_in) = rest[13:18]
    scatter_buffers = rest[18:44]
    scatter_sems = rest[44:47]
    small_send, small_recv, load_sem = rest[47:50]

    place = Place()
    loads = {}

    def load(name, source, target):
        copy = pltpu.make_async_copy(source, target, load_sem.at[len(loads)])
        copy.start()
        loads[name] = copy

    def ready(*names):
        for name in names:
            loads[name].wait()

    load("residual", saved[11], residual)
    load("out_mat", saved[1], out_mat)
    load("inner", saved[10], mixed)
    load("down", saved[3], down)

    def load_chunk(chunk):
        columns = pl.ds(1536 * chunk, 1536)
        load(("factors", chunk), saved[9].at[:, columns], factors.at[chunk % 2])
        load(("gate_up", chunk), saved[2].at[:, columns], gate_up.at[chunk % 2])

    load_chunk(0)
    load("norm_two", saved[8], norm_two)
    load_chunk(1)
    load("hidden", saved[7], hidden)
    load("context", saved[6], context)
    load("norm_three", saved[12], norm_three)

    place.barrier()

    def settled(s, total):
        array, first, width = SCATTER_STAGES[s]
        if array == 3:
            for tile in range(3):
                line = 3 * (first // 1536) + tile
                flats[6][pl.ds(line, 96, 6), :] = total[:, 128 * tile : 128 * tile + 128]
        elif array == 2:
            for tile in range(12):
                line = 6 * (first // 1536) + tile % 6
                flats[4 + tile // 6][pl.ds(line, 24, 24), :] = total[
                    :, 128 * tile : 128 * tile + 128
                ]
        else:
            for tile in range(6):
                flats[3 if array == 1 else first // D][pl.ds(tile, 24, 6), :] = total[
                    :, 128 * tile : 128 * tile + 128
                ]
            if array == 1:
                flats[7][...] = total[:, D:]

    scatter = Scatter(place, scatter_buffers, settled, scatter_sems)
    gain_terms[...] = jnp.zeros_like(gain_terms)
    diagonal_rows[...] = jnp.zeros_like(diagonal_rows)
    cotangent[0:512] = doc_cotangent[...]
    cotangent[512:768] = qry_cotangent[...]

    def final_norm(index):
        rows = aligned(128 * index, 128, 128)
        grad, terms = norm_back(
            residual[rows], gains[2:3, :], dot(cotangent[rows], out_mat[:, D:], 1, 1)
        )
        residual[rows] = grad
        narrow[rows] = grad.astype(BF)
        gain_terms[2] = gain_terms[2] + terms

    ready("residual", "out_mat")
    loop(6, final_norm)

    ready("inner")
    for half in range(2):
        scatter.free(half)
        local = scatter.local(half)

        def piece(index):
            total = dot(
                mixed[:, aligned(D * index, 128, D)],
                narrow[:, 384 * half : 384 * half + 384],
                0,
                0,
            ).astype(BF)
            for core in range(2):
                for other in range(4):
                    first = 384 * core + 96 * other
                    local[index, core, :, 384 * other : 384 * other + 384] = total[
                        first : first + 96
                    ]

        loop(4, piece)
        scatter.step(half, half)
    load("qkv", saved[5], mixed.at[:, pl.ds(0, 3 * D)])
    load("norm_one", saved[4], mixed.at[:, pl.ds(3 * D, D)])

    def put(local, total, first):
        total = total.astype(BF)
        width = total.shape[1]
        for block in range(8):
            local[block // 2, block % 2, :, first : first + width] = total[
                96 * block : 96 * block + 96
            ]

    ready("down", "norm_two")
    for chunk in range(4):
        slot = chunk % 2
        ready(("factors", chunk), ("gate_up", chunk))

        def gated_back(index):
            rows = aligned(256 * index, 256, 256)
            grad = dot(narrow[rows], down[D * chunk : D * chunk + D], 1, 1)
            for side in (0, D):
                factors[slot, rows, side : side + D] = (
                    grad * factors[slot, rows, side : side + D].astype(F32)
                ).astype(BF)

        loop(3, gated_back)
        stage = 2 + chunk
        scatter.free(stage)
        for side in (0, D):
            put(
                scatter.local(stage),
                dot(norm_two[...], factors[slot, :, side : side + D], 0, 0),
                side,
            )
        scatter.step(stage, stage)

        def collect(index):
            rows = aligned(256 * index, 256, 256)
            part = dot(factors[slot, rows], gate_up[slot], 1, 1)
            incoming[rows] = part if chunk == 0 else incoming[rows] + part

        loop(3, collect)
        if chunk < 2:
            load_chunk(chunk + 2)
        if chunk == 2:
            load(("share", 0), saved[13].at[0], factors.at[0, pl.ds(0, 512), pl.ds(0, 1024)])
            load("share_qry", saved[14], gate_up.at[0, pl.ds(0, 256)])
    load(("share", 1), saved[13].at[1], factors.at[1, pl.ds(0, 512), pl.ds(0, 1024)])
    for index in range(3):
        load(
            ("qkv_mat", index),
            saved[0].at[:, pl.ds(D * index, D)],
            down.at[pl.ds(D * index, D)],
        )
    load("doc", doc, down.at[pl.ds(3 * D, 512)])
    load("qry", qry, down.at[pl.ds(3 * D + 512, 256)])

    def middle_norm(index):
        rows = aligned(128 * index, 128, 128)
        grad, terms = norm_back(hidden[rows], gains[1:2, :], incoming[rows])
        grad = grad + residual[rows]
        residual[rows] = grad
        narrow[rows] = grad.astype(BF)
        gain_terms[1] = gain_terms[1] + terms

    ready("hidden")
    loop(6, middle_norm)
    ready("context", "norm_three")
    scatter.free(6)
    put(scatter.local(6), dot(context[...], narrow[...], 0, 0), 0)
    put(scatter.local(6), dot(norm_three[...], cotangent[...], 0, 0), D)
    scatter.step(6, 6)
    grad_context = norm_three
    grad_context[...] = dot(narrow[...], out_mat[:, 0:D], 1, 1).astype(BF)

    nothing = jnp.zeros((128, 128), BF)
    grad_scores = gate_up.at[1]
    for which in range(2):
        grad_scores[0:128, 512 * which + 384 : 512 * which + 512] = nothing
        grad_scores[384:512, 512 * which : 512 * which + 128] = nothing

    def two(values):
        return jnp.concatenate([keep(values, 0), keep(values, 1)], axis=0)

    def attention_back(pair, share):
        columns = [aligned(D * index + 128 * pair, 128, 128) for index in range(3)]
        rows = slice(0, 512)
        query, key, value = (mixed[rows, column] for column in columns)
        grad = grad_context[rows, columns[0]]
        near_sums, far_sums = [], []
        for which in range(2):
            scores[...] = dot(keep(grad, which), value, 1, 1)
            near = [None, None, None]
            far = [None, None]
            for block in range(4):
                low, high = window(block)
                rows_here = slice(128 * block, 128 * block + 128)
                reach = slice(512 * which + 128 * low, 512 * which + 128 * high + 128)
                part = share[rows_here, reach].astype(F32)
                grad_share = scores[rows_here, 128 * low : 128 * high + 128]
                weighted = jnp.sum(part * grad_share, axis=-1, keepdims=True)
                result = (part * (grad_share - weighted)).astype(BF)
                grad_scores[rows_here, reach] = result
                result = result.astype(F32)
                for other in range(low, high + 1):
                    tile = result[:, 128 * (other - low) : 128 * (other - low) + 128]
                    place_at = other - block
                    if abs(place_at) == 2:
                        side = 0 if place_at < 0 else 1
                        far[side] = tile if far[side] is None else far[side] + tile
                    else:
                        side = place_at + 1
                        near[side] = tile if near[side] is None else near[side] + tile
            near_sums.append(near)
            far_sums.append(far)
        grad_query = dot(grad_scores[0:512, 0:1024], two(key))
        grad_key = dot(grad_scores[0:512, 0:512], keep(query, 0), 0, 0) + dot(
            grad_scores[0:512, 512:1024], keep(query, 1), 0, 0
        )
        grad_value = dot(share[0:512, 0:512], keep(grad, 0), 0, 0) + dot(
            share[0:512, 512:1024], keep(grad, 1), 0, 0
        )
        mixed[rows, columns[0]] = grad_query.astype(BF)
        mixed[rows, columns[1]] = grad_key.astype(BF)
        mixed[rows, columns[2]] = grad_value.astype(BF)
        for block in range(2):
            rows = slice(512 + 128 * block, 640 + 128 * block)
            query, key, value = (mixed[rows, column] for column in columns)
            grad = grad_context[rows, columns[0]]
            small_share = gate_up[
                0, 128 * block : 128 * block + 128, aligned(256 * pair, 128, 256)
            ]
            results = []
            grad_key = jnp.zeros((128, 128), F32)
            grad_value = jnp.zeros((128, 128), F32)
            for which in range(2):
                part = small_share[:, 128 * which : 128 * which + 128]
                grad_share = dot(keep(grad, which), value, 1, 1)
                wide = part.astype(F32)
                weighted = jnp.sum(wide * grad_share, axis=-1, keepdims=True)
                result = (wide * (grad_share - weighted)).astype(BF)
                near_sums[which][1] = near_sums[which][1] + result.astype(F32)
                results.append(result)
                grad_key = grad_key + dot(result, keep(query, which), 0, 0)
                grad_value = grad_value + dot(part, keep(grad, which), 0, 0)
            grad_query = dot(jnp.concatenate(results, axis=1), two(key))
            mixed[rows, columns[0]] = grad_query.astype(BF)
            mixed[rows, columns[1]] = grad_key.astype(BF)
            mixed[rows, columns[2]] = grad_value.astype(BF)
        lane = lax.broadcasted_iota(jnp.int32, (1, 512), 1)
        for which in range(2):
            row = diagonal_sums(jnp.concatenate(near_sums[which], axis=1))
            for side, column in ((0, 28), (1, 228)):
                total = jnp.sum(far_sums[which][side], axis=(0, 1), keepdims=True)
                row = row + jnp.where(lane == column, total, 0.0)
            diagonal_rows[pl.ds(2 * pair + which, 1), :] = row

    ready("qkv", "norm_one", "share_qry")
    turn = 7
    for pair in range(6):
        slot = pair % 2
        ready(("share", pair))
        attention_back(pair, factors.at[slot])
        if pair < 4:
            load(
                ("share", pair + 2),
                saved[13].at[pair + 2],
                factors.at[slot, pl.ds(0, 512), pl.ds(0, 1024)],
            )
        if pair in (1, 3):
            scatter.step(turn)
            turn = turn + 1

    for index in range(3):
        stage = 7 + index
        scatter.free(stage)
        put(
            scatter.local(stage),
            dot(mixed[:, 3 * D :], mixed[:, D * index : D * index + D], 0, 0),
            0,
        )
        scatter.step(turn, stage)
        turn = turn + 1

    ready(("qkv_mat", 0), ("qkv_mat", 1), ("qkv_mat", 2), "doc", "qry")

    def first_norm(index):
        rows = aligned(128 * index, 128, 128)
        part = dot(mixed[rows, 0:D], down[0:D], 1, 1)
        part = part + dot(mixed[rows, D : 2 * D], down[D : 2 * D], 1, 1)
        part = part + dot(mixed[rows, 2 * D : 3 * D], down[2 * D : 3 * D], 1, 1)
        here = aligned(3 * D + 128 * index, 128, 128)
        grad, terms = norm_back(down[here].astype(F32), gains[0:1, :], part)
        down[here] = (residual[rows] + grad).astype(BF)
        gain_terms[0] = gain_terms[0] + terms

    lax.fori_loop(0, 3, lambda index, carry: (first_norm(index), carry)[1], 0)
    scatter.step(turn)
    turn = turn + 1
    lax.fori_loop(3, 6, lambda index, carry: (first_norm(index), carry)[1], 0)
    stores = [
        pltpu.make_async_copy(down.at[pl.ds(3 * D, 512)], doc_grad, load_sem.at[len(loads)]),
        pltpu.make_async_copy(
            down.at[pl.ds(3 * D + 512, 256)], qry_grad, load_sem.at[len(loads) + 1]
        ),
    ]
    for copy in stores:
        copy.start()

    small[0] = jnp.zeros((40, 128), F32)
    for row in range(3):
        total = jnp.sum(gain_terms[row], axis=0, keepdims=True)
        for tile in range(6):
            line = 6 * row + tile
            small[0, line : line + 1, :] = total[:, 128 * tile : 128 * tile + 128]
    column = lax.broadcasted_iota(jnp.int32, (BUCKETS, 512), 1)
    relative = jnp.where(column < 384, column - 128, column - 640)
    marks = marks_of(relative).astype(F32)
    small[0, 24:40, 0:BUCKETS] = lax.dot_general(
        diagonal_rows[...],
        marks,
        (((1,), (1,)), ((), ())),
        precision=lax.Precision.HIGHEST,
        preferred_element_type=F32,
    )

    def small_copy(index):
        device = ([place.to_sib, place.to_x, place.to_y] + place.to_z)[index]
        return remote(
            small.at[min(index, 3)],
            small_in.at[index],
            small_send.at[index],
            small_recv.at[index],
            device,
        )

    small_copy(0).start()
    for index in range(3):
        scatter.step(turn)
        turn = turn + 1
        small_copy(index).wait_recv()
        small[index + 1] = small[index] + small_in[index]
        if index < 2:
            small_copy(index + 1).start()
    for k in range(3):
        small_copy(3 + k).start()
    scatter.step(turn)
    for k in range(3):
        small_copy(3 + k).wait_recv()
    total = jnp.zeros((40, 128), F32)
    for other in range(4):
        piece = small[3]
        for k in range(3):
            here = lax.rem(place.z + 3 - k, 4) == other
            piece = jnp.where(here, small_in[3 + k], piece)
        total = total + piece
    small_out[...] = total

    scatter.finish()
    for index in range(6):
        small_copy(index).wait_send()
    for copy in stores:
        copy.wait()


def backward(doc, qry, doc_cotangent, qry_cotangent, gains, saved):
    vmem = pl.BlockSpec(memory_space=pltpu.VMEM)
    hbm = pl.BlockSpec(memory_space=pl.ANY)
    dma = pltpu.SemaphoreType.DMA
    scratch = [
        pltpu.VMEM((768, D + PROJ), BF),
        pltpu.VMEM((FF, D), BF),
        pltpu.VMEM((2, 768, 1536), BF),
        pltpu.VMEM((2, 768, 1536), BF),
        pltpu.VMEM((768, FF), BF),
        pltpu.VMEM((768, D), F32),
        pltpu.VMEM((768, D), F32),
        pltpu.VMEM((768, D), F32),
        pltpu.VMEM((768, D), BF),
        pltpu.VMEM((768, D), BF),
        pltpu.VMEM((768, D), BF),
        pltpu.VMEM((768, D), BF),
        pltpu.VMEM((768, PROJ), BF),
        pltpu.VMEM((3, 8, D), F32),
        pltpu.VMEM((16, 512), F32),
        pltpu.VMEM((512, 512), F32),
        pltpu.VMEM((4, 40, 128), F32),
        pltpu.VMEM((6, 40, 128), F32),
    ]
    scratch += Scatter.scratch() + Scatter.semaphores() + [dma((6,)), dma((6,)), dma((36,))]
    lines = (144, 144, 144, 144, 576, 576, 576, 24)
    return pl.pallas_call(
        backward_kernel,
        out_shape=(
            jax.ShapeDtypeStruct((512, D), BF),
            jax.ShapeDtypeStruct((256, D), BF),
        )
        + tuple(jax.ShapeDtypeStruct((count, 128), F32) for count in lines)
        + (jax.ShapeDtypeStruct((40, 128), F32),),
        in_specs=[hbm, hbm, vmem, vmem, vmem] + [hbm] * len(saved),
        out_specs=(hbm, hbm) + (vmem,) * 9,
        scratch_shapes=scratch,
        compiler_params=pltpu.CompilerParams(
            collective_id=1, has_side_effects=True, vmem_limit_bytes=VMEM_LIMIT
        ),
        name="backward",
    )(doc, qry, doc_cotangent, qry_cotangent, gains, *saved)


def local_fast(
    document_tokens,
    document_lengths,
    query_tokens,
    query_lengths,
    weight_query,
    weight_key,
    weight_value,
    weight_out,
    weight_gate,
    weight_up,
    weight_down,
    weight_proj,
    norm_gains,
    rel_table,
    document_cotangent,
    query_cotangent,
):
    doc = document_tokens.reshape(DOC_LEN, D)
    qry = query_tokens.reshape(-1, D)
    units = norm_gains.astype(jnp.float32).reshape(9, 64)
    units = jnp.pad(jnp.concatenate([units, units], axis=1), ((0, 7), (0, 0)))
    table = jnp.pad(rel_table.astype(jnp.float32).reshape(8, HEADS), ((0, 0), (0, 128 - HEADS)))
    small = jnp.concatenate([units, table], axis=0)
    flats = [
        w.reshape(-1, 128)
        for w in (
            weight_query,
            weight_key,
            weight_value,
            weight_out,
            weight_gate,
            weight_up,
            weight_down,
            weight_proj,
        )
    ]
    results = forward(doc, qry, document_lengths, query_lengths.reshape(1, 8), small, flats)
    doc_out, qry_out, gains = results[0:3]
    grads = backward(
        doc,
        qry,
        document_cotangent.reshape(DOC_LEN, PROJ),
        query_cotangent.reshape(-1, PROJ),
        gains,
        results[3:],
    )
    fsdp_index = lax.axis_index("fsdp")
    small = grads[10]
    own_gains = lax.dynamic_slice_in_dim(small[0:18].reshape(-1), fsdp_index * 576, 576)
    own_table = lax.dynamic_slice_in_dim(small[24 : 24 + HEADS], fsdp_index * 8, 8, 1)
    return (
        doc_out.reshape(document_cotangent.shape),
        qry_out.reshape(query_cotangent.shape),
        grads[0].reshape(document_tokens.shape),
        grads[1].reshape(query_tokens.shape),
        *[grad.reshape(-1) for grad in grads[2:10]],
        own_gains,
        jnp.transpose(own_table).reshape(-1),
    )


def solution(mesh):
    placed = (
        P(("dp", "fsdp"), None, None),
        P(("dp", "fsdp"), None),
        P(("dp", "fsdp"), None, None),
        P(("dp", "fsdp")),
        P(("dp", "fsdp")),
        P(("dp", "fsdp")),
        P(("dp", "fsdp")),
        P(("dp", "fsdp")),
        P(("dp", "fsdp")),
        P(("dp", "fsdp")),
        P(("dp", "fsdp")),
        P(("dp", "fsdp")),
        P("fsdp"),
        P("fsdp"),
        P(("dp", "fsdp"), None, None),
        P(("dp", "fsdp"), None, None),
    )
    return jax.shard_map(
        local_fast if (mesh.shape["dp"], mesh.shape["fsdp"]) == (8, 4) else local,
        mesh=mesh,
        in_specs=placed,
        out_specs=(
            P(("dp", "fsdp"), None, None),
            P(("dp", "fsdp"), None, None),
            P(("dp", "fsdp"), None, None),
            P(("dp", "fsdp"), None, None),
            P(("dp", "fsdp")),
            P(("dp", "fsdp")),
            P(("dp", "fsdp")),
            P(("dp", "fsdp")),
            P(("dp", "fsdp")),
            P(("dp", "fsdp")),
            P(("dp", "fsdp")),
            P(("dp", "fsdp")),
            P("fsdp"),
            P("fsdp"),
        ),
        check_vma=False,
    )
```

```python
import jax
import jax.numpy as jnp
from jax import lax
from jax.experimental import pallas as pl
from jax.experimental.pallas import tpu as pltpu
from jax.sharding import PartitionSpec as P

D = 768
HEADS = 12
HEAD_DIM = 64
FF = 3072
BUCKETS = 32
PROJ = 128
DOC_LEN = 512
QRY_LEN = 32


EPSILON = 1e-06
NEGATIVE = -1e30


def rms_norm(values, gain_row):
    inverse = lax.rsqrt(jnp.mean(values * values, axis=-1, keepdims=True) + EPSILON)
    return values * inverse * gain_row


def gated_unit(gate_in, upper_in):
    return jax.nn.gelu(gate_in, approximate=True) * upper_in


def bucket_ids(length):
    positions = jnp.arange(length, dtype=jnp.int32)
    relative = positions[None, :] - positions[:, None]
    distance = jnp.abs(relative)
    distant = 8 + sum(
        ((distance * distance >= 64 * 2**power).astype(jnp.int32) for power in range(1, 8))
    )
    nearby = jnp.where(distance < 8, distance, distant)
    return nearby + 16 * (relative > 0).astype(jnp.int32)


def bucket_onehot(length):
    flat_ids = bucket_ids(length).reshape(1, length * length)
    labels = jnp.arange(BUCKETS, dtype=jnp.int32).reshape(BUCKETS, 1)
    return (flat_ids == labels).astype(jnp.bfloat16)


def segment_ids(lengths, length):
    boundary = jnp.cumsum(lengths, axis=-1)
    positions = jnp.arange(length, dtype=jnp.int32)
    return jnp.sum((positions[None, :, None] >= boundary[:, None, :]).astype(jnp.int32), axis=-1)


def outer_sum(left_rows, right_rows):
    return lax.dot_general(
        left_rows, right_rows, (((0,), (0,)), ((), ())), preferred_element_type=jnp.float32
    )


def times_transposed(left_rows, matrix):
    return lax.dot_general(
        left_rows, matrix, (((1,), (1,)), ((), ())), preferred_element_type=jnp.float32
    )


def flat_piece(left_rows, right_rows, start, count):
    width = right_rows.shape[1]
    needed = count // width + 2
    padded = jnp.pad(left_rows, ((0, 0), (0, needed)))
    first_row = start // width
    columns = lax.dynamic_slice_in_dim(padded, first_row, needed, 1)
    block = outer_sum(columns, right_rows).reshape(-1)
    return lax.dynamic_slice_in_dim(block, start, count)


def grad_terms(pairs, devices):
    shares = [pair[0].shape[1] * pair[1].shape[1] // devices for pair in pairs]
    total_share = sum(shares)

    def term(start, count):
        blocks = count // total_share
        first_block = start // total_share
        pieces = [
            flat_piece(pair[0], pair[1], first_block * share, blocks * share).reshape(blocks, share)
            for pair, share in zip(pairs, shares)
        ]
        return jnp.concatenate(pieces, axis=1).reshape(-1)

    return (term, total_share, shares)


def split_shares(mine, shares):
    results = []
    offset = 0
    for share in shares:
        results.append(mine[offset : offset + share])
        offset = offset + share
    return results


def bias_rows(table_mat, onehot, length):
    rel_bias = lax.dot_general(
        table_mat, onehot, (((0,), (0,)), ((), ())), preferred_element_type=jnp.float32
    )
    return rel_bias.reshape(1, HEADS, length, length)


def masked_scores(queries, key_rows, rel_bias, allowed):
    scores = (
        jnp.einsum("bqhd,bkhd->bhqk", queries, key_rows, preferred_element_type=jnp.float32)
        + rel_bias
    )
    return jnp.where(allowed, scores, NEGATIVE)


def attend(queries, key_rows, values, rel_bias, allowed):
    scores = masked_scores(queries, key_rows, rel_bias, allowed)
    largest = jnp.max(scores, axis=-1, keepdims=True)
    summed = jnp.sum(jnp.exp(scores - largest), axis=-1, keepdims=True)
    log_total = largest + jnp.log(summed)
    attention = jnp.exp(scores - log_total).astype(jnp.bfloat16)
    context = jnp.einsum("bhqk,bkhd->bqhd", attention, values, preferred_element_type=jnp.float32)
    return (context.astype(jnp.bfloat16), log_total)


def attend_back(queries, key_rows, values, rel_bias, allowed, log_total, grad_context):
    scores = masked_scores(queries, key_rows, rel_bias, allowed)
    attention = jnp.exp(scores - log_total)
    grad_attention = jnp.einsum(
        "bqhd,bkhd->bhqk", grad_context, values, preferred_element_type=jnp.float32
    )
    grad_values = jnp.einsum(
        "bhqk,bqhd->bkhd",
        attention.astype(jnp.bfloat16),
        grad_context,
        preferred_element_type=jnp.float32,
    )
    weighted = jnp.sum(attention * grad_attention, axis=-1, keepdims=True)
    grad_scores = (attention * (grad_attention - weighted)).astype(jnp.bfloat16)
    grad_queries = jnp.einsum(
        "bhqk,bkhd->bqhd", grad_scores, key_rows, preferred_element_type=jnp.float32
    )
    grad_keys = jnp.einsum(
        "bhqk,bqhd->bkhd", grad_scores, queries, preferred_element_type=jnp.float32
    )
    return (
        grad_queries.astype(jnp.bfloat16),
        grad_keys.astype(jnp.bfloat16),
        grad_values.astype(jnp.bfloat16),
        grad_scores,
    )


def bias_grads(grad_scores, onehot):
    members = grad_scores.shape[0]
    flattened = grad_scores.reshape(members * HEADS, -1)
    summed = lax.dot_general(
        flattened, onehot, (((1,), (1,)), ((), ())), preferred_element_type=jnp.float32
    )
    return jnp.sum(summed.reshape(members, HEADS, BUCKETS), axis=0)


def local(
    document_tokens,
    document_lengths,
    query_tokens,
    query_lengths,
    weight_query,
    weight_key,
    weight_value,
    weight_out,
    weight_gate,
    weight_up,
    weight_down,
    weight_proj,
    norm_gains,
    rel_table,
    document_cotangent,
    query_cotangent,
):
    layouts = ((D, D), (D, D), (D, D), (D, D), (D, FF), (D, FF), (FF, D), (D, PROJ))
    devices = lax.axis_size("dp") * lax.axis_size("fsdp")
    gathered = (
        lax.all_gather(weight_query, ("dp", "fsdp"), axis=0, tiled=True),
        lax.all_gather(weight_key, ("dp", "fsdp"), axis=0, tiled=True),
        lax.all_gather(weight_value, ("dp", "fsdp"), axis=0, tiled=True),
        lax.all_gather(weight_out, ("dp", "fsdp"), axis=0, tiled=True),
        lax.all_gather(weight_gate, ("dp", "fsdp"), axis=0, tiled=True),
        lax.all_gather(weight_up, ("dp", "fsdp"), axis=0, tiled=True),
        lax.all_gather(weight_down, ("dp", "fsdp"), axis=0, tiled=True),
        lax.all_gather(weight_proj, ("dp", "fsdp"), axis=0, tiled=True),
    )
    matrices = [flat_rows.reshape(layout) for flat_rows, layout in zip(gathered, layouts)]
    gains_all, table_all = (
        lax.all_gather(norm_gains, "fsdp", axis=0, tiled=True),
        lax.all_gather(rel_table, "fsdp", axis=0, tiled=True),
    )
    gain_rows = gains_all.astype(jnp.float32).reshape(3, D)
    table_mat = table_all.reshape(BUCKETS, HEADS)
    documents = document_tokens.shape[0]
    queries_here = query_tokens.shape[0]
    doc_rows = documents * DOC_LEN
    doc_segments = segment_ids(document_lengths, DOC_LEN)
    query_segments = segment_ids(query_lengths.reshape(queries_here, 1), QRY_LEN)
    doc_allowed = doc_segments[:, None, :, None] == doc_segments[:, None, None, :]
    query_allowed = query_segments[:, None, :, None] == query_segments[:, None, None, :]
    doc_onehot = bucket_onehot(DOC_LEN)
    query_onehot = bucket_onehot(QRY_LEN)
    doc_bias = bias_rows(table_mat, doc_onehot, DOC_LEN)
    query_bias = bias_rows(table_mat, query_onehot, QRY_LEN)
    settings = [(doc_bias, doc_allowed, doc_onehot)]
    settings.append((query_bias, query_allowed, query_onehot))

    def split_blocks(matrix):
        blocks_out = [matrix[0:DOC_LEN].reshape(1, DOC_LEN, HEADS, HEAD_DIM)]
        blocks_out.append(matrix[doc_rows:].reshape(queries_here, QRY_LEN, HEADS, HEAD_DIM))
        return blocks_out

    query_mat, key_mat, value_mat, out_mat, gate_mat, up_mat, down_mat, proj_mat = matrices
    inputs = jnp.concatenate(
        [document_tokens.reshape(doc_rows, D), query_tokens.reshape(-1, D)], axis=0
    )
    residual_in = inputs.astype(jnp.float32)
    normed_one, norm_one_back = jax.vjp(rms_norm, residual_in, gain_rows[0])
    normed_one = normed_one.astype(jnp.bfloat16)
    queries = jnp.dot(normed_one, query_mat, preferred_element_type=jnp.float32).astype(
        jnp.bfloat16
    )
    key_rows = jnp.dot(normed_one, key_mat, preferred_element_type=jnp.float32).astype(jnp.bfloat16)
    values = jnp.dot(normed_one, value_mat, preferred_element_type=jnp.float32).astype(jnp.bfloat16)
    query_blocks = split_blocks(queries)
    key_blocks = split_blocks(key_rows)
    value_blocks = split_blocks(values)
    contexts = []
    log_totals = []
    for query_block, key_block, value_block, setting in zip(
        query_blocks, key_blocks, value_blocks, settings
    ):
        context_block, log_total = attend(
            query_block, key_block, value_block, setting[0], setting[1]
        )
        contexts.append(context_block.reshape(-1, D))
        log_totals.append(log_total)
    context = jnp.concatenate(contexts, axis=0)
    hidden = residual_in + jnp.dot(context, out_mat, preferred_element_type=jnp.float32)
    normed_two, norm_two_back = jax.vjp(rms_norm, hidden, gain_rows[1])
    normed_two = normed_two.astype(jnp.bfloat16)
    gate = jnp.dot(normed_two, gate_mat, preferred_element_type=jnp.float32)
    upper = jnp.dot(normed_two, up_mat, preferred_element_type=jnp.float32)
    inner, gated_back = jax.vjp(gated_unit, gate, upper)
    inner = inner.astype(jnp.bfloat16)
    final = hidden + jnp.dot(inner, down_mat, preferred_element_type=jnp.float32)
    normed_three, norm_three_back = jax.vjp(rms_norm, final, gain_rows[2])
    normed_three = normed_three.astype(jnp.bfloat16)
    output = jnp.dot(normed_three, proj_mat, preferred_element_type=jnp.float32).astype(
        jnp.bfloat16
    )
    again = (
        lax.all_gather(weight_query, ("dp", "fsdp"), axis=0, tiled=True),
        lax.all_gather(weight_key, ("dp", "fsdp"), axis=0, tiled=True),
        lax.all_gather(weight_value, ("dp", "fsdp"), axis=0, tiled=True),
        lax.all_gather(weight_out, ("dp", "fsdp"), axis=0, tiled=True),
        lax.all_gather(weight_gate, ("dp", "fsdp"), axis=0, tiled=True),
        lax.all_gather(weight_up, ("dp", "fsdp"), axis=0, tiled=True),
        lax.all_gather(weight_down, ("dp", "fsdp"), axis=0, tiled=True),
        lax.all_gather(weight_proj, ("dp", "fsdp"), axis=0, tiled=True),
    )
    back_mats = [flat_rows.reshape(layout) for flat_rows, layout in zip(again, layouts)]
    back_query, back_key, back_value, back_out, back_gate, back_up, back_down, back_proj = back_mats
    cotangent = jnp.concatenate(
        [document_cotangent.reshape(doc_rows, PROJ), query_cotangent.reshape(-1, PROJ)], axis=0
    )
    grad_final, grad_gain_three = norm_three_back(times_transposed(cotangent, back_proj))
    grad_ffn = grad_final.astype(jnp.bfloat16)
    grad_gate_f, grad_upper_f = gated_back(times_transposed(grad_ffn, back_down))
    grad_gate_b = grad_gate_f.astype(jnp.bfloat16)
    grad_upper_b = grad_upper_f.astype(jnp.bfloat16)
    grad_normed_two = times_transposed(grad_gate_b, back_gate) + times_transposed(
        grad_upper_b, back_up
    )
    grad_hidden_part, grad_gain_two = norm_two_back(grad_normed_two)
    grad_hidden = grad_final + grad_hidden_part
    ffn_pairs = [
        (normed_two, grad_gate_b),
        (normed_two, grad_upper_b),
        (inner, grad_ffn),
        (normed_three, cotangent),
    ]
    grad_branch = grad_hidden.astype(jnp.bfloat16)
    grad_context = times_transposed(grad_branch, back_out).astype(jnp.bfloat16)
    table_grad = jnp.zeros((HEADS, BUCKETS), jnp.float32)
    grad_query_parts = []
    grad_key_parts = []
    grad_value_parts = []
    for query_block, key_block, value_block, setting, log_total, grad_block in zip(
        query_blocks, key_blocks, value_blocks, settings, log_totals, split_blocks(grad_context)
    ):
        grad_q_block, grad_k_block, grad_v_block, grad_scores = attend_back(
            query_block, key_block, value_block, setting[0], setting[1], log_total, grad_block
        )
        table_grad = table_grad + bias_grads(grad_scores, setting[2])
        grad_query_parts.append(grad_q_block.reshape(-1, D))
        grad_key_parts.append(grad_k_block.reshape(-1, D))
        grad_value_parts.append(grad_v_block.reshape(-1, D))
    grad_queries = jnp.concatenate(grad_query_parts, axis=0)
    grad_keys = jnp.concatenate(grad_key_parts, axis=0)
    grad_values = jnp.concatenate(grad_value_parts, axis=0)
    grad_normed_one = (
        times_transposed(grad_queries, back_query)
        + times_transposed(grad_keys, back_key)
        + times_transposed(grad_values, back_value)
    )
    grad_input_part, grad_gain_one = norm_one_back(grad_normed_one)
    grad_inputs = (grad_hidden + grad_input_part).astype(jnp.bfloat16)
    attn_pairs = [
        (normed_one, grad_queries),
        (normed_one, grad_keys),
        (normed_one, grad_values),
        (context, grad_branch),
    ]
    all_term, all_total, all_shares = grad_terms(attn_pairs + ffn_pairs, devices)
    shares = tuple(
        split_shares(
            lax.psum_scatter(
                all_term(jnp.int32(0), lax.axis_size(("dp", "fsdp")) * all_total),
                ("dp", "fsdp"),
                scatter_dimension=0,
                tiled=True,
            ),
            all_shares,
        )
    )
    gain_grads = jnp.concatenate([grad_gain_one, grad_gain_two, grad_gain_three], axis=0)
    table_flat = jnp.transpose(table_grad).reshape(-1)
    gain_whole, table_whole = lax.psum((gain_grads, table_flat), ("dp", "fsdp"))
    fsdp_index = lax.axis_index("fsdp")
    fsdp_count = lax.axis_size("fsdp")
    gain_share = 3 * D // fsdp_count
    table_share = BUCKETS * HEADS // fsdp_count
    own_gains = lax.dynamic_slice_in_dim(gain_whole, fsdp_index * gain_share, gain_share)
    own_table = lax.dynamic_slice_in_dim(table_whole, fsdp_index * table_share, table_share)
    return (
        output[:doc_rows].reshape(documents, DOC_LEN, PROJ),
        output[doc_rows:].reshape(queries_here, QRY_LEN, PROJ),
        grad_inputs[:doc_rows].reshape(documents, DOC_LEN, D),
        grad_inputs[doc_rows:].reshape(queries_here, QRY_LEN, D),
        shares[0],
        shares[1],
        shares[2],
        shares[3],
        shares[4],
        shares[5],
        shares[6],
        shares[7],
        own_gains,
        own_table,
    )


WIDTHS = (3 * D, D + PROJ, 2 * FF, D)
SHARE_ROWS = (24, 24, 24, 96)
GATHER_STAGES = (
    (0, 0, 768),
    (0, 768, 768),
    (0, 1536, 768),
    (1, 0, 896),
    (2, 0, 1536),
    (2, 1536, 1536),
    (2, 3072, 1536),
    (2, 4608, 1536),
    (3, 0, 384),
    (3, 384, 384),
)
MESH_ID = pl.DeviceIdType.MESH


def remote(source, target, send_sem, recv_sem, device):
    return pltpu.make_async_remote_copy(
        src_ref=source,
        dst_ref=target,
        send_sem=send_sem,
        recv_sem=recv_sem,
        device_id=device,
        device_id_type=MESH_ID,
    )


class Place:
    def __init__(self):
        self.dp = lax.axis_index("dp")
        self.z = lax.axis_index("fsdp")
        self.core = lax.rem(self.dp, 2)
        self.xy = self.dp // 2
        self.xy_x = self.xy + 1 - 2 * lax.rem(self.xy, 2)
        self.xy_y = lax.rem(self.xy + 2, 4)
        self.xy_d = 3 - self.xy
        self.sib = self.dp + 1 - 2 * self.core
        self.dp_x = 2 * self.xy_x + self.core
        self.dp_y = 2 * self.xy_y + self.core
        self.dp_d = 2 * self.xy_d + self.core
        self.zs = [lax.rem(self.z + step, 4) for step in (1, 2, 3)]
        self.to_sib = {"dp": self.sib}
        self.to_x = {"dp": self.dp_x}
        self.to_y = {"dp": self.dp_y}
        self.to_z = [{"fsdp": other} for other in self.zs]

    def barrier(self):
        semaphore = pltpu.get_barrier_semaphore()
        for device in [self.to_sib, self.to_x, self.to_y] + self.to_z:
            pl.semaphore_signal(semaphore, inc=1, device_id=device, device_id_type=MESH_ID)
        pl.semaphore_wait(semaphore, 6)


class Gather:
    def __init__(self, place, shards, whole, parts, sems):
        self.place, self.shards, self.whole, self.parts = place, shards, whole, parts
        (self.z_send, self.z_recv, self.send, self.recv, self.early_send, self.early_recv) = sems
        self.stages = GATHER_STAGES
        self.early = len(GATHER_STAGES) - 1

    @staticmethod
    def scratch():
        count = len(GATHER_STAGES)
        dma = pltpu.SemaphoreType.DMA
        return [dma((count, 3)), dma((count, 3)), dma((count, 9)), dma((count, 9)), dma((4, 3)), dma((4, 3))]

    def z_copy(self, s, k):
        array, first, width = self.stages[s]
        place = self.place
        columns = pl.ds(first, width)
        if array == 3:
            target = self.whole[3].at[place.xy, place.core, place.z, :, columns]
        else:
            target = self.parts[array].at[k, :, columns]
        return remote(
            self.shards[array].at[:, columns],
            target,
            self.z_send.at[s, k],
            self.z_recv.at[s, k],
            place.to_z[k],
        )

    def block(self, s, dp, half=None):
        array, first, width = self.stages[s]
        columns = pl.ds(first, width)
        if s == self.early:
            rows = pl.ds(0, 96) if half is None else pl.ds(48 * half, 48)
            return self.whole[3].at[dp // 2, self.place.core, self.place.z, rows, columns]
        if array == 3:
            layers = pl.ds(0, 4) if half is None else pl.ds(2 * half, 2)
            return self.whole[3].at[dp // 2, self.place.core, layers, :, columns]
        start, count = (96 * dp, 96) if half is None else (96 * dp + 48 * half, 48)
        return self.whole[array].at[pl.ds(pl.multiple_of(start, 48), count), columns]

    def hop(self, s, index):
        place = self.place
        dp, half, device = (
            (place.dp, None, place.to_x),
            (place.dp, None, place.to_y),
            (place.dp_x, 0, place.to_y),
            (place.dp_y, 1, place.to_x),
            (place.dp, None, place.to_sib),
            (place.dp_x, None, place.to_sib),
            (place.dp_y, None, place.to_sib),
            (place.dp_d, 0, place.to_sib),
            (place.dp_d, 1, place.to_sib),
        )[index]
        block = self.block(s, dp, half)
        return remote(block, block, self.send.at[s, index], self.recv.at[s, index], device)

    def begin(self, s):
        for k in range(3):
            self.z_copy(s, k).start()

    def spread(self, s):
        array, first, width = self.stages[s]
        place = self.place
        columns = pl.ds(first, width)
        for k in range(3):
            self.z_copy(s, k).wait_recv()
        if array == 3:
            self.whole[3][place.xy, place.core, place.z, :, columns] = self.shards[3][:, columns]
        else:
            pieces = []
            for other in range(4):
                piece = self.shards[array][:, columns]
                for k in range(3):
                    here = lax.rem(place.z + 3 - k, 4) == other
                    piece = jnp.where(here, self.parts[array][k, :, columns], piece)
                pieces.append(piece)
            rows = pl.ds(pl.multiple_of(96 * place.dp, 96), 96)
            self.whole[array][rows, columns] = jnp.concatenate(pieces, axis=0)
        for index in (0, 1, 4):
            self.hop(s, index).start()

    def relay(self, s):
        self.hop(s, 0).wait_recv()
        self.hop(s, 2).start()
        self.hop(s, 5).start()
        self.hop(s, 1).wait_recv()
        self.hop(s, 3).start()
        self.hop(s, 6).start()

    def hand_over(self, s):
        self.hop(s, 2).wait_recv()
        self.hop(s, 7).start()
        self.hop(s, 3).wait_recv()
        self.hop(s, 8).start()

    def arrive(self, s):
        for index in range(4, 9):
            self.hop(s, index).wait_recv()

    def step(self, t):
        for lag, work in enumerate((self.spread, self.relay, self.hand_over, self.arrive)):
            if 0 <= t - lag < self.early:
                work(t - lag)

    def early_layer(self, index):
        place = self.place
        array, first, width = self.stages[self.early]
        z = place.z if index == 0 else lax.rem(place.z + 4 - index, 4)
        block = self.whole[3].at[:, place.core, z, :, pl.ds(first, width)]
        return remote(
            block,
            block,
            self.send.at[self.early, 4 + index],
            self.recv.at[self.early, 4 + index],
            place.to_sib,
        )

    def early_z(self, piece, k):
        place = self.place
        array, first, width = self.stages[self.early]
        xy = (place.xy, place.xy_x, place.xy_y, place.xy_d)[piece]
        block = self.whole[3].at[xy, place.core, place.z, :, pl.ds(first, width)]
        return remote(
            block, block, self.early_send.at[piece, k], self.early_recv.at[piece, k], place.to_z[k]
        )

    def early_begin(self):
        place = self.place
        array, first, width = self.stages[self.early]
        columns = pl.ds(first, width)
        self.whole[3][place.xy, place.core, place.z, :, columns] = self.shards[3][:, columns]
        self.hop(self.early, 0).start()
        self.hop(self.early, 1).start()

    def early_relay(self):
        self.hop(self.early, 0).wait_recv()
        self.hop(self.early, 2).start()
        self.hop(self.early, 1).wait_recv()
        self.hop(self.early, 3).start()

    def early_square(self):
        self.hop(self.early, 2).wait_recv()
        self.hop(self.early, 3).wait_recv()
        self.early_layer(0).start()

    def early_send_z(self, piece):
        for k in range(3):
            self.early_z(piece, k).start()

    def early_layers(self):
        for k in range(3):
            for piece in range(4):
                self.early_z(piece, k).wait_recv()
            self.early_layer(k + 1).start()

    def early_arrive(self):
        for index in range(4):
            self.early_layer(index).wait_recv()

    def finish(self):
        for s in range(self.early):
            for k in range(3):
                self.z_copy(s, k).wait_send()
            for index in range(9):
                self.hop(s, index).wait_send()
        for index in range(4):
            self.hop(self.early, index).wait_send()
            self.early_layer(index).wait_send()
            for k in range(3):
                self.early_z(index, k).wait_send()


SCATTER_WIDTHS = (3 * D, D + PROJ, 2 * FF, 1920)
SCATTER_STAGES = (
    (3, 0, 1536),
    (3, 384, 1536),
    (2, 0, 1536),
    (2, 1536, 1536),
    (2, 3072, 1536),
    (2, 4608, 1536),
    (1, 0, 896),
    (0, 0, 768),
    (0, 768, 768),
    (0, 1536, 768),
)
SCATTER_LAGS = ((0, 1, 6, 8, 10),) + ((0, 1, 2, 4, 6),) * 6 + ((0, 1, 2, 3, 4),) * 3
SCATTER_ORDER = (1, 0, 2, 3, 4, 5, 6, 7, 8, 9)
SCATTER_HELD = (
    (0, 0),
    (1, 0),
    (2, 0),
    (3, 0),
    (4, 0),
    (5, 0),
    (6, 0),
    (7, 0),
    (7, 768),
    (8, 0),
)


class Scatter:
    def __init__(self, place, buffers, settled, sems):
        self.place, self.settled = place, settled
        self.local_all, self.held_all = buffers[0:2]
        self.from_x, self.from_y = buffers[2:6], buffers[6:10]
        self.diag_x, self.diag_y = buffers[10:14], buffers[14:18]
        self.z_out, self.z_in = buffers[18:22], buffers[22:26]
        self.early, self.early_in = self.held_all.at[0], buffers[26]
        self.send, self.recv = sems
        self.begun = {}

    @staticmethod
    def scratch():
        kind = jnp.bfloat16
        shapes = [pltpu.VMEM((2, 4, 2, 96, 1536), kind), pltpu.VMEM((9, 4, 96, 1536), kind)]
        shapes += [pltpu.VMEM((96, w), kind) for w in SCATTER_WIDTHS] * 2
        shapes += [pltpu.VMEM((48, w), kind) for w in SCATTER_WIDTHS] * 2
        pieces = [(24, w) for w in SCATTER_WIDTHS[:3]] + [(96, 384)]
        shapes += [pltpu.VMEM((4, r, w), kind) for r, w in pieces]
        shapes += [pltpu.VMEM((3, r, w), kind) for r, w in pieces]
        shapes += [pltpu.VMEM((3, 4, 96, 384), kind)]
        return shapes

    @staticmethod
    def semaphores():
        count = len(SCATTER_STAGES)
        dma = pltpu.SemaphoreType.DMA
        return [dma((count, 8)), dma((count, 8))]

    def local(self, s):
        slot = SCATTER_ORDER.index(s) % 2
        return self.local_all.at[slot, :, :, :, pl.ds(0, SCATTER_STAGES[s][2])]

    def held(self, s):
        slot, first = SCATTER_HELD[s]
        return self.held_all.at[slot, :, :, pl.ds(first, SCATTER_STAGES[s][2])]

    def columns(self, s):
        return pl.ds(SCATTER_STAGES[s][1], SCATTER_STAGES[s][2])

    def z_columns(self, s):
        array, first, width = SCATTER_STAGES[s]
        return pl.ds(0, 384) if array == 3 else pl.ds(first, width)

    def early_columns(self, z):
        return pl.ds(pl.multiple_of(384 * z, 128), 384)

    def early_copy(self, index):
        place = self.place
        mine = self.early_columns(place.z)
        column = pl.ds(0, 384)
        if index == 1:
            source = self.early.at[place.xy_d, pl.ds(0, 48), mine]
            target, device = self.diag_x[3].at[:, column], place.to_x
        elif index == 2:
            source = self.early.at[place.xy_d, pl.ds(48, 48), mine]
            target, device = self.diag_y[3].at[:, column], place.to_y
        elif index == 3:
            source = self.early.at[place.xy_x, :, mine]
            target, device = self.from_x[3].at[:, column], place.to_x
        elif index == 4:
            source = self.early.at[place.xy_y, :, mine]
            target, device = self.from_y[3].at[:, column], place.to_y
        else:
            k = index - 5
            source = self.early.at[:, :, self.early_columns(place.zs[k])]
            target, device = self.early_in.at[k], place.to_z[k]
        return remote(source, target, self.send.at[0, index], self.recv.at[0, index], device)

    def early_pair(self):
        self.copy(0, 0).wait_recv()
        self.gather_pair(0, range(4))
        for k in range(3):
            self.early_copy(5 + k).start()

    def early_sum(self):
        place = self.place
        mine = self.early_columns(place.z)
        for k in range(3):
            self.early_copy(5 + k).wait_recv()
        for block in range(4):
            total = self.early[block, :, mine].astype(jnp.float32)
            for k in range(3):
                total = total + self.early_in[k, block].astype(jnp.float32)
            self.early[block, :, mine] = total.astype(jnp.bfloat16)
        self.early_copy(1).start()
        self.early_copy(2).start()

    def early_cross(self):
        place = self.place
        mine = self.early_columns(place.z)
        for index, block, half, source in (
            (1, place.xy_y, slice(0, 48), self.diag_x[3]),
            (2, place.xy_x, slice(48, 96), self.diag_y[3]),
        ):
            self.early_copy(index).wait_recv()
            total = self.early[block, half, mine].astype(jnp.float32)
            total = total + source[:, 0:384].astype(jnp.float32)
            self.early[block, half, mine] = total.astype(jnp.bfloat16)
            self.early_copy(5 - index).start()

    def early_settle(self):
        place = self.place
        self.early_copy(3).wait_recv()
        self.early_copy(4).wait_recv()
        total = self.early[place.xy, :, self.early_columns(place.z)].astype(jnp.float32)
        total = total + self.from_x[3][:, 0:384].astype(jnp.float32)
        total = total + self.from_y[3][:, 0:384].astype(jnp.float32)
        self.settled(0, total)

    def copy(self, s, index):
        array, first, width = SCATTER_STAGES[s]
        place = self.place
        columns = self.columns(s)
        held = self.held(s)
        if index == 0:
            source = self.local(s).at[:, 1 - place.core]
            target = held
            device = place.to_sib
        elif index == 1:
            source = held.at[place.xy_d, pl.ds(0, 48)]
            target = self.diag_x[array].at[:, columns]
            device = place.to_x
        elif index == 2:
            source = held.at[place.xy_d, pl.ds(48, 48)]
            target = self.diag_y[array].at[:, columns]
            device = place.to_y
        elif index == 3:
            source = held.at[place.xy_x]
            target = self.from_x[array].at[:, columns]
            device = place.to_x
        elif index == 4:
            source = held.at[place.xy_y]
            target = self.from_y[array].at[:, columns]
            device = place.to_y
        else:
            k = index - 5
            source = self.z_out[array].at[place.zs[k], :, self.z_columns(s)]
            target = self.z_in[array].at[k, :, self.z_columns(s)]
            device = place.to_z[k]
        return remote(source, target, self.send.at[s, index], self.recv.at[s, index], device)

    def add(self, s, block, other, rows=slice(None)):
        held = self.held(s)
        total = held[block, rows].astype(jnp.float32) + other.astype(jnp.float32)
        held[block, rows] = total.astype(jnp.bfloat16)

    def free(self, s):
        turn = SCATTER_ORDER.index(s)
        if turn >= 2:
            self.copy(SCATTER_ORDER[turn - 2], 0).wait_send()

    def begin(self, s):
        self.copy(s, 0).start()

    def gather_pair(self, s, blocks):
        local = self.local(s)
        for block in blocks:
            self.add(s, block, local[block, self.place.core])

    def pair(self, s):
        place = self.place
        self.copy(s, 0).wait_recv()
        self.gather_pair(s, [place.xy_d])
        self.copy(s, 1).start()
        self.copy(s, 2).start()
        self.gather_pair(s, [place.xy_x, place.xy_y, place.xy])

    def cross(self, s):
        array = SCATTER_STAGES[s][0]
        place = self.place
        columns = self.columns(s)
        self.copy(s, 1).wait_recv()
        self.add(s, place.xy_y, self.diag_x[array][:, columns], slice(0, 48))
        self.copy(s, 4).start()
        self.copy(s, 2).wait_recv()
        self.add(s, place.xy_x, self.diag_y[array][:, columns], slice(48, 96))
        self.copy(s, 3).start()

    def square(self, s):
        array, first, width = SCATTER_STAGES[s]
        place = self.place
        self.copy(s, 3).wait_recv()
        self.copy(s, 4).wait_recv()
        held = self.held(s)
        for other in range(4):
            if array == 3:
                rows, inside = slice(0, 96), pl.ds(384 * other, 384)
                outside = pl.ds(first + 384 * other, 384)
            else:
                rows, inside = slice(24 * other, 24 * other + 24), pl.ds(0, width)
                outside = pl.ds(first, width)
            total = (
                held[place.xy, rows, inside].astype(jnp.float32)
                + self.from_x[array][rows, outside].astype(jnp.float32)
                + self.from_y[array][rows, outside].astype(jnp.float32)
            )
            self.z_out[array][other, :, self.z_columns(s)] = total.astype(jnp.bfloat16)
        for k in range(3):
            self.copy(s, 5 + k).start()

    def settle(self, s):
        array = SCATTER_STAGES[s][0]
        columns = self.z_columns(s)
        total = self.z_out[array][self.place.z, :, columns].astype(jnp.float32)
        for k in range(3):
            self.copy(s, 5 + k).wait_recv()
            total = total + self.z_in[array][k, :, columns].astype(jnp.float32)
        self.settled(s, total)

    def step(self, turn, s=None):
        if s is not None:
            self.begun[s] = turn
        for other in sorted(self.begun, reverse=True):
            lag = turn - self.begun[other]
            if lag in SCATTER_LAGS[other]:
                phase = SCATTER_LAGS[other].index(lag)
                if other == 0 and phase:
                    (self.early_pair, self.early_sum, self.early_cross, self.early_settle)[phase - 1]()
                else:
                    (self.begin, self.pair, self.cross, self.square, self.settle)[phase](other)

    def finish(self):
        for index in range(1, 8):
            self.early_copy(index).wait_send()
        count = len(SCATTER_STAGES)
        for s in range(1, count):
            for index in range(0 if s >= count - 2 else 1, 8):
                self.copy(s, index).wait_send()

ROW_BLOCK = 128
SCALE = 0.7978845608028654
BF = jnp.bfloat16
F32 = jnp.float32
ROWS_ALL = 768
NEAR = 3 * ROW_BLOCK


def dot(left, right, left_dim=1, right_dim=0):
    return lax.dot_general(
        left, right, (((left_dim,), (right_dim,)), ((), ())), preferred_element_type=F32
    )


def loop(count, body):
    def step(index, carry):
        body(index)
        return carry

    lax.fori_loop(0, count, step, 0)


def aligned(start, multiple, size):
    return pl.ds(pl.multiple_of(start, multiple), size)


def unflatten(flat, wide, target, start_of):
    lines = flat.shape[0]
    rows = target.shape[0]
    blocks = lines // rows
    wide[0:lines] = flat[...].astype(F32)
    for block in range(blocks):
        first = start_of(block)
        target[:, first : first + 128] = wide[pl.ds(block, rows, blocks), :].astype(BF)


def marks_of(relative):
    distance = jnp.abs(relative)
    distant = jnp.full_like(distance, 8)
    for power in range(1, 8):
        distant = distant + (distance * distance >= 64 * 2**power).astype(jnp.int32)
    bucket = jnp.where(distance < 8, distance, distant)
    bucket = bucket + 16 * (relative > 0).astype(jnp.int32)
    labels = lax.broadcasted_iota(jnp.int32, relative.shape, 0)
    return bucket == labels


def normed(values, gain_row):
    inverse = lax.rsqrt(jnp.mean(values * values, axis=-1, keepdims=True) + EPSILON)
    return values * inverse * gain_row


def window(block):
    return max(0, block - 2), min(3, block + 2)


def head_lanes(rows, which):
    lane = lax.broadcasted_iota(jnp.int32, (rows, 128), 1)
    return lane < HEAD_DIM if which == 0 else lane >= HEAD_DIM


def keep(values, which):
    return jnp.where(head_lanes(values.shape[0], which), values, jnp.zeros_like(values))


def softmax_rows(scores):
    largest = jnp.max(scores, axis=-1, keepdims=True)
    powers = jnp.exp(scores - largest)
    return (powers * (1.0 / jnp.sum(powers, axis=-1, keepdims=True))).astype(BF)


FORWARD_SAVED = (
    ((768, 3 * D), BF),
    ((768, D + PROJ), BF),
    ((768, 2 * FF), BF),
    ((4, 2, 4, 96, D), BF),
    ((768, D), BF),
    ((768, 3 * D), BF),
    ((768, D), BF),
    ((768, D), F32),
    ((768, D), BF),
    ((768, 2 * FF), BF),
    ((768, FF), BF),
    ((768, D), F32),
    ((768, D), BF),
    ((6, 512, 1024), BF),
    ((256, 1536), BF),
)


def forward_kernel(*refs):
    (doc, qry, doc_lengths, qry_lengths, small) = refs[0:5]
    flats = refs[5:13]
    doc_out, qry_out, gains_out = refs[13:16]
    saved = refs[16:31]
    rest = refs[31:]
    whole, parts, shards = rest[0:4], rest[4:7], rest[7:11]
    (wide, small_in, gains, diagonals, bias, id_column, id_row) = rest[11:18]
    (norm_one, qkv, context, hidden, norm_two, factors, inner, norm_three) = rest[18:26]
    (prob_doc, prob_qry, scores) = rest[26:29]
    gather_sems = rest[29:35]
    small_send, small_recv, save_sem, whole_sem, chunk_sem = rest[35:40]

    place = Place()
    place.barrier()
    gains[...] = jnp.zeros_like(gains)
    gather = Gather(place, shards, whole, parts, gather_sems)

    def small_copy(k):
        return remote(
            small, small_in.at[k], small_send.at[k], small_recv.at[k], place.to_z[k]
        )

    for k in range(3):
        small_copy(k).start()
    unflatten(flats[6], wide, shards[3], lambda j: 128 * j)
    gather.early_begin()
    for index in range(3):
        unflatten(flats[index], wide, shards[0].at[:, D * index : D * index + D], lambda j: 128 * j)
        gather.begin(index)

    def later_shards(turn):
        if turn == 0:
            unflatten(flats[3], wide, shards[1].at[:, 0:D], lambda j: 128 * j)
            shards[1][:, D:] = flats[7][...]
            gather.begin(3)
            unflatten(flats[4], wide, shards[2], lambda j: 1536 * (j // 6) + 128 * (j % 6))
            unflatten(flats[5], wide, shards[2], lambda j: 1536 * (j // 6) + 128 * (j % 6) + D)
        if 4 <= turn + 3 < 9:
            gather.begin(turn + 3)

    saves = []

    def save(index, source, target=None):
        copy = pltpu.make_async_copy(
            source, saved[index] if target is None else target, save_sem.at[index]
        )
        copy.start()
        saves.append((index, copy))
        return copy

    def save_part(semaphore, source, target):
        copy = pltpu.make_async_copy(source, target, semaphore)
        copy.start()
        saves.append((-1, copy))

    def save_whole(s):
        array, first, width = GATHER_STAGES[s]
        columns = pl.ds(first, width)
        if array == 3:
            here = (slice(None), slice(None), slice(None), slice(None), columns)
        else:
            here = (slice(None), columns)
        save_part(whole_sem.at[s], whole[array].at[here], saved[array].at[here])

    def small_arrive():
        for k in range(3):
            small_copy(k).wait_recv()
        pieces = []
        for other in range(4):
            piece = small[...]
            for k in range(3):
                here = lax.rem(place.z + 3 - k, 4) == other
                piece = jnp.where(here, small_in[k], piece)
            pieces.append(piece)
        low = lax.broadcasted_iota(jnp.int32, (1, 128), 1) < 64
        for row in range(3):
            for tile in range(6):
                unit = 12 * row + 2 * tile
                left = pieces[unit // 9][unit % 9 : unit % 9 + 1, :]
                unit = unit + 1
                right = pieces[unit // 9][unit % 9 : unit % 9 + 1, :]
                gains[row : row + 1, 128 * tile : 128 * tile + 128] = jnp.where(low, left, right)
        gains_out[...] = gains[...]
        table = jnp.concatenate([piece[16:24, :] for piece in pieces], axis=0).astype(BF)
        relative = lax.broadcasted_iota(jnp.int32, (BUCKETS, 512), 1) - 256
        diagonals[...] = dot(table, marks_of(relative).astype(BF), 0, 0)[0:16]

    def make_bias(head):
        rows = jnp.broadcast_to(diagonals[pl.ds(head, 1), :], (8, 512))
        lines = lax.broadcasted_iota(jnp.int32, (8, 512), 0)
        for bit in range(3):
            moved = pltpu.roll(rows, 2**bit, 1)
            rows = jnp.where(lax.rem(lines // 2**bit, 2) == 1, moved, rows)
        for group in range(ROW_BLOCK // 8):
            moved = pltpu.roll(rows, 8 * group, 1) if group else rows
            bias[head, 8 * group : 8 * group + 8, :] = moved[:, 128:512]

    def make_ids():
        position = lax.broadcasted_iota(jnp.int32, (512, 128), 0)
        across = lax.broadcasted_iota(jnp.int32, (8, 512), 1)
        down_id, across_id = jnp.zeros_like(position), jnp.zeros_like(across)
        edge = 0
        for index in range(4):
            edge = edge + doc_lengths[0, index]
            down_id = down_id + (position >= edge).astype(jnp.int32)
            across_id = across_id + (across >= edge).astype(jnp.int32)
        id_column[0:512] = down_id
        id_row[:, 0:512] = across_id
        position = lax.broadcasted_iota(jnp.int32, (32, 128), 0)
        across = lax.broadcasted_iota(jnp.int32, (8, 256), 1)
        across_id = jnp.zeros_like(across)
        for index in range(8):
            length = qry_lengths[0, index]
            id_column[512 + 32 * index : 544 + 32 * index] = 2 * index + (
                position >= length
            ).astype(jnp.int32)
            mine = (across >= 32 * index) & (across < 32 * index + 32)
            value = 2 * index + (across >= length + 32 * index).astype(jnp.int32)
            across_id = jnp.where(mine, value, across_id)
        id_row[:, 512:768] = across_id

    def first_norm():
        gain = gains[0:1, :]

        def documents(index):
            rows = aligned(128 * index, 128, 128)
            norm_one[rows] = normed(doc[rows].astype(F32), gain).astype(BF)

        def queries(index):
            rows = aligned(128 * index, 128, 128)
            norm_one[aligned(512 + 128 * index, 128, 128)] = normed(
                qry[rows].astype(F32), gain
            ).astype(BF)

        loop(4, documents)
        loop(2, queries)
        save(4, norm_one)

    def project(index):
        columns = pl.ds(D * index, D)
        qkv[:, columns] = dot(norm_one[...], whole[0][:, columns]).astype(BF)

    def attend_pair(pair):
        query = qkv[0:512, aligned(128 * pair, 128, 128)]
        key = qkv[0:512, aligned(D + 128 * pair, 128, 128)]
        value = qkv[0:512, aligned(2 * D + 128 * pair, 128, 128)]
        for which in range(2):
            head = 2 * pair + which
            scores[...] = dot(keep(query, which), key, 1, 1)
            far_left = jnp.broadcast_to(bias[head, 127:128, 0:1], (128, 128))
            far_right = jnp.broadcast_to(bias[head, 0:1, NEAR - 1 : NEAR], (128, 128))
            for block in range(4):
                low, high = window(block)
                near_low, near_high = max(low, block - 1), min(high, block + 1)
                pieces = [far_left] * (near_low - low)
                pieces.append(
                    bias[
                        head,
                        :,
                        128 * (near_low - block + 1) : 128 * (near_high - block + 2),
                    ]
                )
                pieces += [far_right] * (high - near_high)
                rows = slice(128 * block, 128 * block + 128)
                columns = slice(128 * low, 128 * high + 128)
                allowed = id_column[rows, 0:1] == id_row[0:1, columns]
                values = scores[rows, columns] + jnp.concatenate(pieces, axis=1)
                share = softmax_rows(jnp.where(allowed, values, NEGATIVE))
                prob_doc[
                    pair, rows, 512 * which + 128 * low : 512 * which + 128 * high + 128
                ] = share
        both = jnp.concatenate([keep(value, 0), keep(value, 1)], axis=0)
        context[0:512, aligned(128 * pair, 128, 128)] = dot(prob_doc[pair], both).astype(BF)
        for block in range(2):
            rows = slice(512 + 128 * block, 640 + 128 * block)
            query = qkv[rows, aligned(128 * pair, 128, 128)]
            key = qkv[rows, aligned(D + 128 * pair, 128, 128)]
            value = qkv[rows, aligned(2 * D + 128 * pair, 128, 128)]
            allowed = id_column[rows, 0:1] == id_row[0:1, rows]
            shares = []
            for which in range(2):
                values = dot(keep(query, which), key, 1, 1)
                values = values + bias[2 * pair + which, :, 128:256]
                shares.append(softmax_rows(jnp.where(allowed, values, NEGATIVE)))
            shares = jnp.concatenate(shares, axis=1)
            prob_qry[128 * block : 128 * block + 128, aligned(256 * pair, 128, 256)] = shares
            both = jnp.concatenate([keep(value, 0), keep(value, 1)], axis=0)
            context[rows, aligned(128 * pair, 128, 128)] = dot(shares, both).astype(BF)

    def attend(first, last):
        lax.fori_loop(first, last, lambda pair, carry: (attend_pair(pair), carry)[1], 0)

    def after_attention():
        save(5, qkv)
        save(6, context)
        save(13, prob_doc)
        save(14, prob_qry)

        def one(tokens, offset):
            def block(index):
                source = aligned(128 * index, 128, 128)
                rows = aligned(offset + 128 * index, 128, 128)
                total = tokens[source].astype(F32) + dot(context[rows], whole[1][:, 0:D])
                hidden[rows] = total
                norm_two[rows] = normed(total, gains[1:2, :]).astype(BF)

            return block

        loop(4, one(doc, 0))
        loop(2, one(qry, 512))
        copy = save(7, hidden)
        save(8, norm_two)
        return copy

    def gated(chunk):
        def block(index):
            rows = aligned(256 * index, 256, 256)
            left = norm_two[rows]
            gate = dot(left, whole[2][:, 1536 * chunk : 1536 * chunk + D])
            upper = dot(left, whole[2][:, 1536 * chunk + D : 1536 * chunk + 2 * D])
            square = gate * gate
            bend = jnp.tanh(SCALE * gate * (1.0 + 0.044715 * square))
            half = 0.5 * (1.0 + bend)
            active = gate * half
            slope = half + 0.5 * gate * (1.0 - bend * bend) * (
                SCALE + (3.0 * 0.044715 * SCALE) * square
            )
            inner[rows, D * chunk : D * chunk + D] = (active * upper).astype(BF)
            factors[rows, 1536 * chunk : 1536 * chunk + D] = (upper * slope).astype(BF)
            factors[rows, 1536 * chunk + D : 1536 * chunk + 2 * D] = active.astype(BF)

        loop(3, block)
        here = (slice(None), pl.ds(1536 * chunk, 1536))
        save_part(chunk_sem.at[0, chunk], factors.at[here], saved[9].at[here])
        here = (slice(None), pl.ds(D * chunk, D))
        save_part(chunk_sem.at[1, chunk], inner.at[here], saved[10].at[here])

    def descend(half):
        columns = slice(384 * half, 384 * half + 384)

        def block(index):
            rows = aligned(256 * index, 256, 256)
            matrix = whole[3][:, :, :, :, columns].reshape(FF, 384)
            hidden[rows, columns] = hidden[rows, columns] + dot(inner[rows], matrix)

        loop(3, block)

    def last():
        def block(index):
            rows = aligned(128 * index, 128, 128)
            norm_three[rows] = normed(hidden[rows], gains[2:3, :]).astype(BF)

        loop(6, block)
        result = dot(norm_three[...], whole[1][:, D:]).astype(BF)
        doc_out[...] = result[0:512]
        qry_out[...] = result[512:768]
        save(11, hidden)
        save(12, norm_three)

    def clear(pair):
        nothing = jnp.zeros((128, 128), BF)
        for which in range(2):
            prob_doc[pair, 0:128, 512 * which + 384 : 512 * which + 512] = nothing
            prob_doc[pair, 384:512, 512 * which : 512 * which + 128] = nothing

    hidden_copy = None
    for t in range(12):
        gather.step(t)
        later_shards(t)
        if t == 0:
            gather.early_relay()
        if t == 1:
            gather.early_square()
        if 5 <= t < 9:
            gather.early_send_z(t - 5)
        if t == 10:
            gather.early_layers()
        if t == 11:
            gather.early_arrive()
            save_whole(9)
        if t >= 3:
            save_whole(t - 3)
        if t == 1:
            small_arrive()
            first_norm()
        if t == 2:
            loop(6, make_bias)
            make_ids()
        if 3 <= t < 6:
            project(t - 3)
        if t == 3:
            lax.fori_loop(6, 12, lambda head, carry: (make_bias(head), carry)[1], 0)
            loop(6, clear)
        if t == 5:
            attend(0, 2)
        if t == 6:
            attend(2, 5)
        if t == 7:
            attend(5, 6)
            hidden_copy = after_attention()
        if 7 <= t < 11:
            gated(t - 7)
        if t == 10:
            hidden_copy.wait()
        if t == 11:
            descend(1)
            descend(0)
    last()
    gather.finish()
    for k in range(3):
        small_copy(k).wait_send()
    for index, copy in saves:
        if index != 7:
            copy.wait()


def forward(doc, qry, doc_lengths, qry_lengths, small, flats):
    vmem = pl.BlockSpec(memory_space=pltpu.VMEM)
    smem = pl.BlockSpec(memory_space=pltpu.SMEM)
    hbm = pl.BlockSpec(memory_space=pl.ANY)
    dma = pltpu.SemaphoreType.DMA
    whole_rows = [32 * count for count in SHARE_ROWS]
    scratch = [pltpu.VMEM((r, w), BF) for r, w in zip(whole_rows[:3], WIDTHS[:3])]
    scratch += [pltpu.VMEM((4, 2, 4, 96, D), BF)]
    scratch += [pltpu.VMEM((3, r, w), BF) for r, w in zip(SHARE_ROWS[:3], WIDTHS[:3])]
    scratch += [pltpu.VMEM((r, w), BF) for r, w in zip(SHARE_ROWS, WIDTHS)]
    scratch += [
        pltpu.VMEM((576, 128), F32),
        pltpu.VMEM((3, 24, 128), F32),
        pltpu.VMEM((8, D), F32),
        pltpu.VMEM((16, 512), F32),
        pltpu.VMEM((HEADS, 128, NEAR), F32),
        pltpu.VMEM((768, 128), jnp.int32),
        pltpu.VMEM((8, 768), jnp.int32),
        pltpu.VMEM((768, D), BF),
        pltpu.VMEM((768, 3 * D), BF),
        pltpu.VMEM((768, D), BF),
        pltpu.VMEM((768, D), F32),
        pltpu.VMEM((768, D), BF),
        pltpu.VMEM((768, 2 * FF), BF),
        pltpu.VMEM((768, FF), BF),
        pltpu.VMEM((768, D), BF),
        pltpu.VMEM((6, 512, 1024), BF),
        pltpu.VMEM((256, 1536), BF),
        pltpu.VMEM((512, 512), F32),
    ]
    scratch += Gather.scratch()
    scratch += [dma((3,)), dma((3,)), dma((15,)), dma((len(GATHER_STAGES),)), dma((2, 4))]
    return pl.pallas_call(
        forward_kernel,
        out_shape=(
            jax.ShapeDtypeStruct((512, PROJ), BF),
            jax.ShapeDtypeStruct((256, PROJ), BF),
            jax.ShapeDtypeStruct((8, D), F32),
        )
        + tuple(jax.ShapeDtypeStruct(shape, kind) for shape, kind in FORWARD_SAVED),
        in_specs=[vmem, vmem, smem, smem, vmem] + [vmem] * 8,
        out_specs=(vmem, vmem, vmem) + (hbm,) * len(FORWARD_SAVED),
        scratch_shapes=scratch,
        compiler_params=pltpu.CompilerParams(
            collective_id=0, has_side_effects=True, vmem_limit_bytes=VMEM_LIMIT
        ),
        name="forward",
    )(doc, qry, doc_lengths, qry_lengths, small, *flats)


VMEM_LIMIT = 63 * 2**20


def norm_back(values, gain_row, incoming):
    inverse = lax.rsqrt(jnp.mean(values * values, axis=-1, keepdims=True) + EPSILON)
    scaled = gain_row * incoming
    inner = jnp.mean(scaled * values, axis=-1, keepdims=True)
    result = inverse * scaled - values * (inverse * inverse * inverse * inner)
    terms = incoming * values * inverse
    return result, jnp.sum(terms.reshape(-1, 8, D), axis=0)


def diagonal_sums(near):
    wide = jnp.concatenate([near, jnp.zeros((128, 128), F32)], axis=1)
    rows = wide[0:8]
    for group in range(1, 16):
        rows = rows + pltpu.roll(wide[8 * group : 8 * group + 8], 512 - 8 * group, 1)
    lines = lax.broadcasted_iota(jnp.int32, (8, 512), 0)
    for bit in range(3):
        moved = pltpu.roll(rows, 512 - 2**bit, 1)
        rows = jnp.where(lax.rem(lines // 2**bit, 2) == 1, moved, rows)
    return jnp.sum(rows, axis=0, keepdims=True)


def backward_kernel(*refs):
    doc, qry, doc_cotangent, qry_cotangent, gains = refs[0:5]
    saved = refs[5:20]
    doc_grad, qry_grad = refs[20:22]
    flats = refs[22:30]
    small_out = refs[30]
    rest = refs[31:]
    (out_mat, down, gate_up, factors, mixed, residual, hidden, incoming) = rest[0:8]
    (norm_two, norm_three, narrow, context, cotangent) = rest[8:13]
    (gain_terms, diagonal_rows, scores, small, small_in) = rest[13:18]
    scatter_buffers = rest[18:45]
    scatter_sems = rest[45:47]
    small_send, small_recv, load_sem = rest[47:50]

    place = Place()
    small_out[...] = jnp.zeros_like(small_out)
    loads = {}

    def load(name, source, target):
        copy = pltpu.make_async_copy(source, target, load_sem.at[len(loads)])
        copy.start()
        loads[name] = copy

    def ready(*names):
        for name in names:
            loads[name].wait()

    load("residual", saved[11], residual)
    load("out_mat", saved[1], out_mat)
    load("inner", saved[10], mixed)
    load("down", saved[3], down)

    def load_chunk(chunk):
        columns = pl.ds(1536 * chunk, 1536)
        load(("factors", chunk), saved[9].at[:, columns], factors.at[chunk % 2])
        load(("gate_up", chunk), saved[2].at[:, columns], gate_up.at[chunk % 2])

    load_chunk(0)
    load("norm_two", saved[8], norm_two)
    load_chunk(1)
    load("hidden", saved[7], hidden)
    load("context", saved[6], context)
    load("norm_three", saved[12], norm_three)

    place.barrier()

    def settled(s, total):
        array, first, width = SCATTER_STAGES[s]
        if array == 3:
            for tile in range(3):
                line = 3 * s + tile
                flats[6][pl.ds(line, 96, 6), :] = total[:, 128 * tile : 128 * tile + 128]
        elif array == 2:
            for tile in range(12):
                line = 6 * (first // 1536) + tile % 6
                flats[4 + tile // 6][pl.ds(line, 24, 24), :] = total[
                    :, 128 * tile : 128 * tile + 128
                ]
        else:
            for tile in range(6):
                flats[3 if array == 1 else first // D][pl.ds(tile, 24, 6), :] = total[
                    :, 128 * tile : 128 * tile + 128
                ]
            if array == 1:
                flats[7][...] = total[:, D:]

    scatter = Scatter(place, scatter_buffers, settled, scatter_sems)
    gain_terms[...] = jnp.zeros_like(gain_terms)
    diagonal_rows[...] = jnp.zeros_like(diagonal_rows)
    cotangent[0:512] = doc_cotangent[...]
    cotangent[512:768] = qry_cotangent[...]

    def final_norm(index):
        rows = aligned(128 * index, 128, 128)
        grad, terms = norm_back(
            residual[rows], gains[2:3, :], dot(cotangent[rows], out_mat[:, D:], 1, 1)
        )
        residual[rows] = grad
        narrow[rows] = grad.astype(BF)
        gain_terms[2] = gain_terms[2] + terms

    ready("residual", "out_mat")
    loop(6, final_norm)

    ready("inner")
    for half in (1, 0):
        scatter.free(half)
        local = scatter.local(half)

        def piece(index):
            total = dot(
                mixed[:, aligned(D * index, 128, D)],
                narrow[:, 384 * half : 384 * half + 384],
                0,
                0,
            ).astype(BF)
            for core in range(2):
                for other in range(4):
                    first = 384 * core + 96 * other
                    local[index, core, :, 384 * other : 384 * other + 384] = total[
                        first : first + 96
                    ]

        loop(4, piece)
        scatter.step(1 - half, half)
    load("qkv", saved[5], mixed.at[:, pl.ds(0, 3 * D)])
    load("norm_one", saved[4], mixed.at[:, pl.ds(3 * D, D)])

    def put(local, total, first):
        total = total.astype(BF)
        width = total.shape[1]
        for block in range(8):
            local[block // 2, block % 2, :, first : first + width] = total[
                96 * block : 96 * block + 96
            ]

    ready("down", "norm_two")
    for chunk in range(4):
        slot = chunk % 2
        ready(("factors", chunk), ("gate_up", chunk))

        def gated_back(index):
            rows = aligned(256 * index, 256, 256)
            grad = dot(narrow[rows], down[D * chunk : D * chunk + D], 1, 1)
            for side in (0, D):
                factors[slot, rows, side : side + D] = (
                    grad * factors[slot, rows, side : side + D].astype(F32)
                ).astype(BF)

        loop(3, gated_back)
        stage = 2 + chunk
        scatter.free(stage)
        for side in (0, D):
            put(
                scatter.local(stage),
                dot(norm_two[...], factors[slot, :, side : side + D], 0, 0),
                side,
            )
        scatter.step(stage, stage)

        part = dot(factors[slot], gate_up[slot], 1, 1)
        incoming[...] = part if chunk == 0 else incoming[...] + part
        if chunk < 2:
            load_chunk(chunk + 2)
        if chunk == 2:
            load(("share", 0), saved[13].at[0], factors.at[0, pl.ds(0, 512), pl.ds(0, 1024)])
            load("share_qry", saved[14], gate_up.at[0, pl.ds(0, 256)])
    load(("share", 1), saved[13].at[1], factors.at[1, pl.ds(0, 512), pl.ds(0, 1024)])
    for index in range(3):
        load(
            ("qkv_mat", index),
            saved[0].at[:, pl.ds(D * index, D)],
            down.at[pl.ds(D * index, D)],
        )
    load("doc", doc, down.at[pl.ds(3 * D, 512)])
    load("qry", qry, down.at[pl.ds(3 * D + 512, 256)])

    def middle_norm(index):
        rows = aligned(128 * index, 128, 128)
        grad, terms = norm_back(hidden[rows], gains[1:2, :], incoming[rows])
        grad = grad + residual[rows]
        residual[rows] = grad
        narrow[rows] = grad.astype(BF)
        gain_terms[1] = gain_terms[1] + terms

    ready("hidden")
    loop(6, middle_norm)
    ready("context", "norm_three")
    scatter.free(6)
    put(scatter.local(6), dot(context[...], narrow[...], 0, 0), 0)
    put(scatter.local(6), dot(norm_three[...], cotangent[...], 0, 0), D)
    scatter.step(6, 6)
    grad_context = norm_three
    grad_context[...] = dot(narrow[...], out_mat[:, 0:D], 1, 1).astype(BF)

    nothing = jnp.zeros((128, 128), BF)
    grad_scores = gate_up.at[1]
    for which in range(2):
        grad_scores[0:128, 512 * which + 384 : 512 * which + 512] = nothing
        grad_scores[384:512, 512 * which : 512 * which + 128] = nothing

    def two(values):
        return jnp.concatenate([keep(values, 0), keep(values, 1)], axis=0)

    def attention_back(pair, share):
        columns = [aligned(D * index + 128 * pair, 128, 128) for index in range(3)]
        rows = slice(0, 512)
        query, key, value = (mixed[rows, column] for column in columns)
        grad = grad_context[rows, columns[0]]
        near_sums, far_sums = [], []
        for which in range(2):
            scores[...] = dot(keep(grad, which), value, 1, 1)
            near = [None, None, None]
            far = [None, None]
            for block in range(4):
                low, high = window(block)
                rows_here = slice(128 * block, 128 * block + 128)
                reach = slice(512 * which + 128 * low, 512 * which + 128 * high + 128)
                part = share[rows_here, reach].astype(F32)
                grad_share = scores[rows_here, 128 * low : 128 * high + 128]
                weighted = jnp.sum(part * grad_share, axis=-1, keepdims=True)
                result = (part * (grad_share - weighted)).astype(BF)
                grad_scores[rows_here, reach] = result
                result = result.astype(F32)
                for other in range(low, high + 1):
                    tile = result[:, 128 * (other - low) : 128 * (other - low) + 128]
                    place_at = other - block
                    if abs(place_at) == 2:
                        side = 0 if place_at < 0 else 1
                        far[side] = tile if far[side] is None else far[side] + tile
                    else:
                        side = place_at + 1
                        near[side] = tile if near[side] is None else near[side] + tile
            near_sums.append(near)
            far_sums.append(far)
        grad_query = dot(grad_scores[0:512, 0:1024], two(key))
        grad_key = dot(grad_scores[0:512, 0:512], keep(query, 0), 0, 0) + dot(
            grad_scores[0:512, 512:1024], keep(query, 1), 0, 0
        )
        grad_value = dot(share[0:512, 0:512], keep(grad, 0), 0, 0) + dot(
            share[0:512, 512:1024], keep(grad, 1), 0, 0
        )
        mixed[rows, columns[0]] = grad_query.astype(BF)
        mixed[rows, columns[1]] = grad_key.astype(BF)
        mixed[rows, columns[2]] = grad_value.astype(BF)
        for block in range(2):
            rows = slice(512 + 128 * block, 640 + 128 * block)
            query, key, value = (mixed[rows, column] for column in columns)
            grad = grad_context[rows, columns[0]]
            small_share = gate_up[
                0, 128 * block : 128 * block + 128, aligned(256 * pair, 128, 256)
            ]
            results = []
            grad_key = jnp.zeros((128, 128), F32)
            grad_value = jnp.zeros((128, 128), F32)
            for which in range(2):
                part = small_share[:, 128 * which : 128 * which + 128]
                grad_share = dot(keep(grad, which), value, 1, 1)
                wide = part.astype(F32)
                weighted = jnp.sum(wide * grad_share, axis=-1, keepdims=True)
                result = (wide * (grad_share - weighted)).astype(BF)
                near_sums[which][1] = near_sums[which][1] + result.astype(F32)
                results.append(result)
                grad_key = grad_key + dot(result, keep(query, which), 0, 0)
                grad_value = grad_value + dot(part, keep(grad, which), 0, 0)
            grad_query = dot(jnp.concatenate(results, axis=1), two(key))
            mixed[rows, columns[0]] = grad_query.astype(BF)
            mixed[rows, columns[1]] = grad_key.astype(BF)
            mixed[rows, columns[2]] = grad_value.astype(BF)
        lane = lax.broadcasted_iota(jnp.int32, (1, 512), 1)
        for which in range(2):
            row = diagonal_sums(jnp.concatenate(near_sums[which], axis=1))
            for side, column in ((0, 28), (1, 228)):
                total = jnp.sum(far_sums[which][side], axis=(0, 1), keepdims=True)
                row = row + jnp.where(lane == column, total, 0.0)
            diagonal_rows[pl.ds(2 * pair + which, 1), :] = row

    ready("qkv", "norm_one", "share_qry")
    turn = 7
    for pair in range(6):
        slot = pair % 2
        ready(("share", pair))
        attention_back(pair, factors.at[slot])
        if pair < 4:
            load(
                ("share", pair + 2),
                saved[13].at[pair + 2],
                factors.at[slot, pl.ds(0, 512), pl.ds(0, 1024)],
            )
        if pair in (1, 3):
            scatter.step(turn)
            turn = turn + 1

    for index in range(3):
        stage = 7 + index
        scatter.free(stage)
        put(
            scatter.local(stage),
            dot(mixed[:, 3 * D :], mixed[:, D * index : D * index + D], 0, 0),
            0,
        )
        scatter.step(turn, stage)
        turn = turn + 1

    ready(("qkv_mat", 0), ("qkv_mat", 1), ("qkv_mat", 2), "doc", "qry")

    for index in range(3):
        part = dot(mixed[:, D * index : D * index + D], down[D * index : D * index + D], 1, 1)
        incoming[...] = part if index == 0 else incoming[...] + part
    scatter.step(turn)
    turn = turn + 1

    def first_norm(index):
        rows = aligned(128 * index, 128, 128)
        part = incoming[rows]
        here = aligned(3 * D + 128 * index, 128, 128)
        grad, terms = norm_back(down[here].astype(F32), gains[0:1, :], part)
        down[here] = (residual[rows] + grad).astype(BF)
        gain_terms[0] = gain_terms[0] + terms

    loop(6, first_norm)
    stores = [
        pltpu.make_async_copy(down.at[pl.ds(3 * D, 512)], doc_grad, load_sem.at[len(loads)]),
        pltpu.make_async_copy(
            down.at[pl.ds(3 * D + 512, 256)], qry_grad, load_sem.at[len(loads) + 1]
        ),
    ]
    for copy in stores:
        copy.start()

    small[0] = jnp.zeros((40, 128), F32)
    for row in range(3):
        total = jnp.sum(gain_terms[row], axis=0, keepdims=True)
        for tile in range(6):
            line = 6 * row + tile
            small[0, line : line + 1, :] = total[:, 128 * tile : 128 * tile + 128]
    column = lax.broadcasted_iota(jnp.int32, (BUCKETS, 512), 1)
    relative = jnp.where(column < 384, column - 128, column - 640)
    marks = marks_of(relative).astype(F32)
    small[0, 24:40, 0:BUCKETS] = lax.dot_general(
        diagonal_rows[...],
        marks,
        (((1,), (1,)), ((), ())),
        precision=lax.Precision.HIGHEST,
        preferred_element_type=F32,
    )

    def small_copy(index):
        device = ([place.to_sib, place.to_x, place.to_y] + place.to_z)[index]
        return remote(
            small.at[min(index, 3)],
            small_in.at[index],
            small_send.at[index],
            small_recv.at[index],
            device,
        )

    small_copy(0).start()
    for index in range(3):
        scatter.step(turn)
        turn = turn + 1
        small_copy(index).wait_recv()
        small[index + 1] = small[index] + small_in[index]
        if index < 2:
            small_copy(index + 1).start()
    for k in range(3):
        small_copy(3 + k).start()
    scatter.step(turn)
    for k in range(3):
        small_copy(3 + k).wait_recv()
    total = jnp.zeros((40, 128), F32)
    for other in range(4):
        piece = small[3]
        for k in range(3):
            here = lax.rem(place.z + 3 - k, 4) == other
            piece = jnp.where(here, small_in[3 + k], piece)
        total = total + piece
    small[4] = total
    first = 9 * place.z // 2
    plain = small[4, pl.ds(first, 5), :]
    turned, later = (
        pltpu.roll(small[4, pl.ds(first + more, 5), :], 64, 1) for more in range(2)
    )
    low = lax.broadcasted_iota(jnp.int32, (5, 128), 1) < 64
    odd = lax.rem(place.z, 2) == 1
    small_out[0:5] = jnp.where(odd, jnp.where(low, turned, later), plain)
    lane = lax.broadcasted_iota(jnp.int32, (BUCKETS, 128), 1)
    bucket = lax.broadcasted_iota(jnp.int32, (BUCKETS, 128), 0)
    chosen = (8 * place.z + lane // HEADS == bucket).astype(F32)
    spread = lax.dot_general(
        total[24:40, 0:BUCKETS],
        chosen,
        (((1,), (0,)), ((), ())),
        precision=lax.Precision.HIGHEST,
        preferred_element_type=F32,
    )
    lane = lax.broadcasted_iota(jnp.int32, (16, 128), 1)
    head = lax.broadcasted_iota(jnp.int32, (16, 128), 0)
    spread = jnp.where(lax.rem(lane, HEADS) == head, spread, 0.0)
    small_out[8:9] = jnp.sum(spread, axis=0, keepdims=True)

    scatter.finish()
    for index in range(6):
        small_copy(index).wait_send()
    for copy in stores:
        copy.wait()


def backward(doc, qry, doc_cotangent, qry_cotangent, gains, saved):
    vmem = pl.BlockSpec(memory_space=pltpu.VMEM)
    hbm = pl.BlockSpec(memory_space=pl.ANY)
    dma = pltpu.SemaphoreType.DMA
    scratch = [
        pltpu.VMEM((768, D + PROJ), BF),
        pltpu.VMEM((FF, D), BF),
        pltpu.VMEM((2, 768, 1536), BF),
        pltpu.VMEM((2, 768, 1536), BF),
        pltpu.VMEM((768, FF), BF),
        pltpu.VMEM((768, D), F32),
        pltpu.VMEM((768, D), F32),
        pltpu.VMEM((768, D), F32),
        pltpu.VMEM((768, D), BF),
        pltpu.VMEM((768, D), BF),
        pltpu.VMEM((768, D), BF),
        pltpu.VMEM((768, D), BF),
        pltpu.VMEM((768, PROJ), BF),
        pltpu.VMEM((3, 8, D), F32),
        pltpu.VMEM((16, 512), F32),
        pltpu.VMEM((512, 512), F32),
        pltpu.VMEM((5, 40, 128), F32),
        pltpu.VMEM((6, 40, 128), F32),
    ]
    scratch += Scatter.scratch() + Scatter.semaphores() + [dma((6,)), dma((6,)), dma((36,))]
    lines = (144, 144, 144, 144, 576, 576, 576, 24)
    return pl.pallas_call(
        backward_kernel,
        out_shape=(
            jax.ShapeDtypeStruct((512, D), BF),
            jax.ShapeDtypeStruct((256, D), BF),
        )
        + tuple(jax.ShapeDtypeStruct((count, 128), F32) for count in lines)
        + (jax.ShapeDtypeStruct((16, 128), F32),),
        in_specs=[hbm, hbm, vmem, vmem, vmem] + [hbm] * len(saved),
        out_specs=(hbm, hbm) + (vmem,) * 9,
        scratch_shapes=scratch,
        compiler_params=pltpu.CompilerParams(
            collective_id=1, has_side_effects=True, vmem_limit_bytes=VMEM_LIMIT
        ),
        name="backward",
    )(doc, qry, doc_cotangent, qry_cotangent, gains, *saved)


def hand_out_kernel(*refs):
    count = len(refs) // 2
    copies = [
        pltpu.make_async_copy(refs[index], refs[count + index], refs[-1].at[index])
        for index in range(count)
    ]
    for copy in copies:
        copy.start()
    for copy in copies:
        copy.wait()


def hand_out(arrays):
    hbm = pl.BlockSpec(memory_space=pl.ANY)
    return pl.pallas_call(
        hand_out_kernel,
        out_shape=tuple(jax.ShapeDtypeStruct(array.shape, array.dtype) for array in arrays),
        in_specs=[pl.BlockSpec(memory_space=pltpu.VMEM)] * len(arrays),
        out_specs=(hbm,) * len(arrays),
        scratch_shapes=[pltpu.SemaphoreType.DMA((len(arrays),))],
        name="hand_out",
    )(*arrays)


def local_fast(
    document_tokens,
    document_lengths,
    query_tokens,
    query_lengths,
    weight_query,
    weight_key,
    weight_value,
    weight_out,
    weight_gate,
    weight_up,
    weight_down,
    weight_proj,
    norm_gains,
    rel_table,
    document_cotangent,
    query_cotangent,
):
    doc = document_tokens.reshape(DOC_LEN, D)
    qry = query_tokens.reshape(-1, D)
    units = norm_gains.astype(jnp.float32).reshape(9, 64)
    units = jnp.pad(jnp.concatenate([units, units], axis=1), ((0, 7), (0, 0)))
    table = jnp.pad(rel_table.astype(jnp.float32).reshape(8, HEADS), ((0, 0), (0, 128 - HEADS)))
    small = jnp.concatenate([units, table], axis=0)
    flats = [
        w.reshape(-1, 128)
        for w in (
            weight_query,
            weight_key,
            weight_value,
            weight_out,
            weight_gate,
            weight_up,
            weight_down,
            weight_proj,
        )
    ]
    results = forward(doc, qry, document_lengths, query_lengths.reshape(1, 8), small, flats)
    doc_out, qry_out, gains = results[0:3]
    grads = backward(
        doc,
        qry,
        document_cotangent.reshape(DOC_LEN, PROJ),
        query_cotangent.reshape(-1, PROJ),
        gains,
        results[3:6] + (results[6].reshape(FF, D),) + results[7:],
    )
    small = grads[10]
    results = hand_out((doc_out, qry_out) + tuple(grads[0:10]))
    return (
        results[0].reshape(document_cotangent.shape),
        results[1].reshape(query_cotangent.shape),
        results[2].reshape(document_tokens.shape),
        results[3].reshape(query_tokens.shape),
        *[grad.reshape(-1) for grad in results[4:12]],
        small[0:5].reshape(-1)[0:576],
        small[8, 0:96],
    )


def solution(mesh):
    placed = (
        P(("dp", "fsdp"), None, None),
        P(("dp", "fsdp"), None),
        P(("dp", "fsdp"), None, None),
        P(("dp", "fsdp")),
        P(("dp", "fsdp")),
        P(("dp", "fsdp")),
        P(("dp", "fsdp")),
        P(("dp", "fsdp")),
        P(("dp", "fsdp")),
        P(("dp", "fsdp")),
        P(("dp", "fsdp")),
        P(("dp", "fsdp")),
        P("fsdp"),
        P("fsdp"),
        P(("dp", "fsdp"), None, None),
        P(("dp", "fsdp"), None, None),
    )
    return jax.shard_map(
        local_fast if (mesh.shape["dp"], mesh.shape["fsdp"]) == (8, 4) else local,
        mesh=mesh,
        in_specs=placed,
        out_specs=(
            P(("dp", "fsdp"), None, None),
            P(("dp", "fsdp"), None, None),
            P(("dp", "fsdp"), None, None),
            P(("dp", "fsdp"), None, None),
            P(("dp", "fsdp")),
            P(("dp", "fsdp")),
            P(("dp", "fsdp")),
            P(("dp", "fsdp")),
            P(("dp", "fsdp")),
            P(("dp", "fsdp")),
            P(("dp", "fsdp")),
            P(("dp", "fsdp")),
            P("fsdp"),
            P("fsdp"),
        ),
        check_vma=False,
    )
```

```python
import jax
import jax.numpy as jnp
from jax import lax
from jax.experimental import pallas as pl
from jax.experimental.pallas import tpu as pltpu
from jax.sharding import PartitionSpec as P

D = 768
HEADS = 12
HEAD_DIM = 64
FF = 3072
BUCKETS = 32
PROJ = 128
DOC_LEN = 512
QRY_LEN = 32


EPSILON = 1e-06
NEGATIVE = -1e30


def rms_norm(values, gain_row):
    inverse = lax.rsqrt(jnp.mean(values * values, axis=-1, keepdims=True) + EPSILON)
    return values * inverse * gain_row


def gated_unit(gate_in, upper_in):
    return jax.nn.gelu(gate_in, approximate=True) * upper_in


def bucket_ids(length):
    positions = jnp.arange(length, dtype=jnp.int32)
    relative = positions[None, :] - positions[:, None]
    distance = jnp.abs(relative)
    distant = 8 + sum(
        ((distance * distance >= 64 * 2**power).astype(jnp.int32) for power in range(1, 8))
    )
    nearby = jnp.where(distance < 8, distance, distant)
    return nearby + 16 * (relative > 0).astype(jnp.int32)


def bucket_onehot(length):
    flat_ids = bucket_ids(length).reshape(1, length * length)
    labels = jnp.arange(BUCKETS, dtype=jnp.int32).reshape(BUCKETS, 1)
    return (flat_ids == labels).astype(jnp.bfloat16)


def segment_ids(lengths, length):
    boundary = jnp.cumsum(lengths, axis=-1)
    positions = jnp.arange(length, dtype=jnp.int32)
    return jnp.sum((positions[None, :, None] >= boundary[:, None, :]).astype(jnp.int32), axis=-1)


def outer_sum(left_rows, right_rows):
    return lax.dot_general(
        left_rows, right_rows, (((0,), (0,)), ((), ())), preferred_element_type=jnp.float32
    )


def times_transposed(left_rows, matrix):
    return lax.dot_general(
        left_rows, matrix, (((1,), (1,)), ((), ())), preferred_element_type=jnp.float32
    )


def flat_piece(left_rows, right_rows, start, count):
    width = right_rows.shape[1]
    needed = count // width + 2
    padded = jnp.pad(left_rows, ((0, 0), (0, needed)))
    first_row = start // width
    columns = lax.dynamic_slice_in_dim(padded, first_row, needed, 1)
    block = outer_sum(columns, right_rows).reshape(-1)
    return lax.dynamic_slice_in_dim(block, start, count)


def grad_terms(pairs, devices):
    shares = [pair[0].shape[1] * pair[1].shape[1] // devices for pair in pairs]
    total_share = sum(shares)

    def term(start, count):
        blocks = count // total_share
        first_block = start // total_share
        pieces = [
            flat_piece(pair[0], pair[1], first_block * share, blocks * share).reshape(blocks, share)
            for pair, share in zip(pairs, shares)
        ]
        return jnp.concatenate(pieces, axis=1).reshape(-1)

    return (term, total_share, shares)


def split_shares(mine, shares):
    results = []
    offset = 0
    for share in shares:
        results.append(mine[offset : offset + share])
        offset = offset + share
    return results


def bias_rows(table_mat, onehot, length):
    rel_bias = lax.dot_general(
        table_mat, onehot, (((0,), (0,)), ((), ())), preferred_element_type=jnp.float32
    )
    return rel_bias.reshape(1, HEADS, length, length)


def masked_scores(queries, key_rows, rel_bias, allowed):
    scores = (
        jnp.einsum("bqhd,bkhd->bhqk", queries, key_rows, preferred_element_type=jnp.float32)
        + rel_bias
    )
    return jnp.where(allowed, scores, NEGATIVE)


def attend(queries, key_rows, values, rel_bias, allowed):
    scores = masked_scores(queries, key_rows, rel_bias, allowed)
    largest = jnp.max(scores, axis=-1, keepdims=True)
    summed = jnp.sum(jnp.exp(scores - largest), axis=-1, keepdims=True)
    log_total = largest + jnp.log(summed)
    attention = jnp.exp(scores - log_total).astype(jnp.bfloat16)
    context = jnp.einsum("bhqk,bkhd->bqhd", attention, values, preferred_element_type=jnp.float32)
    return (context.astype(jnp.bfloat16), log_total)


def attend_back(queries, key_rows, values, rel_bias, allowed, log_total, grad_context):
    scores = masked_scores(queries, key_rows, rel_bias, allowed)
    attention = jnp.exp(scores - log_total)
    grad_attention = jnp.einsum(
        "bqhd,bkhd->bhqk", grad_context, values, preferred_element_type=jnp.float32
    )
    grad_values = jnp.einsum(
        "bhqk,bqhd->bkhd",
        attention.astype(jnp.bfloat16),
        grad_context,
        preferred_element_type=jnp.float32,
    )
    weighted = jnp.sum(attention * grad_attention, axis=-1, keepdims=True)
    grad_scores = (attention * (grad_attention - weighted)).astype(jnp.bfloat16)
    grad_queries = jnp.einsum(
        "bhqk,bkhd->bqhd", grad_scores, key_rows, preferred_element_type=jnp.float32
    )
    grad_keys = jnp.einsum(
        "bhqk,bqhd->bkhd", grad_scores, queries, preferred_element_type=jnp.float32
    )
    return (
        grad_queries.astype(jnp.bfloat16),
        grad_keys.astype(jnp.bfloat16),
        grad_values.astype(jnp.bfloat16),
        grad_scores,
    )


def bias_grads(grad_scores, onehot):
    members = grad_scores.shape[0]
    flattened = grad_scores.reshape(members * HEADS, -1)
    summed = lax.dot_general(
        flattened, onehot, (((1,), (1,)), ((), ())), preferred_element_type=jnp.float32
    )
    return jnp.sum(summed.reshape(members, HEADS, BUCKETS), axis=0)


def local(
    document_tokens,
    document_lengths,
    query_tokens,
    query_lengths,
    weight_query,
    weight_key,
    weight_value,
    weight_out,
    weight_gate,
    weight_up,
    weight_down,
    weight_proj,
    norm_gains,
    rel_table,
    document_cotangent,
    query_cotangent,
):
    layouts = ((D, D), (D, D), (D, D), (D, D), (D, FF), (D, FF), (FF, D), (D, PROJ))
    devices = lax.axis_size("dp") * lax.axis_size("fsdp")
    gathered = (
        lax.all_gather(weight_query, ("dp", "fsdp"), axis=0, tiled=True),
        lax.all_gather(weight_key, ("dp", "fsdp"), axis=0, tiled=True),
        lax.all_gather(weight_value, ("dp", "fsdp"), axis=0, tiled=True),
        lax.all_gather(weight_out, ("dp", "fsdp"), axis=0, tiled=True),
        lax.all_gather(weight_gate, ("dp", "fsdp"), axis=0, tiled=True),
        lax.all_gather(weight_up, ("dp", "fsdp"), axis=0, tiled=True),
        lax.all_gather(weight_down, ("dp", "fsdp"), axis=0, tiled=True),
        lax.all_gather(weight_proj, ("dp", "fsdp"), axis=0, tiled=True),
    )
    matrices = [flat_rows.reshape(layout) for flat_rows, layout in zip(gathered, layouts)]
    gains_all, table_all = (
        lax.all_gather(norm_gains, "fsdp", axis=0, tiled=True),
        lax.all_gather(rel_table, "fsdp", axis=0, tiled=True),
    )
    gain_rows = gains_all.astype(jnp.float32).reshape(3, D)
    table_mat = table_all.reshape(BUCKETS, HEADS)
    documents = document_tokens.shape[0]
    queries_here = query_tokens.shape[0]
    doc_rows = documents * DOC_LEN
    doc_segments = segment_ids(document_lengths, DOC_LEN)
    query_segments = segment_ids(query_lengths.reshape(queries_here, 1), QRY_LEN)
    doc_allowed = doc_segments[:, None, :, None] == doc_segments[:, None, None, :]
    query_allowed = query_segments[:, None, :, None] == query_segments[:, None, None, :]
    doc_onehot = bucket_onehot(DOC_LEN)
    query_onehot = bucket_onehot(QRY_LEN)
    doc_bias = bias_rows(table_mat, doc_onehot, DOC_LEN)
    query_bias = bias_rows(table_mat, query_onehot, QRY_LEN)
    settings = [(doc_bias, doc_allowed, doc_onehot)]
    settings.append((query_bias, query_allowed, query_onehot))

    def split_blocks(matrix):
        blocks_out = [matrix[0:DOC_LEN].reshape(1, DOC_LEN, HEADS, HEAD_DIM)]
        blocks_out.append(matrix[doc_rows:].reshape(queries_here, QRY_LEN, HEADS, HEAD_DIM))
        return blocks_out

    query_mat, key_mat, value_mat, out_mat, gate_mat, up_mat, down_mat, proj_mat = matrices
    inputs = jnp.concatenate(
        [document_tokens.reshape(doc_rows, D), query_tokens.reshape(-1, D)], axis=0
    )
    residual_in = inputs.astype(jnp.float32)
    normed_one, norm_one_back = jax.vjp(rms_norm, residual_in, gain_rows[0])
    normed_one = normed_one.astype(jnp.bfloat16)
    queries = jnp.dot(normed_one, query_mat, preferred_element_type=jnp.float32).astype(
        jnp.bfloat16
    )
    key_rows = jnp.dot(normed_one, key_mat, preferred_element_type=jnp.float32).astype(jnp.bfloat16)
    values = jnp.dot(normed_one, value_mat, preferred_element_type=jnp.float32).astype(jnp.bfloat16)
    query_blocks = split_blocks(queries)
    key_blocks = split_blocks(key_rows)
    value_blocks = split_blocks(values)
    contexts = []
    log_totals = []
    for query_block, key_block, value_block, setting in zip(
        query_blocks, key_blocks, value_blocks, settings
    ):
        context_block, log_total = attend(
            query_block, key_block, value_block, setting[0], setting[1]
        )
        contexts.append(context_block.reshape(-1, D))
        log_totals.append(log_total)
    context = jnp.concatenate(contexts, axis=0)
    hidden = residual_in + jnp.dot(context, out_mat, preferred_element_type=jnp.float32)
    normed_two, norm_two_back = jax.vjp(rms_norm, hidden, gain_rows[1])
    normed_two = normed_two.astype(jnp.bfloat16)
    gate = jnp.dot(normed_two, gate_mat, preferred_element_type=jnp.float32)
    upper = jnp.dot(normed_two, up_mat, preferred_element_type=jnp.float32)
    inner, gated_back = jax.vjp(gated_unit, gate, upper)
    inner = inner.astype(jnp.bfloat16)
    final = hidden + jnp.dot(inner, down_mat, preferred_element_type=jnp.float32)
    normed_three, norm_three_back = jax.vjp(rms_norm, final, gain_rows[2])
    normed_three = normed_three.astype(jnp.bfloat16)
    output = jnp.dot(normed_three, proj_mat, preferred_element_type=jnp.float32).astype(
        jnp.bfloat16
    )
    again = (
        lax.all_gather(weight_query, ("dp", "fsdp"), axis=0, tiled=True),
        lax.all_gather(weight_key, ("dp", "fsdp"), axis=0, tiled=True),
        lax.all_gather(weight_value, ("dp", "fsdp"), axis=0, tiled=True),
        lax.all_gather(weight_out, ("dp", "fsdp"), axis=0, tiled=True),
        lax.all_gather(weight_gate, ("dp", "fsdp"), axis=0, tiled=True),
        lax.all_gather(weight_up, ("dp", "fsdp"), axis=0, tiled=True),
        lax.all_gather(weight_down, ("dp", "fsdp"), axis=0, tiled=True),
        lax.all_gather(weight_proj, ("dp", "fsdp"), axis=0, tiled=True),
    )
    back_mats = [flat_rows.reshape(layout) for flat_rows, layout in zip(again, layouts)]
    back_query, back_key, back_value, back_out, back_gate, back_up, back_down, back_proj = back_mats
    cotangent = jnp.concatenate(
        [document_cotangent.reshape(doc_rows, PROJ), query_cotangent.reshape(-1, PROJ)], axis=0
    )
    grad_final, grad_gain_three = norm_three_back(times_transposed(cotangent, back_proj))
    grad_ffn = grad_final.astype(jnp.bfloat16)
    grad_gate_f, grad_upper_f = gated_back(times_transposed(grad_ffn, back_down))
    grad_gate_b = grad_gate_f.astype(jnp.bfloat16)
    grad_upper_b = grad_upper_f.astype(jnp.bfloat16)
    grad_normed_two = times_transposed(grad_gate_b, back_gate) + times_transposed(
        grad_upper_b, back_up
    )
    grad_hidden_part, grad_gain_two = norm_two_back(grad_normed_two)
    grad_hidden = grad_final + grad_hidden_part
    ffn_pairs = [
        (normed_two, grad_gate_b),
        (normed_two, grad_upper_b),
        (inner, grad_ffn),
        (normed_three, cotangent),
    ]
    grad_branch = grad_hidden.astype(jnp.bfloat16)
    grad_context = times_transposed(grad_branch, back_out).astype(jnp.bfloat16)
    table_grad = jnp.zeros((HEADS, BUCKETS), jnp.float32)
    grad_query_parts = []
    grad_key_parts = []
    grad_value_parts = []
    for query_block, key_block, value_block, setting, log_total, grad_block in zip(
        query_blocks, key_blocks, value_blocks, settings, log_totals, split_blocks(grad_context)
    ):
        grad_q_block, grad_k_block, grad_v_block, grad_scores = attend_back(
            query_block, key_block, value_block, setting[0], setting[1], log_total, grad_block
        )
        table_grad = table_grad + bias_grads(grad_scores, setting[2])
        grad_query_parts.append(grad_q_block.reshape(-1, D))
        grad_key_parts.append(grad_k_block.reshape(-1, D))
        grad_value_parts.append(grad_v_block.reshape(-1, D))
    grad_queries = jnp.concatenate(grad_query_parts, axis=0)
    grad_keys = jnp.concatenate(grad_key_parts, axis=0)
    grad_values = jnp.concatenate(grad_value_parts, axis=0)
    grad_normed_one = (
        times_transposed(grad_queries, back_query)
        + times_transposed(grad_keys, back_key)
        + times_transposed(grad_values, back_value)
    )
    grad_input_part, grad_gain_one = norm_one_back(grad_normed_one)
    grad_inputs = (grad_hidden + grad_input_part).astype(jnp.bfloat16)
    attn_pairs = [
        (normed_one, grad_queries),
        (normed_one, grad_keys),
        (normed_one, grad_values),
        (context, grad_branch),
    ]
    all_term, all_total, all_shares = grad_terms(attn_pairs + ffn_pairs, devices)
    shares = tuple(
        split_shares(
            lax.psum_scatter(
                all_term(jnp.int32(0), lax.axis_size(("dp", "fsdp")) * all_total),
                ("dp", "fsdp"),
                scatter_dimension=0,
                tiled=True,
            ),
            all_shares,
        )
    )
    gain_grads = jnp.concatenate([grad_gain_one, grad_gain_two, grad_gain_three], axis=0)
    table_flat = jnp.transpose(table_grad).reshape(-1)
    gain_whole, table_whole = lax.psum((gain_grads, table_flat), ("dp", "fsdp"))
    fsdp_index = lax.axis_index("fsdp")
    fsdp_count = lax.axis_size("fsdp")
    gain_share = 3 * D // fsdp_count
    table_share = BUCKETS * HEADS // fsdp_count
    own_gains = lax.dynamic_slice_in_dim(gain_whole, fsdp_index * gain_share, gain_share)
    own_table = lax.dynamic_slice_in_dim(table_whole, fsdp_index * table_share, table_share)
    return (
        output[:doc_rows].reshape(documents, DOC_LEN, PROJ),
        output[doc_rows:].reshape(queries_here, QRY_LEN, PROJ),
        grad_inputs[:doc_rows].reshape(documents, DOC_LEN, D),
        grad_inputs[doc_rows:].reshape(queries_here, QRY_LEN, D),
        shares[0],
        shares[1],
        shares[2],
        shares[3],
        shares[4],
        shares[5],
        shares[6],
        shares[7],
        own_gains,
        own_table,
    )


WIDTHS = (3 * D, D + PROJ, 2 * FF, D)
SHARE_ROWS = (24, 24, 24, 96)
GATHER_STAGES = (
    (0, 0, 768),
    (0, 768, 768),
    (0, 1536, 768),
    (1, 0, 896),
    (2, 0, 1536),
    (2, 1536, 1536),
    (2, 3072, 1536),
    (2, 4608, 1536),
    (3, 0, 384),
    (3, 384, 384),
)
MESH_ID = pl.DeviceIdType.MESH


def remote(source, target, send_sem, recv_sem, device):
    return pltpu.make_async_remote_copy(
        src_ref=source,
        dst_ref=target,
        send_sem=send_sem,
        recv_sem=recv_sem,
        device_id=device,
        device_id_type=MESH_ID,
    )


class Place:
    def __init__(self):
        self.dp = lax.axis_index("dp")
        self.z = lax.axis_index("fsdp")
        self.core = lax.rem(self.dp, 2)
        self.xy = self.dp // 2
        self.xy_x = self.xy + 1 - 2 * lax.rem(self.xy, 2)
        self.xy_y = lax.rem(self.xy + 2, 4)
        self.xy_d = 3 - self.xy
        self.sib = self.dp + 1 - 2 * self.core
        self.dp_x = 2 * self.xy_x + self.core
        self.dp_y = 2 * self.xy_y + self.core
        self.dp_d = 2 * self.xy_d + self.core
        self.zs = [lax.rem(self.z + step, 4) for step in (1, 2, 3)]
        self.to_sib = {"dp": self.sib}
        self.to_x = {"dp": self.dp_x}
        self.to_y = {"dp": self.dp_y}
        self.to_z = [{"fsdp": other} for other in self.zs]

    def barrier(self):
        semaphore = pltpu.get_barrier_semaphore()
        for device in [self.to_sib, self.to_x, self.to_y] + self.to_z:
            pl.semaphore_signal(semaphore, inc=1, device_id=device, device_id_type=MESH_ID)
        pl.semaphore_wait(semaphore, 6)


class Gather:
    def __init__(self, place, shards, whole, parts, sems):
        self.place, self.shards, self.whole, self.parts = place, shards, whole, parts
        (self.z_send, self.z_recv, self.send, self.recv, self.early_send, self.early_recv) = sems
        self.stages = GATHER_STAGES
        self.early = len(GATHER_STAGES) - 1

    @staticmethod
    def scratch():
        count = len(GATHER_STAGES)
        dma = pltpu.SemaphoreType.DMA
        return [dma((count, 3)), dma((count, 3)), dma((count, 9)), dma((count, 9)), dma((4, 3)), dma((4, 3))]

    def z_copy(self, s, k):
        array, first, width = self.stages[s]
        place = self.place
        columns = pl.ds(first, width)
        if array == 3:
            target = self.whole[3].at[place.xy, place.core, place.z, :, columns]
        else:
            target = self.parts[array].at[k, :, columns]
        return remote(
            self.shards[array].at[:, columns],
            target,
            self.z_send.at[s, k],
            self.z_recv.at[s, k],
            place.to_z[k],
        )

    def block(self, s, dp, half=None):
        array, first, width = self.stages[s]
        columns = pl.ds(first, width)
        if s == self.early:
            rows = pl.ds(0, 96) if half is None else pl.ds(48 * half, 48)
            return self.whole[3].at[dp // 2, self.place.core, self.place.z, rows, columns]
        if array == 3:
            layers = pl.ds(0, 4) if half is None else pl.ds(2 * half, 2)
            return self.whole[3].at[dp // 2, self.place.core, layers, :, columns]
        start, count = (96 * dp, 96) if half is None else (96 * dp + 48 * half, 48)
        return self.whole[array].at[pl.ds(pl.multiple_of(start, 48), count), columns]

    def hop(self, s, index):
        place = self.place
        dp, half, device = (
            (place.dp, None, place.to_x),
            (place.dp, None, place.to_y),
            (place.dp_x, 0, place.to_y),
            (place.dp_y, 1, place.to_x),
            (place.dp, None, place.to_sib),
            (place.dp_x, None, place.to_sib),
            (place.dp_y, None, place.to_sib),
            (place.dp_d, 0, place.to_sib),
            (place.dp_d, 1, place.to_sib),
        )[index]
        block = self.block(s, dp, half)
        return remote(block, block, self.send.at[s, index], self.recv.at[s, index], device)

    def begin(self, s):
        for k in range(3):
            self.z_copy(s, k).start()

    def spread(self, s):
        array, first, width = self.stages[s]
        place = self.place
        columns = pl.ds(first, width)
        for k in range(3):
            self.z_copy(s, k).wait_recv()
        if array == 3:
            self.whole[3][place.xy, place.core, place.z, :, columns] = self.shards[3][:, columns]
        else:
            pieces = []
            for other in range(4):
                piece = self.shards[array][:, columns]
                for k in range(3):
                    here = lax.rem(place.z + 3 - k, 4) == other
                    piece = jnp.where(here, self.parts[array][k, :, columns], piece)
                pieces.append(piece)
            rows = pl.ds(pl.multiple_of(96 * place.dp, 96), 96)
            self.whole[array][rows, columns] = jnp.concatenate(pieces, axis=0)
        for index in (0, 1, 4):
            self.hop(s, index).start()

    def relay(self, s):
        self.hop(s, 0).wait_recv()
        self.hop(s, 2).start()
        self.hop(s, 5).start()
        self.hop(s, 1).wait_recv()
        self.hop(s, 3).start()
        self.hop(s, 6).start()

    def hand_over(self, s):
        self.hop(s, 2).wait_recv()
        self.hop(s, 7).start()
        self.hop(s, 3).wait_recv()
        self.hop(s, 8).start()

    def arrive(self, s):
        for index in range(4, 9):
            self.hop(s, index).wait_recv()

    def step(self, t):
        for lag, work in enumerate((self.spread, self.relay, self.hand_over, self.arrive)):
            if 0 <= t - lag < self.early:
                work(t - lag)

    def early_layer(self, index):
        place = self.place
        array, first, width = self.stages[self.early]
        z = place.z if index == 0 else lax.rem(place.z + 4 - index, 4)
        block = self.whole[3].at[:, place.core, z, :, pl.ds(first, width)]
        return remote(
            block,
            block,
            self.send.at[self.early, 4 + index],
            self.recv.at[self.early, 4 + index],
            place.to_sib,
        )

    def early_z(self, piece, k):
        place = self.place
        array, first, width = self.stages[self.early]
        xy = (place.xy, place.xy_x, place.xy_y, place.xy_d)[piece]
        block = self.whole[3].at[xy, place.core, place.z, :, pl.ds(first, width)]
        return remote(
            block, block, self.early_send.at[piece, k], self.early_recv.at[piece, k], place.to_z[k]
        )

    def early_begin(self):
        place = self.place
        array, first, width = self.stages[self.early]
        columns = pl.ds(first, width)
        self.whole[3][place.xy, place.core, place.z, :, columns] = self.shards[3][:, columns]
        self.hop(self.early, 0).start()
        self.hop(self.early, 1).start()

    def early_relay(self):
        self.hop(self.early, 0).wait_recv()
        self.hop(self.early, 2).start()
        self.hop(self.early, 1).wait_recv()
        self.hop(self.early, 3).start()

    def early_square(self):
        self.hop(self.early, 2).wait_recv()
        self.hop(self.early, 3).wait_recv()
        self.early_layer(0).start()

    def early_send_z(self, piece):
        for k in range(3):
            self.early_z(piece, k).start()

    def early_layers(self):
        for k in range(3):
            for piece in range(4):
                self.early_z(piece, k).wait_recv()
            self.early_layer(k + 1).start()

    def early_arrive(self):
        for index in range(4):
            self.early_layer(index).wait_recv()

    def finish(self):
        for s in range(self.early):
            for k in range(3):
                self.z_copy(s, k).wait_send()
            for index in range(9):
                self.hop(s, index).wait_send()
        for index in range(4):
            self.hop(self.early, index).wait_send()
            self.early_layer(index).wait_send()
            for k in range(3):
                self.early_z(index, k).wait_send()


SCATTER_WIDTHS = (3 * D, D + PROJ, 2 * FF, 1920)
SCATTER_STAGES = (
    (3, 0, 1536),
    (3, 384, 1536),
    (2, 0, 1536),
    (2, 1536, 1536),
    (2, 3072, 1536),
    (2, 4608, 1536),
    (1, 0, 896),
    (0, 0, 1152),
    (0, 1152, 1152),
)
SCATTER_LAGS = ((0, 1, 6, 8, 10),) + ((0, 1, 2, 4, 6),) * 6 + ((0, 1, 2, 3, 4),) * 2
SCATTER_ORDER = (1, 0, 2, 3, 4, 5, 6, 7, 8)
SCATTER_HELD = (
    (0, 0),
    (1, 0),
    (2, 0),
    (3, 0),
    (4, 0),
    (5, 0),
    (6, 0),
    (7, 0),
    (8, 0),
)


class Scatter:
    def __init__(self, place, buffers, settled, sems):
        self.place, self.settled = place, settled
        self.local_all, self.held_all = buffers[0:2]
        self.from_x, self.from_y = buffers[2:6], buffers[6:10]
        self.diag_x, self.diag_y = buffers[10:14], buffers[14:18]
        self.z_out, self.z_in = buffers[18:22], buffers[22:26]
        self.early, self.early_in = self.held_all.at[0], buffers[26]
        self.send, self.recv = sems
        self.begun = {}

    @staticmethod
    def scratch():
        kind = jnp.bfloat16
        shapes = [pltpu.VMEM((2, 4, 2, 96, 1536), kind), pltpu.VMEM((9, 4, 96, 1536), kind)]
        shapes += [pltpu.VMEM((96, w), kind) for w in SCATTER_WIDTHS] * 2
        shapes += [pltpu.VMEM((48, w), kind) for w in SCATTER_WIDTHS] * 2
        pieces = [(24, w) for w in SCATTER_WIDTHS[:3]] + [(96, 384)]
        shapes += [pltpu.VMEM((4, r, w), kind) for r, w in pieces]
        shapes += [pltpu.VMEM((3, r, w), kind) for r, w in pieces]
        shapes += [pltpu.VMEM((3, 4, 96, 384), kind)]
        return shapes

    @staticmethod
    def semaphores():
        count = len(SCATTER_STAGES)
        dma = pltpu.SemaphoreType.DMA
        return [dma((count, 8)), dma((count, 8))]

    def local(self, s):
        slot = SCATTER_ORDER.index(s) % 2
        return self.local_all.at[slot, :, :, :, pl.ds(0, SCATTER_STAGES[s][2])]

    def held(self, s):
        slot, first = SCATTER_HELD[s]
        return self.held_all.at[slot, :, :, pl.ds(first, SCATTER_STAGES[s][2])]

    def columns(self, s):
        return pl.ds(SCATTER_STAGES[s][1], SCATTER_STAGES[s][2])

    def z_columns(self, s):
        array, first, width = SCATTER_STAGES[s]
        return pl.ds(0, 384) if array == 3 else pl.ds(first, width)

    def early_columns(self, z):
        return pl.ds(pl.multiple_of(384 * z, 128), 384)

    def early_copy(self, index):
        place = self.place
        mine = self.early_columns(place.z)
        column = pl.ds(0, 384)
        if index == 1:
            source = self.early.at[place.xy_d, pl.ds(0, 48), mine]
            target, device = self.diag_x[3].at[:, column], place.to_x
        elif index == 2:
            source = self.early.at[place.xy_d, pl.ds(48, 48), mine]
            target, device = self.diag_y[3].at[:, column], place.to_y
        elif index == 3:
            source = self.early.at[place.xy_x, :, mine]
            target, device = self.from_x[3].at[:, column], place.to_x
        elif index == 4:
            source = self.early.at[place.xy_y, :, mine]
            target, device = self.from_y[3].at[:, column], place.to_y
        else:
            k = index - 5
            source = self.early.at[:, :, self.early_columns(place.zs[k])]
            target, device = self.early_in.at[k], place.to_z[k]
        return remote(source, target, self.send.at[0, index], self.recv.at[0, index], device)

    def early_pair(self):
        self.copy(0, 0).wait_recv()
        self.gather_pair(0, range(4))
        for k in range(3):
            self.early_copy(5 + k).start()

    def early_sum(self):
        place = self.place
        mine = self.early_columns(place.z)
        for k in range(3):
            self.early_copy(5 + k).wait_recv()
        for block in range(4):
            total = self.early[block, :, mine].astype(jnp.float32)
            for k in range(3):
                total = total + self.early_in[k, block].astype(jnp.float32)
            self.early[block, :, mine] = total.astype(jnp.bfloat16)
        self.early_copy(1).start()
        self.early_copy(2).start()

    def early_cross(self):
        place = self.place
        mine = self.early_columns(place.z)
        for index, block, half, source in (
            (1, place.xy_y, slice(0, 48), self.diag_x[3]),
            (2, place.xy_x, slice(48, 96), self.diag_y[3]),
        ):
            self.early_copy(index).wait_recv()
            total = self.early[block, half, mine].astype(jnp.float32)
            total = total + source[:, 0:384].astype(jnp.float32)
            self.early[block, half, mine] = total.astype(jnp.bfloat16)
            self.early_copy(5 - index).start()

    def early_settle(self):
        place = self.place
        self.early_copy(3).wait_recv()
        self.early_copy(4).wait_recv()
        total = self.early[place.xy, :, self.early_columns(place.z)].astype(jnp.float32)
        total = total + self.from_x[3][:, 0:384].astype(jnp.float32)
        total = total + self.from_y[3][:, 0:384].astype(jnp.float32)
        self.settled(0, total)

    def copy(self, s, index):
        array, first, width = SCATTER_STAGES[s]
        place = self.place
        columns = self.columns(s)
        held = self.held(s)
        if index == 0:
            source = self.local(s).at[:, 1 - place.core]
            target = held
            device = place.to_sib
        elif index == 1:
            source = held.at[place.xy_d, pl.ds(0, 48)]
            target = self.diag_x[array].at[:, columns]
            device = place.to_x
        elif index == 2:
            source = held.at[place.xy_d, pl.ds(48, 48)]
            target = self.diag_y[array].at[:, columns]
            device = place.to_y
        elif index == 3:
            source = held.at[place.xy_x]
            target = self.from_x[array].at[:, columns]
            device = place.to_x
        elif index == 4:
            source = held.at[place.xy_y]
            target = self.from_y[array].at[:, columns]
            device = place.to_y
        else:
            k = index - 5
            source = self.z_out[array].at[place.zs[k], :, self.z_columns(s)]
            target = self.z_in[array].at[k, :, self.z_columns(s)]
            device = place.to_z[k]
        return remote(source, target, self.send.at[s, index], self.recv.at[s, index], device)

    def add(self, s, block, other, rows=slice(None)):
        held = self.held(s)
        total = held[block, rows].astype(jnp.float32) + other.astype(jnp.float32)
        held[block, rows] = total.astype(jnp.bfloat16)

    def free(self, s):
        turn = SCATTER_ORDER.index(s)
        if turn >= 2:
            self.copy(SCATTER_ORDER[turn - 2], 0).wait_send()

    def begin(self, s):
        self.copy(s, 0).start()

    def gather_pair(self, s, blocks):
        local = self.local(s)
        for block in blocks:
            self.add(s, block, local[block, self.place.core])

    def pair(self, s):
        place = self.place
        self.copy(s, 0).wait_recv()
        self.gather_pair(s, [place.xy_d])
        self.copy(s, 1).start()
        self.copy(s, 2).start()
        self.gather_pair(s, [place.xy_x, place.xy_y, place.xy])

    def cross(self, s):
        array = SCATTER_STAGES[s][0]
        place = self.place
        columns = self.columns(s)
        self.copy(s, 1).wait_recv()
        self.add(s, place.xy_y, self.diag_x[array][:, columns], slice(0, 48))
        self.copy(s, 4).start()
        self.copy(s, 2).wait_recv()
        self.add(s, place.xy_x, self.diag_y[array][:, columns], slice(48, 96))
        self.copy(s, 3).start()

    def square(self, s):
        array, first, width = SCATTER_STAGES[s]
        place = self.place
        self.copy(s, 3).wait_recv()
        self.copy(s, 4).wait_recv()
        held = self.held(s)
        for other in range(4):
            if array == 3:
                rows, inside = slice(0, 96), pl.ds(384 * other, 384)
                outside = pl.ds(first + 384 * other, 384)
            else:
                rows, inside = slice(24 * other, 24 * other + 24), pl.ds(0, width)
                outside = pl.ds(first, width)
            total = (
                held[place.xy, rows, inside].astype(jnp.float32)
                + self.from_x[array][rows, outside].astype(jnp.float32)
                + self.from_y[array][rows, outside].astype(jnp.float32)
            )
            self.z_out[array][other, :, self.z_columns(s)] = total.astype(jnp.bfloat16)
        for k in range(3):
            self.copy(s, 5 + k).start()

    def settle(self, s):
        array = SCATTER_STAGES[s][0]
        columns = self.z_columns(s)
        total = self.z_out[array][self.place.z, :, columns].astype(jnp.float32)
        for k in range(3):
            self.copy(s, 5 + k).wait_recv()
            total = total + self.z_in[array][k, :, columns].astype(jnp.float32)
        self.settled(s, total)

    def step(self, turn, s=None):
        if s is not None:
            self.begun[s] = turn
        for other in sorted(self.begun, reverse=True):
            lag = turn - self.begun[other]
            if lag in SCATTER_LAGS[other]:
                phase = SCATTER_LAGS[other].index(lag)
                if other == 0 and phase:
                    (self.early_pair, self.early_sum, self.early_cross, self.early_settle)[phase - 1]()
                else:
                    (self.begin, self.pair, self.cross, self.square, self.settle)[phase](other)

    def finish(self):
        for index in range(1, 8):
            self.early_copy(index).wait_send()
        count = len(SCATTER_STAGES)
        for s in range(1, count):
            for index in range(0 if s >= count - 2 else 1, 8):
                self.copy(s, index).wait_send()

ROW_BLOCK = 128
SCALE = 0.7978845608028654
BF = jnp.bfloat16
F32 = jnp.float32
ROWS_ALL = 768
NEAR = 3 * ROW_BLOCK


def dot(left, right, left_dim=1, right_dim=0):
    return lax.dot_general(
        left, right, (((left_dim,), (right_dim,)), ((), ())), preferred_element_type=F32
    )


def loop(count, body):
    def step(index, carry):
        body(index)
        return carry

    lax.fori_loop(0, count, step, 0)


def aligned(start, multiple, size):
    return pl.ds(pl.multiple_of(start, multiple), size)


def unflatten(flat, wide, target, start_of):
    lines = flat.shape[0]
    rows = target.shape[0]
    blocks = lines // rows
    wide[0:lines] = flat[...].astype(F32)
    for block in range(blocks):
        first = start_of(block)
        target[:, first : first + 128] = wide[pl.ds(block, rows, blocks), :].astype(BF)


def marks_of(relative):
    distance = jnp.abs(relative)
    distant = jnp.full_like(distance, 8)
    for power in range(1, 8):
        distant = distant + (distance * distance >= 64 * 2**power).astype(jnp.int32)
    bucket = jnp.where(distance < 8, distance, distant)
    bucket = bucket + 16 * (relative > 0).astype(jnp.int32)
    labels = lax.broadcasted_iota(jnp.int32, relative.shape, 0)
    return bucket == labels


def normed(values, gain_row):
    inverse = lax.rsqrt(jnp.mean(values * values, axis=-1, keepdims=True) + EPSILON)
    return values * inverse * gain_row


def window(block):
    return max(0, block - 2), min(3, block + 2)


def head_lanes(rows, which):
    lane = lax.broadcasted_iota(jnp.int32, (rows, 128), 1)
    return lane < HEAD_DIM if which == 0 else lane >= HEAD_DIM


def keep(values, which):
    return jnp.where(head_lanes(values.shape[0], which), values, jnp.zeros_like(values))


def softmax_rows(scores):
    largest = jnp.max(scores, axis=-1, keepdims=True)
    powers = jnp.exp(scores - largest)
    return (powers * (1.0 / jnp.sum(powers, axis=-1, keepdims=True))).astype(BF)


FORWARD_SAVED = (
    ((768, 3 * D), BF),
    ((768, D + PROJ), BF),
    ((768, 2 * FF), BF),
    ((4, 2, 4, 96, D), BF),
    ((768, D), BF),
    ((768, 3 * D), BF),
    ((768, D), BF),
    ((768, D), F32),
    ((768, D), BF),
    ((768, 2 * FF), BF),
    ((768, FF), BF),
    ((768, D), F32),
    ((768, D), BF),
    ((6, 512, 1024), BF),
    ((256, 1536), BF),
)


def forward_kernel(*refs):
    (doc, qry, doc_lengths, qry_lengths, small) = refs[0:5]
    flats = refs[5:13]
    doc_out, qry_out, gains_out = refs[13:16]
    saved = refs[16:31]
    rest = refs[31:]
    whole, parts, shards = rest[0:4], rest[4:7], rest[7:11]
    (wide, small_in, gains, diagonals, bias, id_column, id_row) = rest[11:18]
    (norm_one, qkv, context, hidden, norm_two, factors, inner, norm_three) = rest[18:26]
    (prob_doc, prob_qry, scores) = rest[26:29]
    gather_sems = rest[29:35]
    small_send, small_recv, save_sem, whole_sem, chunk_sem = rest[35:40]

    place = Place()
    place.barrier()
    gains[...] = jnp.zeros_like(gains)
    gather = Gather(place, shards, whole, parts, gather_sems)

    def small_copy(k):
        return remote(
            small, small_in.at[k], small_send.at[k], small_recv.at[k], place.to_z[k]
        )

    for k in range(3):
        small_copy(k).start()
    unflatten(flats[6], wide, shards[3], lambda j: 128 * j)
    gather.early_begin()
    for index in range(3):
        unflatten(flats[index], wide, shards[0].at[:, D * index : D * index + D], lambda j: 128 * j)
        gather.begin(index)

    def later_shards(turn):
        if turn == 0:
            unflatten(flats[3], wide, shards[1].at[:, 0:D], lambda j: 128 * j)
            shards[1][:, D:] = flats[7][...]
            gather.begin(3)
            unflatten(flats[4], wide, shards[2], lambda j: 1536 * (j // 6) + 128 * (j % 6))
            unflatten(flats[5], wide, shards[2], lambda j: 1536 * (j // 6) + 128 * (j % 6) + D)
        if 4 <= turn + 3 < 9:
            gather.begin(turn + 3)

    saves = []

    def save(index, source, target=None):
        copy = pltpu.make_async_copy(
            source, saved[index] if target is None else target, save_sem.at[index]
        )
        copy.start()
        saves.append((index, copy))
        return copy

    def save_part(semaphore, source, target):
        copy = pltpu.make_async_copy(source, target, semaphore)
        copy.start()
        saves.append((-1, copy))

    def save_whole(s):
        array, first, width = GATHER_STAGES[s]
        columns = pl.ds(first, width)
        if array == 3:
            here = (slice(None), slice(None), slice(None), slice(None), columns)
        else:
            here = (slice(None), columns)
        save_part(whole_sem.at[s], whole[array].at[here], saved[array].at[here])

    def small_arrive():
        for k in range(3):
            small_copy(k).wait_recv()
        pieces = []
        for other in range(4):
            piece = small[...]
            for k in range(3):
                here = lax.rem(place.z + 3 - k, 4) == other
                piece = jnp.where(here, small_in[k], piece)
            pieces.append(piece)
        low = lax.broadcasted_iota(jnp.int32, (1, 128), 1) < 64
        for row in range(3):
            for tile in range(6):
                unit = 12 * row + 2 * tile
                left = pieces[unit // 9][unit % 9 : unit % 9 + 1, :]
                unit = unit + 1
                right = pieces[unit // 9][unit % 9 : unit % 9 + 1, :]
                gains[row : row + 1, 128 * tile : 128 * tile + 128] = jnp.where(low, left, right)
        gains_out[...] = gains[...]
        table = jnp.concatenate([piece[16:24, :] for piece in pieces], axis=0).astype(BF)
        relative = lax.broadcasted_iota(jnp.int32, (BUCKETS, 512), 1) - 256
        diagonals[...] = dot(table, marks_of(relative).astype(BF), 0, 0)[0:16]

    def make_bias(head):
        rows = jnp.broadcast_to(diagonals[pl.ds(head, 1), :], (8, 512))
        lines = lax.broadcasted_iota(jnp.int32, (8, 512), 0)
        for bit in range(3):
            moved = pltpu.roll(rows, 2**bit, 1)
            rows = jnp.where(lax.rem(lines // 2**bit, 2) == 1, moved, rows)
        for group in range(ROW_BLOCK // 8):
            moved = pltpu.roll(rows, 8 * group, 1) if group else rows
            bias[head, 8 * group : 8 * group + 8, :] = moved[:, 128:512]

    def make_ids():
        position = lax.broadcasted_iota(jnp.int32, (512, 128), 0)
        across = lax.broadcasted_iota(jnp.int32, (8, 512), 1)
        down_id, across_id = jnp.zeros_like(position), jnp.zeros_like(across)
        edge = 0
        for index in range(4):
            edge = edge + doc_lengths[0, index]
            down_id = down_id + (position >= edge).astype(jnp.int32)
            across_id = across_id + (across >= edge).astype(jnp.int32)
        id_column[0:512] = down_id
        id_row[:, 0:512] = across_id
        position = lax.broadcasted_iota(jnp.int32, (32, 128), 0)
        across = lax.broadcasted_iota(jnp.int32, (8, 256), 1)
        across_id = jnp.zeros_like(across)
        for index in range(8):
            length = qry_lengths[0, index]
            id_column[512 + 32 * index : 544 + 32 * index] = 2 * index + (
                position >= length
            ).astype(jnp.int32)
            mine = (across >= 32 * index) & (across < 32 * index + 32)
            value = 2 * index + (across >= length + 32 * index).astype(jnp.int32)
            across_id = jnp.where(mine, value, across_id)
        id_row[:, 512:768] = across_id

    def first_norm():
        gain = gains[0:1, :]

        def documents(index):
            rows = aligned(128 * index, 128, 128)
            norm_one[rows] = normed(doc[rows].astype(F32), gain).astype(BF)

        def queries(index):
            rows = aligned(128 * index, 128, 128)
            norm_one[aligned(512 + 128 * index, 128, 128)] = normed(
                qry[rows].astype(F32), gain
            ).astype(BF)

        loop(4, documents)
        loop(2, queries)
        save(4, norm_one)

    def project(index):
        columns = pl.ds(D * index, D)
        qkv[:, columns] = dot(norm_one[...], whole[0][:, columns]).astype(BF)

    def attend_pair(pair):
        query = qkv[0:512, aligned(128 * pair, 128, 128)]
        key = qkv[0:512, aligned(D + 128 * pair, 128, 128)]
        value = qkv[0:512, aligned(2 * D + 128 * pair, 128, 128)]
        for which in range(2):
            head = 2 * pair + which
            scores[...] = dot(keep(query, which), key, 1, 1)
            far_left = jnp.broadcast_to(bias[head, 127:128, 0:1], (128, 128))
            far_right = jnp.broadcast_to(bias[head, 0:1, NEAR - 1 : NEAR], (128, 128))
            for block in range(4):
                low, high = window(block)
                near_low, near_high = max(low, block - 1), min(high, block + 1)
                pieces = [far_left] * (near_low - low)
                pieces.append(
                    bias[
                        head,
                        :,
                        128 * (near_low - block + 1) : 128 * (near_high - block + 2),
                    ]
                )
                pieces += [far_right] * (high - near_high)
                rows = slice(128 * block, 128 * block + 128)
                columns = slice(128 * low, 128 * high + 128)
                allowed = id_column[rows, 0:1] == id_row[0:1, columns]
                values = scores[rows, columns] + jnp.concatenate(pieces, axis=1)
                share = softmax_rows(jnp.where(allowed, values, NEGATIVE))
                prob_doc[
                    pair, rows, 512 * which + 128 * low : 512 * which + 128 * high + 128
                ] = share
        both = jnp.concatenate([keep(value, 0), keep(value, 1)], axis=0)
        context[0:512, aligned(128 * pair, 128, 128)] = dot(prob_doc[pair], both).astype(BF)
        for block in range(2):
            rows = slice(512 + 128 * block, 640 + 128 * block)
            query = qkv[rows, aligned(128 * pair, 128, 128)]
            key = qkv[rows, aligned(D + 128 * pair, 128, 128)]
            value = qkv[rows, aligned(2 * D + 128 * pair, 128, 128)]
            allowed = id_column[rows, 0:1] == id_row[0:1, rows]
            shares = []
            for which in range(2):
                values = dot(keep(query, which), key, 1, 1)
                values = values + bias[2 * pair + which, :, 128:256]
                shares.append(softmax_rows(jnp.where(allowed, values, NEGATIVE)))
            shares = jnp.concatenate(shares, axis=1)
            prob_qry[128 * block : 128 * block + 128, aligned(256 * pair, 128, 256)] = shares
            both = jnp.concatenate([keep(value, 0), keep(value, 1)], axis=0)
            context[rows, aligned(128 * pair, 128, 128)] = dot(shares, both).astype(BF)

    def attend(first, last):
        lax.fori_loop(first, last, lambda pair, carry: (attend_pair(pair), carry)[1], 0)

    def after_attention():
        save(5, qkv)
        save(6, context)
        save(13, prob_doc)
        save(14, prob_qry)

        def one(tokens, offset):
            def block(index):
                source = aligned(128 * index, 128, 128)
                rows = aligned(offset + 128 * index, 128, 128)
                total = tokens[source].astype(F32) + dot(context[rows], whole[1][:, 0:D])
                hidden[rows] = total
                norm_two[rows] = normed(total, gains[1:2, :]).astype(BF)

            return block

        loop(4, one(doc, 0))
        loop(2, one(qry, 512))
        copy = save(7, hidden)
        save(8, norm_two)
        return copy

    def gated(chunk):
        def block(index):
            rows = aligned(256 * index, 256, 256)
            left = norm_two[rows]
            gate = dot(left, whole[2][:, 1536 * chunk : 1536 * chunk + D])
            upper = dot(left, whole[2][:, 1536 * chunk + D : 1536 * chunk + 2 * D])
            square = gate * gate
            bend = jnp.tanh(SCALE * gate * (1.0 + 0.044715 * square))
            half = 0.5 * (1.0 + bend)
            active = gate * half
            slope = half + 0.5 * gate * (1.0 - bend * bend) * (
                SCALE + (3.0 * 0.044715 * SCALE) * square
            )
            inner[rows, D * chunk : D * chunk + D] = (active * upper).astype(BF)
            factors[rows, 1536 * chunk : 1536 * chunk + D] = (upper * slope).astype(BF)
            factors[rows, 1536 * chunk + D : 1536 * chunk + 2 * D] = active.astype(BF)

        loop(3, block)
        here = (slice(None), pl.ds(1536 * chunk, 1536))
        save_part(chunk_sem.at[0, chunk], factors.at[here], saved[9].at[here])
        here = (slice(None), pl.ds(D * chunk, D))
        save_part(chunk_sem.at[1, chunk], inner.at[here], saved[10].at[here])

    def descend(half):
        columns = slice(384 * half, 384 * half + 384)

        def block(index):
            rows = aligned(256 * index, 256, 256)
            matrix = whole[3][:, :, :, :, columns].reshape(FF, 384)
            hidden[rows, columns] = hidden[rows, columns] + dot(inner[rows], matrix)

        loop(3, block)

    def last():
        def block(index):
            rows = aligned(128 * index, 128, 128)
            norm_three[rows] = normed(hidden[rows], gains[2:3, :]).astype(BF)

        loop(6, block)
        result = dot(norm_three[...], whole[1][:, D:]).astype(BF)
        doc_out[...] = result[0:512]
        qry_out[...] = result[512:768]
        save(11, hidden)
        save(12, norm_three)

    def clear(pair):
        nothing = jnp.zeros((128, 128), BF)
        for which in range(2):
            prob_doc[pair, 0:128, 512 * which + 384 : 512 * which + 512] = nothing
            prob_doc[pair, 384:512, 512 * which : 512 * which + 128] = nothing

    hidden_copy = None
    for t in range(12):
        gather.step(t)
        later_shards(t)
        if t == 0:
            gather.early_relay()
        if t == 1:
            gather.early_square()
        if 5 <= t < 9:
            gather.early_send_z(t - 5)
        if t == 10:
            gather.early_layers()
        if t == 11:
            gather.early_arrive()
            save_whole(9)
        if t >= 3:
            save_whole(t - 3)
        if t == 1:
            small_arrive()
            first_norm()
        if t == 2:
            loop(6, make_bias)
            make_ids()
        if 3 <= t < 6:
            project(t - 3)
        if t == 3:
            lax.fori_loop(6, 12, lambda head, carry: (make_bias(head), carry)[1], 0)
            loop(6, clear)
        if t == 5:
            attend(0, 2)
        if t == 6:
            attend(2, 5)
        if t == 7:
            attend(5, 6)
            hidden_copy = after_attention()
        if 7 <= t < 11:
            gated(t - 7)
        if t == 10:
            hidden_copy.wait()
        if t == 11:
            descend(1)
            descend(0)
    last()
    gather.finish()
    for k in range(3):
        small_copy(k).wait_send()
    for index, copy in saves:
        if index != 7:
            copy.wait()


def forward(doc, qry, doc_lengths, qry_lengths, small, flats):
    vmem = pl.BlockSpec(memory_space=pltpu.VMEM)
    smem = pl.BlockSpec(memory_space=pltpu.SMEM)
    hbm = pl.BlockSpec(memory_space=pl.ANY)
    dma = pltpu.SemaphoreType.DMA
    whole_rows = [32 * count for count in SHARE_ROWS]
    scratch = [pltpu.VMEM((r, w), BF) for r, w in zip(whole_rows[:3], WIDTHS[:3])]
    scratch += [pltpu.VMEM((4, 2, 4, 96, D), BF)]
    scratch += [pltpu.VMEM((3, r, w), BF) for r, w in zip(SHARE_ROWS[:3], WIDTHS[:3])]
    scratch += [pltpu.VMEM((r, w), BF) for r, w in zip(SHARE_ROWS, WIDTHS)]
    scratch += [
        pltpu.VMEM((576, 128), F32),
        pltpu.VMEM((3, 24, 128), F32),
        pltpu.VMEM((8, D), F32),
        pltpu.VMEM((16, 512), F32),
        pltpu.VMEM((HEADS, 128, NEAR), F32),
        pltpu.VMEM((768, 128), jnp.int32),
        pltpu.VMEM((8, 768), jnp.int32),
        pltpu.VMEM((768, D), BF),
        pltpu.VMEM((768, 3 * D), BF),
        pltpu.VMEM((768, D), BF),
        pltpu.VMEM((768, D), F32),
        pltpu.VMEM((768, D), BF),
        pltpu.VMEM((768, 2 * FF), BF),
        pltpu.VMEM((768, FF), BF),
        pltpu.VMEM((768, D), BF),
        pltpu.VMEM((6, 512, 1024), BF),
        pltpu.VMEM((256, 1536), BF),
        pltpu.VMEM((512, 512), F32),
    ]
    scratch += Gather.scratch()
    scratch += [dma((3,)), dma((3,)), dma((15,)), dma((len(GATHER_STAGES),)), dma((2, 4))]
    return pl.pallas_call(
        forward_kernel,
        out_shape=(
            jax.ShapeDtypeStruct((512, PROJ), BF),
            jax.ShapeDtypeStruct((256, PROJ), BF),
            jax.ShapeDtypeStruct((8, D), F32),
        )
        + tuple(jax.ShapeDtypeStruct(shape, kind) for shape, kind in FORWARD_SAVED),
        in_specs=[vmem, vmem, smem, smem, vmem] + [vmem] * 8,
        out_specs=(vmem, vmem, vmem) + (hbm,) * len(FORWARD_SAVED),
        scratch_shapes=scratch,
        compiler_params=pltpu.CompilerParams(
            collective_id=0, has_side_effects=True, vmem_limit_bytes=VMEM_LIMIT
        ),
        name="forward",
    )(doc, qry, doc_lengths, qry_lengths, small, *flats)


VMEM_LIMIT = 63 * 2**20


def norm_back(values, gain_row, incoming):
    inverse = lax.rsqrt(jnp.mean(values * values, axis=-1, keepdims=True) + EPSILON)
    scaled = gain_row * incoming
    inner = jnp.mean(scaled * values, axis=-1, keepdims=True)
    result = inverse * scaled - values * (inverse * inverse * inverse * inner)
    terms = incoming * values * inverse
    return result, jnp.sum(terms.reshape(-1, 8, D), axis=0)


def diagonal_sums(near):
    wide = jnp.concatenate([near, jnp.zeros((128, 128), F32)], axis=1)
    rows = wide[0:8]
    for group in range(1, 16):
        rows = rows + pltpu.roll(wide[8 * group : 8 * group + 8], 512 - 8 * group, 1)
    lines = lax.broadcasted_iota(jnp.int32, (8, 512), 0)
    for bit in range(3):
        moved = pltpu.roll(rows, 512 - 2**bit, 1)
        rows = jnp.where(lax.rem(lines // 2**bit, 2) == 1, moved, rows)
    return jnp.sum(rows, axis=0, keepdims=True)


def backward_kernel(*refs):
    doc, qry, doc_cotangent, qry_cotangent, gains = refs[0:5]
    saved = refs[5:20]
    doc_grad, qry_grad = refs[20:22]
    flats = refs[22:30]
    small_out = refs[30]
    rest = refs[31:]
    (out_mat, down, gate_up, factors, mixed, residual, hidden, incoming) = rest[0:8]
    (norm_two, norm_three, narrow, context, cotangent) = rest[8:13]
    (gain_terms, diagonal_rows, scores, small, small_in) = rest[13:18]
    scatter_buffers = rest[18:45]
    scatter_sems = rest[45:47]
    small_send, small_recv, load_sem = rest[47:50]

    place = Place()
    small_out[...] = jnp.zeros_like(small_out)
    loads = {}

    def load(name, source, target):
        copy = pltpu.make_async_copy(source, target, load_sem.at[len(loads)])
        copy.start()
        loads[name] = copy

    def ready(*names):
        for name in names:
            loads[name].wait()

    load("residual", saved[11], residual)
    load("out_mat", saved[1], out_mat)
    load("inner", saved[10], mixed)
    load("down", saved[3], down)

    def load_chunk(chunk):
        columns = pl.ds(1536 * chunk, 1536)
        load(("factors", chunk), saved[9].at[:, columns], factors.at[chunk % 2])
        load(("gate_up", chunk), saved[2].at[:, columns], gate_up.at[chunk % 2])

    load_chunk(0)
    load("norm_two", saved[8], norm_two)
    load_chunk(1)
    load("hidden", saved[7], hidden)
    load("context", saved[6], context)
    load("norm_three", saved[12], norm_three)

    place.barrier()

    def settled(s, total):
        array, first, width = SCATTER_STAGES[s]
        if array == 3:
            for tile in range(3):
                line = 3 * s + tile
                flats[6][pl.ds(line, 96, 6), :] = total[:, 128 * tile : 128 * tile + 128]
        elif array == 2:
            for tile in range(12):
                line = 6 * (first // 1536) + tile % 6
                flats[4 + tile // 6][pl.ds(line, 24, 24), :] = total[
                    :, 128 * tile : 128 * tile + 128
                ]
        else:
            for tile in range(6 if array == 1 else 9):
                flat = flats[3 if array == 1 else tile // 3]
                line = tile if array == 1 else 3 * (first // 1152) + tile % 3
                flat[pl.ds(line, 24, 6), :] = total[:, 128 * tile : 128 * tile + 128]
            if array == 1:
                flats[7][...] = total[:, D:]

    scatter = Scatter(place, scatter_buffers, settled, scatter_sems)
    gain_terms[...] = jnp.zeros_like(gain_terms)
    diagonal_rows[...] = jnp.zeros_like(diagonal_rows)
    cotangent[0:512] = doc_cotangent[...]
    cotangent[512:768] = qry_cotangent[...]

    def final_norm(index):
        rows = aligned(128 * index, 128, 128)
        grad, terms = norm_back(
            residual[rows], gains[2:3, :], dot(cotangent[rows], out_mat[:, D:], 1, 1)
        )
        residual[rows] = grad
        narrow[rows] = grad.astype(BF)
        gain_terms[2] = gain_terms[2] + terms

    ready("residual", "out_mat")
    loop(6, final_norm)

    ready("inner")
    for half in (1, 0):
        scatter.free(half)
        local = scatter.local(half)

        def piece(index):
            total = dot(
                mixed[:, aligned(D * index, 128, D)],
                narrow[:, 384 * half : 384 * half + 384],
                0,
                0,
            ).astype(BF)
            for core in range(2):
                for other in range(4):
                    first = 384 * core + 96 * other
                    local[index, core, :, 384 * other : 384 * other + 384] = total[
                        first : first + 96
                    ]

        loop(4, piece)
        scatter.step(1 - half, half)
    load("qkv", saved[5], mixed.at[:, pl.ds(0, 3 * D)])
    load("norm_one", saved[4], mixed.at[:, pl.ds(3 * D, D)])

    def put(local, total, first):
        total = total.astype(BF)
        width = total.shape[1]
        for block in range(8):
            local[block // 2, block % 2, :, first : first + width] = total[
                96 * block : 96 * block + 96
            ]

    ready("down", "norm_two")
    for chunk in range(4):
        slot = chunk % 2
        ready(("factors", chunk), ("gate_up", chunk))

        def gated_back(index):
            rows = aligned(256 * index, 256, 256)
            grad = dot(narrow[rows], down[D * chunk : D * chunk + D], 1, 1)
            for side in (0, D):
                factors[slot, rows, side : side + D] = (
                    grad * factors[slot, rows, side : side + D].astype(F32)
                ).astype(BF)

        loop(3, gated_back)
        stage = 2 + chunk
        scatter.free(stage)
        for side in (0, D):
            put(
                scatter.local(stage),
                dot(norm_two[...], factors[slot, :, side : side + D], 0, 0),
                side,
            )
        scatter.step(stage, stage)

        part = dot(factors[slot], gate_up[slot], 1, 1)
        incoming[...] = part if chunk == 0 else incoming[...] + part
        if chunk < 2:
            load_chunk(chunk + 2)
        if chunk == 2:
            load(("share", 0), saved[13].at[0], factors.at[0, pl.ds(0, 512), pl.ds(0, 1024)])
            load("share_qry", saved[14], gate_up.at[0, pl.ds(0, 256)])
    load(("share", 1), saved[13].at[1], factors.at[1, pl.ds(0, 512), pl.ds(0, 1024)])
    for index in range(3):
        load(
            ("qkv_mat", index),
            saved[0].at[:, pl.ds(D * index, D)],
            down.at[pl.ds(D * index, D)],
        )
    load("doc", doc, down.at[pl.ds(3 * D, 512)])
    load("qry", qry, down.at[pl.ds(3 * D + 512, 256)])

    def middle_norm(index):
        rows = aligned(128 * index, 128, 128)
        grad, terms = norm_back(hidden[rows], gains[1:2, :], incoming[rows])
        grad = grad + residual[rows]
        residual[rows] = grad
        narrow[rows] = grad.astype(BF)
        gain_terms[1] = gain_terms[1] + terms

    ready("hidden")
    loop(6, middle_norm)
    ready("context", "norm_three")
    scatter.free(6)
    put(scatter.local(6), dot(context[...], narrow[...], 0, 0), 0)
    put(scatter.local(6), dot(norm_three[...], cotangent[...], 0, 0), D)
    scatter.step(6, 6)
    grad_context = norm_three
    grad_context[...] = dot(narrow[...], out_mat[:, 0:D], 1, 1).astype(BF)

    nothing = jnp.zeros((128, 128), BF)
    grad_scores = gate_up.at[1]
    for which in range(2):
        grad_scores[0:128, 512 * which + 384 : 512 * which + 512] = nothing
        grad_scores[384:512, 512 * which : 512 * which + 128] = nothing

    def two(values):
        return jnp.concatenate([keep(values, 0), keep(values, 1)], axis=0)

    def attention_back(pair, share):
        columns = [aligned(D * index + 128 * pair, 128, 128) for index in range(3)]
        rows = slice(0, 512)
        query, key, value = (mixed[rows, column] for column in columns)
        grad = grad_context[rows, columns[0]]
        near_sums, far_sums = [], []
        for which in range(2):
            scores[...] = dot(keep(grad, which), value, 1, 1)
            near = [None, None, None]
            far = [None, None]
            for block in range(4):
                low, high = window(block)
                rows_here = slice(128 * block, 128 * block + 128)
                reach = slice(512 * which + 128 * low, 512 * which + 128 * high + 128)
                part = share[rows_here, reach].astype(F32)
                grad_share = scores[rows_here, 128 * low : 128 * high + 128]
                weighted = jnp.sum(part * grad_share, axis=-1, keepdims=True)
                result = (part * (grad_share - weighted)).astype(BF)
                grad_scores[rows_here, reach] = result
                result = result.astype(F32)
                for other in range(low, high + 1):
                    tile = result[:, 128 * (other - low) : 128 * (other - low) + 128]
                    place_at = other - block
                    if abs(place_at) == 2:
                        side = 0 if place_at < 0 else 1
                        far[side] = tile if far[side] is None else far[side] + tile
                    else:
                        side = place_at + 1
                        near[side] = tile if near[side] is None else near[side] + tile
            near_sums.append(near)
            far_sums.append(far)
        grad_query = dot(grad_scores[0:512, 0:1024], two(key))
        grad_key = dot(grad_scores[0:512, 0:512], keep(query, 0), 0, 0) + dot(
            grad_scores[0:512, 512:1024], keep(query, 1), 0, 0
        )
        grad_value = dot(share[0:512, 0:512], keep(grad, 0), 0, 0) + dot(
            share[0:512, 512:1024], keep(grad, 1), 0, 0
        )
        mixed[rows, columns[0]] = grad_query.astype(BF)
        mixed[rows, columns[1]] = grad_key.astype(BF)
        mixed[rows, columns[2]] = grad_value.astype(BF)
        for block in range(2):
            rows = slice(512 + 128 * block, 640 + 128 * block)
            query, key, value = (mixed[rows, column] for column in columns)
            grad = grad_context[rows, columns[0]]
            small_share = gate_up[
                0, 128 * block : 128 * block + 128, aligned(256 * pair, 128, 256)
            ]
            results = []
            grad_key = jnp.zeros((128, 128), F32)
            grad_value = jnp.zeros((128, 128), F32)
            for which in range(2):
                part = small_share[:, 128 * which : 128 * which + 128]
                grad_share = dot(keep(grad, which), value, 1, 1)
                wide = part.astype(F32)
                weighted = jnp.sum(wide * grad_share, axis=-1, keepdims=True)
                result = (wide * (grad_share - weighted)).astype(BF)
                near_sums[which][1] = near_sums[which][1] + result.astype(F32)
                results.append(result)
                grad_key = grad_key + dot(result, keep(query, which), 0, 0)
                grad_value = grad_value + dot(part, keep(grad, which), 0, 0)
            grad_query = dot(jnp.concatenate(results, axis=1), two(key))
            mixed[rows, columns[0]] = grad_query.astype(BF)
            mixed[rows, columns[1]] = grad_key.astype(BF)
            mixed[rows, columns[2]] = grad_value.astype(BF)
        lane = lax.broadcasted_iota(jnp.int32, (1, 512), 1)
        for which in range(2):
            row = diagonal_sums(jnp.concatenate(near_sums[which], axis=1))
            for side, column in ((0, 28), (1, 228)):
                total = jnp.sum(far_sums[which][side], axis=(0, 1), keepdims=True)
                row = row + jnp.where(lane == column, total, 0.0)
            diagonal_rows[pl.ds(2 * pair + which, 1), :] = row

    ready("qkv", "norm_one", "share_qry")
    turn = 7
    for pair in range(6):
        slot = pair % 2
        ready(("share", pair))
        attention_back(pair, factors.at[slot])
        if pair < 4:
            load(
                ("share", pair + 2),
                saved[13].at[pair + 2],
                factors.at[slot, pl.ds(0, 512), pl.ds(0, 1024)],
            )
        if pair in (2, 5):
            half = pair // 3
            stage = 7 + half
            scatter.free(stage)
            for index in range(3):
                first = D * index + 384 * half
                put(
                    scatter.local(stage),
                    dot(mixed[:, 3 * D :], mixed[:, first : first + 384], 0, 0),
                    384 * index,
                )
            scatter.step(turn, stage)
            turn = turn + 1
        if pair in (1, 4):
            scatter.step(turn)
            turn = turn + 1

    ready(("qkv_mat", 0), ("qkv_mat", 1), ("qkv_mat", 2), "doc", "qry")

    for index in range(3):
        part = dot(mixed[:, D * index : D * index + D], down[D * index : D * index + D], 1, 1)
        incoming[...] = part if index == 0 else incoming[...] + part
    scatter.step(turn)
    turn = turn + 1

    def first_norm(index):
        rows = aligned(128 * index, 128, 128)
        part = incoming[rows]
        here = aligned(3 * D + 128 * index, 128, 128)
        grad, terms = norm_back(down[here].astype(F32), gains[0:1, :], part)
        down[here] = (residual[rows] + grad).astype(BF)
        gain_terms[0] = gain_terms[0] + terms

    loop(6, first_norm)
    stores = [
        pltpu.make_async_copy(down.at[pl.ds(3 * D, 512)], doc_grad, load_sem.at[len(loads)]),
        pltpu.make_async_copy(
            down.at[pl.ds(3 * D + 512, 256)], qry_grad, load_sem.at[len(loads) + 1]
        ),
    ]
    for copy in stores:
        copy.start()

    small[0] = jnp.zeros((40, 128), F32)
    for row in range(3):
        total = jnp.sum(gain_terms[row], axis=0, keepdims=True)
        for tile in range(6):
            line = 6 * row + tile
            small[0, line : line + 1, :] = total[:, 128 * tile : 128 * tile + 128]
    column = lax.broadcasted_iota(jnp.int32, (BUCKETS, 512), 1)
    relative = jnp.where(column < 384, column - 128, column - 640)
    marks = marks_of(relative).astype(F32)
    small[0, 24:40, 0:BUCKETS] = lax.dot_general(
        diagonal_rows[...],
        marks,
        (((1,), (1,)), ((), ())),
        precision=lax.Precision.HIGHEST,
        preferred_element_type=F32,
    )

    def small_copy(index):
        device = ([place.to_sib, place.to_x, place.to_y] + place.to_z)[index]
        return remote(
            small.at[min(index, 3)],
            small_in.at[index],
            small_send.at[index],
            small_recv.at[index],
            device,
        )

    small_copy(0).start()
    for index in range(3):
        scatter.step(turn)
        turn = turn + 1
        small_copy(index).wait_recv()
        small[index + 1] = small[index] + small_in[index]
        if index < 2:
            small_copy(index + 1).start()
    for k in range(3):
        small_copy(3 + k).start()
    scatter.step(turn)
    for k in range(3):
        small_copy(3 + k).wait_recv()
    total = jnp.zeros((40, 128), F32)
    for other in range(4):
        piece = small[3]
        for k in range(3):
            here = lax.rem(place.z + 3 - k, 4) == other
            piece = jnp.where(here, small_in[3 + k], piece)
        total = total + piece
    small[4] = total
    first = 9 * place.z // 2
    plain = small[4, pl.ds(first, 5), :]
    turned, later = (
        pltpu.roll(small[4, pl.ds(first + more, 5), :], 64, 1) for more in range(2)
    )
    low = lax.broadcasted_iota(jnp.int32, (5, 128), 1) < 64
    odd = lax.rem(place.z, 2) == 1
    small_out[0:5] = jnp.where(odd, jnp.where(low, turned, later), plain)
    lane = lax.broadcasted_iota(jnp.int32, (BUCKETS, 128), 1)
    bucket = lax.broadcasted_iota(jnp.int32, (BUCKETS, 128), 0)
    chosen = (8 * place.z + lane // HEADS == bucket).astype(F32)
    spread = lax.dot_general(
        total[24:40, 0:BUCKETS],
        chosen,
        (((1,), (0,)), ((), ())),
        precision=lax.Precision.HIGHEST,
        preferred_element_type=F32,
    )
    lane = lax.broadcasted_iota(jnp.int32, (16, 128), 1)
    head = lax.broadcasted_iota(jnp.int32, (16, 128), 0)
    spread = jnp.where(lax.rem(lane, HEADS) == head, spread, 0.0)
    small_out[8:9] = jnp.sum(spread, axis=0, keepdims=True)

    scatter.finish()
    for index in range(6):
        small_copy(index).wait_send()
    for copy in stores:
        copy.wait()


def backward(doc, qry, doc_cotangent, qry_cotangent, gains, saved):
    vmem = pl.BlockSpec(memory_space=pltpu.VMEM)
    hbm = pl.BlockSpec(memory_space=pl.ANY)
    dma = pltpu.SemaphoreType.DMA
    scratch = [
        pltpu.VMEM((768, D + PROJ), BF),
        pltpu.VMEM((FF, D), BF),
        pltpu.VMEM((2, 768, 1536), BF),
        pltpu.VMEM((2, 768, 1536), BF),
        pltpu.VMEM((768, FF), BF),
        pltpu.VMEM((768, D), F32),
        pltpu.VMEM((768, D), F32),
        pltpu.VMEM((768, D), F32),
        pltpu.VMEM((768, D), BF),
        pltpu.VMEM((768, D), BF),
        pltpu.VMEM((768, D), BF),
        pltpu.VMEM((768, D), BF),
        pltpu.VMEM((768, PROJ), BF),
        pltpu.VMEM((3, 8, D), F32),
        pltpu.VMEM((16, 512), F32),
        pltpu.VMEM((512, 512), F32),
        pltpu.VMEM((5, 40, 128), F32),
        pltpu.VMEM((6, 40, 128), F32),
    ]
    scratch += Scatter.scratch() + Scatter.semaphores() + [dma((6,)), dma((6,)), dma((36,))]
    lines = (144, 144, 144, 144, 576, 576, 576, 24)
    return pl.pallas_call(
        backward_kernel,
        out_shape=(
            jax.ShapeDtypeStruct((512, D), BF),
            jax.ShapeDtypeStruct((256, D), BF),
        )
        + tuple(jax.ShapeDtypeStruct((count, 128), F32) for count in lines)
        + (jax.ShapeDtypeStruct((16, 128), F32),),
        in_specs=[hbm, hbm, vmem, vmem, vmem] + [hbm] * len(saved),
        out_specs=(hbm, hbm) + (vmem,) * 9,
        scratch_shapes=scratch,
        compiler_params=pltpu.CompilerParams(
            collective_id=1, has_side_effects=True, vmem_limit_bytes=VMEM_LIMIT
        ),
        name="backward",
    )(doc, qry, doc_cotangent, qry_cotangent, gains, *saved)


def hand_out_kernel(*refs):
    count = len(refs) // 2
    copies = [
        pltpu.make_async_copy(refs[index], refs[count + index], refs[-1].at[index])
        for index in range(count)
    ]
    for copy in copies:
        copy.start()
    for copy in copies:
        copy.wait()


def hand_out(arrays):
    hbm = pl.BlockSpec(memory_space=pl.ANY)
    return pl.pallas_call(
        hand_out_kernel,
        out_shape=tuple(jax.ShapeDtypeStruct(array.shape, array.dtype) for array in arrays),
        in_specs=[pl.BlockSpec(memory_space=pltpu.VMEM)] * len(arrays),
        out_specs=(hbm,) * len(arrays),
        scratch_shapes=[pltpu.SemaphoreType.DMA((len(arrays),))],
        name="hand_out",
    )(*arrays)


def local_fast(
    document_tokens,
    document_lengths,
    query_tokens,
    query_lengths,
    weight_query,
    weight_key,
    weight_value,
    weight_out,
    weight_gate,
    weight_up,
    weight_down,
    weight_proj,
    norm_gains,
    rel_table,
    document_cotangent,
    query_cotangent,
):
    doc = document_tokens.reshape(DOC_LEN, D)
    qry = query_tokens.reshape(-1, D)
    units = norm_gains.astype(jnp.float32).reshape(9, 64)
    units = jnp.pad(jnp.concatenate([units, units], axis=1), ((0, 7), (0, 0)))
    table = jnp.pad(rel_table.astype(jnp.float32).reshape(8, HEADS), ((0, 0), (0, 128 - HEADS)))
    small = jnp.concatenate([units, table], axis=0)
    flats = [
        w.reshape(-1, 128)
        for w in (
            weight_query,
            weight_key,
            weight_value,
            weight_out,
            weight_gate,
            weight_up,
            weight_down,
            weight_proj,
        )
    ]
    results = forward(doc, qry, document_lengths, query_lengths.reshape(1, 8), small, flats)
    doc_out, qry_out, gains = results[0:3]
    grads = backward(
        doc,
        qry,
        document_cotangent.reshape(DOC_LEN, PROJ),
        query_cotangent.reshape(-1, PROJ),
        gains,
        results[3:6] + (results[6].reshape(FF, D),) + results[7:],
    )
    small = grads[10]
    results = hand_out((doc_out, qry_out) + tuple(grads[0:10]))
    return (
        results[0].reshape(document_cotangent.shape),
        results[1].reshape(query_cotangent.shape),
        results[2].reshape(document_tokens.shape),
        results[3].reshape(query_tokens.shape),
        *[grad.reshape(-1) for grad in results[4:12]],
        small[0:5].reshape(-1)[0:576],
        small[8, 0:96],
    )


def solution(mesh):
    placed = (
        P(("dp", "fsdp"), None, None),
        P(("dp", "fsdp"), None),
        P(("dp", "fsdp"), None, None),
        P(("dp", "fsdp")),
        P(("dp", "fsdp")),
        P(("dp", "fsdp")),
        P(("dp", "fsdp")),
        P(("dp", "fsdp")),
        P(("dp", "fsdp")),
        P(("dp", "fsdp")),
        P(("dp", "fsdp")),
        P(("dp", "fsdp")),
        P("fsdp"),
        P("fsdp"),
        P(("dp", "fsdp"), None, None),
        P(("dp", "fsdp"), None, None),
    )
    return jax.shard_map(
        local_fast if (mesh.shape["dp"], mesh.shape["fsdp"]) == (8, 4) else local,
        mesh=mesh,
        in_specs=placed,
        out_specs=(
            P(("dp", "fsdp"), None, None),
            P(("dp", "fsdp"), None, None),
            P(("dp", "fsdp"), None, None),
            P(("dp", "fsdp"), None, None),
            P(("dp", "fsdp")),
            P(("dp", "fsdp")),
            P(("dp", "fsdp")),
            P(("dp", "fsdp")),
            P(("dp", "fsdp")),
            P(("dp", "fsdp")),
            P(("dp", "fsdp")),
            P(("dp", "fsdp")),
            P("fsdp"),
            P("fsdp"),
        ),
        check_vma=False,
    )
```
